32 devices in a mesh: tok: 8 (over z, x), chan: 4 (over y, core).
Axes of the slice: x: 2, y: 2, z: 4, core: 2. Of those that a mesh axis runs over, the one named last changes fastest.
Arguments:
- query: bfloat16 [2048, 8192], P('tok', 'chan'), may hold values from -12 to 12
- key_in: bfloat16 [2048, 8192], P('tok', 'chan'), may hold values from -6 to 6
- value_in: bfloat16 [2048, 8192], P('tok', 'chan'), may hold values from -6 to 6
- filter_store: bfloat16 [2048, 8192], P('tok', 'chan'), may hold values from -0.125 to 0.125
- lag_of_block: int32 [8], replicated, may hold values from 0 to 7, each once
- skip: float32 [8192], P('chan'), may hold values from 0.3 to 1.5
- out_gain: float32 [8192], P('chan'), may hold values from 0.1 to 1.9
Outputs:
- output: float32 [2048, 8192], P('tok', 'chan')
The draws below stay inside these ranges and needn't reach their ends.
Inputs may be any that keep to these rules, and one draw needn't show every extreme that they name: `lag_of_block`: each of the 8 lag blocks is held by exactly one stored block.
All inputs are finite; a program needn't handle non-finite values.
Results may differ from the reference program's by a relative error of at most 0.0029.
Values may be sent and summed in bfloat16 or wider, within the bound.
No kernel may reach another device: no remote copies, remote signals or barrier semaphores. Data moves between devices by JAX's collectives and lax.ppermute only.
A program may use at most 192 MiB of HBM per device.

```python
import jax
import jax.numpy as jnp
from jax import lax

D = 8192
TOK_DEV = 256
TOKENS = 2048
N_TOK = 8


def draw_query(key, part):
    column = jnp.arange(D, dtype=jnp.float32) / D
    base = jax.random.normal(key, (TOKENS, D), jnp.float32)
    base = jnp.clip(base, -6.0, 6.0)
    scale = 0.6 + 1.2 * column
    return (base * scale[None, :]).astype(jnp.bfloat16)


def levels(key, extent, pieces, least, high):
    loudness, own = 1.0, jax.random.fold_in(key, 6)
    for axis_at, parts in pieces:
        heights = jnp.exp(jax.random.uniform(jax.random.fold_in(own, axis_at), (parts,), jnp.float32, least / len(pieces), high / len(pieces)))
        loudness = loudness * jnp.repeat(heights, extent[axis_at] // parts).reshape([-1 if axis == axis_at else 1 for axis in range(len(extent))])
    return loudness


def noise(key, shape, spread, reach, cuts=(), held_as=jnp.bfloat16):
    values = jax.random.normal(key, shape, jnp.float32) * spread
    if len(cuts) > 0:
        values = levels(key, shape, cuts, -0.22, 0.18) * values
    return jnp.clip(values, min=-reach, max=reach).astype(held_as)


def setup_inputs(seed: int = 0) -> dict:
    key_of = jax.random.split(jax.random.key(seed), 8)
    query = draw_query(jax.random.fold_in(key_of[7], 71), 0)
    key_in = noise(key_of[1], (TOKENS, D), 1.0, 6.0, ((0, 8), (1, 4)))
    value_in = noise(key_of[2], (TOKENS, D), 1.0, 6.0, ((0, 8), (1, 4)))
    filter_store = noise(key_of[3], (TOKENS, D), TOKENS ** -0.5, 0.125, ((0, 8), (1, 4)))
    lag_of_block = jax.random.permutation(key_of[4], N_TOK).astype(jnp.int32)
    skip = jnp.clip(0.3 + 1.2 * jax.random.uniform(key_of[5], (D,), jnp.float32) ** levels(key_of[5], (D,), ((0, 4),), -0.2, 0.2), 0.3, 1.5)
    out_gain = jnp.clip(1.0 + 0.18 * jax.random.normal(key_of[6], (D,), jnp.float32), 0.1, 1.9)
    return dict(query=query, key_in=key_in, value_in=value_in, filter_store=filter_store, lag_of_block=lag_of_block, skip=skip, out_gain=out_gain)


def reference(query, key_in, value_in, filter_store, lag_of_block, skip, out_gain):
    gated = (key_in.astype(jnp.float32) * value_in.astype(jnp.float32)).astype(jnp.bfloat16)
    blocks = filter_store.reshape(N_TOK, TOK_DEV, D)
    inverse = jnp.zeros((N_TOK,), jnp.int32).at[lag_of_block].set(jnp.arange(N_TOK, dtype=jnp.int32))
    filt = blocks[inverse].reshape(TOKENS, D)
    gated_full = gated.astype(jnp.float32)
    length = 2 * TOKENS
    spec_in = jnp.fft.rfft(gated_full, length, axis=0)
    spec_filt = jnp.fft.rfft(filt.astype(jnp.float32), length, axis=0)
    conv = jnp.fft.irfft(spec_in * spec_filt, length, axis=0)[:TOKENS]
    pre = query.astype(jnp.float32) * (conv + skip[None, :] * gated_full)
    mean_sq = lax.optimization_barrier(jnp.mean(pre * pre, axis=1, keepdims=True))
    return out_gain[None, :] * pre * lax.rsqrt(mean_sq + 1e-06)
```

```python
import functools
import math

import jax
import jax.numpy as jnp
import ml_dtypes
import numpy as np
from jax import lax
from jax.experimental import pallas as pl
from jax.experimental.pallas import tpu as pltpu
from jax.sharding import PartitionSpec as P


def split_bf16(table):
    high = table.astype(ml_dtypes.bfloat16)
    low = (table - high.astype(np.float64)).astype(ml_dtypes.bfloat16)
    return high, low


def tables(width):
    freq = np.concatenate([np.arange(0, width, 2), np.arange(1, width, 2)])
    place = np.arange(width)
    steps = ((2 * freq[:, None] + 1) * place[None, :]) % (4 * width)
    angle = math.pi / (2 * width) * steps
    forward = np.concatenate([np.cos(angle), -np.sin(angle)], axis=0)
    inverse = forward.T / width
    return split_bf16(forward) + split_bf16(inverse)


def conv_kernel(count, width, lag_ref, f_ref, g_ref, fh_ref, fl_ref, ih_ref, il_ref, out_ref, fs, gs, ss):
    dot = functools.partial(jnp.dot, preferred_element_type=jnp.float32)
    for i in range(count):
        fs[lag_ref[i]] = dot(fh_ref[...], f_ref[i]) + dot(fl_ref[...], f_ref[i])
        gs[i] = dot(fh_ref[...], g_ref[i]) + dot(fl_ref[...], g_ref[i])
    columns = f_ref.shape[2]
    lane = min(128, columns)

    def products(row, sign):
        re_rows = pl.ds(pl.multiple_of(row * 8, 8), 8)
        im_rows = pl.ds(pl.multiple_of(row * 8 + width, 8), 8)
        for at in range(0, columns, lane):
            lanes = pl.ds(at, lane)
            f_re = [fs[i, re_rows, lanes] for i in range(count)]
            f_im = [fs[i, im_rows, lanes] for i in range(count)]
            h_re, h_im = [], []
            for i in range(count):
                g_re, g_im = gs[i, re_rows, lanes], gs[i, im_rows, lanes]
                if i == 0:
                    h_re.append(g_re)
                    h_im.append(g_im)
                elif sign > 0:
                    h_re.append(g_re - last_im)
                    h_im.append(g_im + last_re)
                else:
                    h_re.append(g_re + last_im)
                    h_im.append(g_im - last_re)
                last_re, last_im = g_re, g_im
            for j in range(count):
                s_re = f_re[0] * h_re[j] - f_im[0] * h_im[j]
                s_im = f_re[0] * h_im[j] + f_im[0] * h_re[j]
                for i in range(1, j + 1):
                    s_re = s_re + f_re[i] * h_re[j - i] - f_im[i] * h_im[j - i]
                    s_im = s_im + f_re[i] * h_im[j - i] + f_im[i] * h_re[j - i]
                ss[j, re_rows, lanes] = s_re
                ss[j, im_rows, lanes] = s_im

    half = width // 16

    @pl.loop(0, half)
    def _(row):
        products(row, 1)

    @pl.loop(half, 2 * half)
    def _(row):
        products(row, -1)

    for j in range(count):
        total = ss[j]
        high = total.astype(jnp.bfloat16)
        low = (total - high.astype(jnp.float32)).astype(jnp.bfloat16)
        out_ref[j] = (dot(ih_ref[...], high) + dot(ih_ref[...], low) + dot(il_ref[...], high)).astype(jnp.bfloat16)


def block_conv(lag_of_block, filt, gated):
    count, width, columns = filt.shape
    tabs = [jnp.asarray(t) for t in tables(width)]
    whole = pl.BlockSpec(memory_space=pltpu.VMEM)
    spectra = pltpu.VMEM((count, 2 * width, columns), jnp.float32)
    return pl.pallas_call(
        functools.partial(conv_kernel, count, width),
        out_shape=jax.ShapeDtypeStruct((count, width, columns), jnp.bfloat16),
        in_specs=[pl.BlockSpec(memory_space=pltpu.SMEM)] + [whole] * 6,
        out_specs=whole,
        scratch_shapes=[spectra, spectra, spectra],
        compiler_params=pltpu.CompilerParams(vmem_limit_bytes=40 * 1024 * 1024),
        cost_estimate=pl.CostEstimate(
            flops=2 * count * width * 2 * width * columns * 7,
            bytes_accessed=6 * count * width * columns,
            transcendentals=0,
        ),
    )(lag_of_block, filt, gated, *tabs)


def local(query, key_in, value_in, filter_store, lag_of_block, skip, out_gain):
    width, columns = query.shape
    count = lax.axis_size("tok")
    part = columns // count

    def to_channels(x):
        return lax.all_to_all(x.reshape(width, count, part).transpose(1, 0, 2), "tok", 0, 0, tiled=True)

    filt_all = to_channels(filter_store)
    gated = (key_in.astype(jnp.float32) * value_in.astype(jnp.float32)).astype(jnp.bfloat16)
    gated_all = to_channels(gated)
    conv_all = block_conv(lag_of_block, filt_all, gated_all)
    conv = lax.all_to_all(conv_all, "tok", 0, 0, tiled=True).transpose(1, 0, 2).reshape(width, columns)
    pre = query.astype(jnp.float32) * (conv.astype(jnp.float32) + skip[None, :] * gated.astype(jnp.float32))
    total = lax.psum(jnp.sum(pre * pre, axis=1), "chan")
    mean_sq = total / (columns * lax.axis_size("chan"))
    return out_gain[None, :] * pre * lax.rsqrt(mean_sq + 1e-06)[:, None]


def solution(mesh):
    in_specs = (
        P("tok", "chan"),
        P("tok", "chan"),
        P("tok", "chan"),
        P("tok", "chan"),
        P(),
        P("chan"),
        P("chan"),
    )
    return jax.shard_map(local, mesh=mesh, in_specs=in_specs, out_specs=P("tok", "chan"), check_vma=False)
```

```python
import functools
import math

import jax
import jax.numpy as jnp
import ml_dtypes
import numpy as np
from jax import lax
from jax.experimental import pallas as pl
from jax.experimental.pallas import tpu as pltpu
from jax.sharding import PartitionSpec as P

MIB = 1024 * 1024
WHOLE = pl.BlockSpec(memory_space=pltpu.VMEM)
IN_HBM = pl.BlockSpec(memory_space=pltpu.HBM)


def split_bf16(table):
    high = table.astype(ml_dtypes.bfloat16)
    low = (table - high.astype(np.float64)).astype(ml_dtypes.bfloat16)
    return high, low


def tables(width):
    freq = np.concatenate([np.arange(0, width, 2), np.arange(1, width, 2)])
    place = np.arange(width)
    steps = ((2 * freq[:, None] + 1) * place[None, :]) % (4 * width)
    angle = math.pi / (2 * width) * steps
    forward = np.concatenate([np.cos(angle), -np.sin(angle)], axis=0)
    inverse = forward.T / width
    return split_bf16(forward) + split_bf16(inverse)


def gate_kernel(count, part, key_ref, value_ref, filt_ref, out_ref, key_buf, value_buf, sems, filt_sems):
    width = key_ref.shape[0]
    copies = []
    for j in range(count):
        cols = pl.ds(j * part, part)
        copies.append(
            (
                pltpu.make_async_copy(key_ref.at[:, cols], key_buf.at[j], sems.at[0, j]),
                pltpu.make_async_copy(value_ref.at[:, cols], value_buf.at[j], sems.at[1, j]),
            )
        )
        for copy in copies[-1]:
            copy.start()
    filts = []
    for j in range(count):
        cols = pl.ds(j * part, part)
        filts.append(pltpu.make_async_copy(filt_ref.at[:, cols], out_ref.at[j, pl.ds(0, width), :], filt_sems.at[j]))
        filts[-1].start()
    for j in range(count):
        for copy in copies[j]:
            copy.wait()
        product = key_buf[j].astype(jnp.float32) * value_buf[j].astype(jnp.float32)
        out_ref[j, pl.ds(width, width), :] = product.astype(jnp.bfloat16)
    for copy in filts:
        copy.wait()


def gate(count, key_in, value_in, filter_store):
    width, columns = key_in.shape
    part = columns // count
    if part % 128:
        gated = (key_in.astype(jnp.float32) * value_in.astype(jnp.float32)).astype(jnp.bfloat16)
        both = jnp.concatenate([filter_store, gated], axis=0)
        return both.reshape(2 * width, count, part).transpose(1, 0, 2)
    block = pltpu.VMEM((count, width, part), jnp.bfloat16)
    return pl.pallas_call(
        functools.partial(gate_kernel, count, part),
        out_shape=jax.ShapeDtypeStruct((count, 2 * width, part), jnp.bfloat16),
        in_specs=[IN_HBM] * 3,
        out_specs=WHOLE,
        scratch_shapes=[block, block, pltpu.SemaphoreType.DMA((2, count)), pltpu.SemaphoreType.DMA((count,))],
        compiler_params=pltpu.CompilerParams(vmem_limit_bytes=16 * MIB),
        cost_estimate=pl.CostEstimate(flops=width * columns, bytes_accessed=10 * width * columns, transcendentals=0),
    )(key_in, value_in, filter_store)


def conv_kernel(count, width, lag_ref, fg_ref, fh_ref, fl_ref, ih_ref, il_ref, out_ref, fs, gs, ss):
    dot = functools.partial(jnp.dot, preferred_element_type=jnp.float32)
    for i in range(count):
        filt, gated = fg_ref[i, pl.ds(0, width), :], fg_ref[i, pl.ds(width, width), :]
        fs[lag_ref[i]] = dot(fh_ref[...], filt) + dot(fl_ref[...], filt)
        gs[i] = dot(fh_ref[...], gated) + dot(fl_ref[...], gated)
    columns = fg_ref.shape[2]
    lane = min(128, columns)

    def products(row, sign):
        re_rows = pl.ds(pl.multiple_of(row * 8, 8), 8)
        im_rows = pl.ds(pl.multiple_of(row * 8 + width, 8), 8)
        for at in range(0, columns, lane):
            lanes = pl.ds(at, lane)
            f_re = [fs[i, re_rows, lanes] for i in range(count)]
            f_im = [fs[i, im_rows, lanes] for i in range(count)]
            h_re, h_im = [], []
            for i in range(count):
                g_re, g_im = gs[i, re_rows, lanes], gs[i, im_rows, lanes]
                if i == 0:
                    h_re.append(g_re)
                    h_im.append(g_im)
                elif sign > 0:
                    h_re.append(g_re - last_im)
                    h_im.append(g_im + last_re)
                else:
                    h_re.append(g_re + last_im)
                    h_im.append(g_im - last_re)
                last_re, last_im = g_re, g_im
            for j in range(count):
                s_re = f_re[0] * h_re[j] - f_im[0] * h_im[j]
                s_im = f_re[0] * h_im[j] + f_im[0] * h_re[j]
                for i in range(1, j + 1):
                    s_re = s_re + f_re[i] * h_re[j - i] - f_im[i] * h_im[j - i]
                    s_im = s_im + f_re[i] * h_im[j - i] + f_im[i] * h_re[j - i]
                ss[j, re_rows, lanes] = s_re
                ss[j, im_rows, lanes] = s_im

    half = width // 16

    @pl.loop(0, half)
    def _(row):
        products(row, 1)

    @pl.loop(half, 2 * half)
    def _(row):
        products(row, -1)

    for j in range(count):
        total = ss[j]
        high = total.astype(jnp.bfloat16)
        low = (total - high.astype(jnp.float32)).astype(jnp.bfloat16)
        out_ref[j] = (dot(ih_ref[...], high) + dot(ih_ref[...], low) + dot(il_ref[...], high)).astype(jnp.bfloat16)


def block_conv(lag_of_block, both):
    count, twice, columns = both.shape
    width = twice // 2
    tabs = [jnp.asarray(t) for t in tables(width)]
    spectra = pltpu.VMEM((count, 2 * width, columns), jnp.float32)
    return pl.pallas_call(
        functools.partial(conv_kernel, count, width),
        out_shape=jax.ShapeDtypeStruct((count, width, columns), jnp.bfloat16),
        in_specs=[pl.BlockSpec(memory_space=pltpu.SMEM)] + [WHOLE] * 5,
        out_specs=WHOLE,
        scratch_shapes=[spectra, spectra, spectra],
        compiler_params=pltpu.CompilerParams(vmem_limit_bytes=32 * MIB),
        cost_estimate=pl.CostEstimate(
            flops=2 * count * width * 2 * width * columns * 7,
            bytes_accessed=6 * count * width * columns,
            transcendentals=0,
        ),
    )(lag_of_block, both, *tabs)


def pre_kernel(query_ref, conv_ref, both_ref, skip_ref, pre_ref, square_ref):
    count, width, part = conv_ref.shape
    total = jnp.zeros((width, 128), jnp.float32)
    for j in range(count):
        for at in range(0, part, 128):
            lanes, cols = pl.ds(at, 128), pl.ds(j * part + at, 128)
            gated = both_ref[j, pl.ds(width, width), lanes].astype(jnp.float32)
            conv = conv_ref[j, :, lanes].astype(jnp.float32)
            pre = query_ref[:, cols].astype(jnp.float32) * (conv + skip_ref[:, cols] * gated)
            pre_ref[:, cols] = pre
            total = total + pre * pre
    square_ref[...] = jnp.sum(total.T, axis=0, keepdims=True)


def gated_output(query, conv, both, skip):
    width, columns = query.shape
    return pl.pallas_call(
        pre_kernel,
        out_shape=(
            jax.ShapeDtypeStruct((width, columns), jnp.float32),
            jax.ShapeDtypeStruct((1, width), jnp.float32),
        ),
        in_specs=[WHOLE] * 4,
        out_specs=(WHOLE, WHOLE),
        compiler_params=pltpu.CompilerParams(vmem_limit_bytes=16 * MIB),
        cost_estimate=pl.CostEstimate(flops=6 * width * columns, bytes_accessed=10 * width * columns, transcendentals=0),
    )(query, conv, both, skip)


def scale_kernel(channels, steps, pre_ref, square_ref, gain_ref, out_ref, buf, sems):
    width = pre_ref.shape[0]
    rows = width // steps
    scale = lax.rsqrt(square_ref[...] * (1.0 / channels) + 1e-06)
    scale = jnp.broadcast_to(scale, (128, width)).T
    copies = []
    for s in range(steps):
        for at in range(0, pre_ref.shape[1], 128):
            cols = pl.ds(at, 128)
            here = scale[s * rows : (s + 1) * rows, :]
            buf[pl.ds(s * rows, rows), cols] = gain_ref[:, cols] * pre_ref[pl.ds(s * rows, rows), cols] * here
        window = pl.ds(s * rows, rows)
        copies.append(pltpu.make_async_copy(buf.at[window, :], out_ref.at[window, :], sems.at[s]))
        copies[-1].start()
    for copy in copies:
        copy.wait()


def scaled(channels, pre, square, out_gain):
    width, columns = pre.shape
    steps = 8
    return pl.pallas_call(
        functools.partial(scale_kernel, channels, steps),
        out_shape=jax.ShapeDtypeStruct((width, columns), jnp.float32),
        in_specs=[WHOLE] * 3,
        out_specs=IN_HBM,
        scratch_shapes=[pltpu.VMEM((width, columns), jnp.float32), pltpu.SemaphoreType.DMA((steps,))],
        compiler_params=pltpu.CompilerParams(vmem_limit_bytes=16 * MIB),
        cost_estimate=pl.CostEstimate(flops=2 * width * columns, bytes_accessed=8 * width * columns, transcendentals=0),
    )(pre, square, out_gain)


def local(query, key_in, value_in, filter_store, lag_of_block, skip, out_gain):
    width, columns = query.shape
    count = lax.axis_size("tok")
    both = gate(count, key_in, value_in, filter_store)
    everywhere = lax.all_to_all(both, "tok", 0, 0, tiled=True)
    conv = lax.all_to_all(block_conv(lag_of_block, everywhere), "tok", 0, 0, tiled=True)
    if conv.shape[2] % 128:
        conv = conv.transpose(1, 0, 2).reshape(1, width, columns)
        both = both.transpose(1, 0, 2).reshape(1, 2 * width, columns)
    pre, square = gated_output(query, conv, both, skip[None, :])
    square = lax.psum(square, "chan")
    return scaled(columns * lax.axis_size("chan"), pre, square, out_gain[None, :])


def solution(mesh):
    in_specs = (
        P("tok", "chan"),
        P("tok", "chan"),
        P("tok", "chan"),
        P("tok", "chan"),
        P(),
        P("chan"),
        P("chan"),
    )
    return jax.shard_map(local, mesh=mesh, in_specs=in_specs, out_specs=P("tok", "chan"), check_vma=False)
```

```python
import functools
import math

import jax
import jax.numpy as jnp
import ml_dtypes
import numpy as np
from jax import lax
from jax.experimental import pallas as pl
from jax.experimental.pallas import tpu as pltpu
from jax.sharding import PartitionSpec as P

MIB = 1024 * 1024
BIG = 48 * MIB
WHOLE = pl.BlockSpec(memory_space=pltpu.VMEM)
IN_HBM = pl.BlockSpec(memory_space=pltpu.HBM)


def split_bf16(table):
    high = table.astype(ml_dtypes.bfloat16)
    low = (table - high.astype(np.float64)).astype(ml_dtypes.bfloat16)
    return high, low


def tables(width):
    freq = np.concatenate([np.arange(0, width, 2), np.arange(1, width, 2)])
    place = np.arange(width)
    steps = ((2 * freq[:, None] + 1) * place[None, :]) % (4 * width)
    angle = math.pi / (2 * width) * steps
    forward = np.concatenate([np.cos(angle), -np.sin(angle)], axis=0)
    inverse = forward.T / width
    return split_bf16(forward) + split_bf16(inverse)


def partner(step):
    return lax.axis_index("tok") ^ step


def exchange(blocks):
    count = len(blocks)
    return [blocks[0]] + [
        lax.ppermute(blocks[k], "tok", [(d, d ^ k) for d in range(count)]) for k in range(1, count)
    ]


def columns_of(step, part):
    return pl.ds(pl.multiple_of(partner(step) * part, 128), part)


def split_kernel(count, part, filt_ref, *refs):
    outs, sems = refs[:count], refs[count]
    copies = []
    for k in range(count):
        copies.append(pltpu.make_async_copy(filt_ref.at[:, columns_of(k, part)], outs[k], sems.at[k]))
        copies[-1].start()
    for copy in copies:
        copy.wait()


def gate_kernel(count, part, key_ref, value_ref, *refs):
    outs, (key_buf, value_buf, sems) = refs[:count], refs[count:]
    copies = []
    for k in range(count):
        cols = columns_of(k, part)
        copies.append(
            (
                pltpu.make_async_copy(key_ref.at[:, cols], key_buf.at[k], sems.at[0, k]),
                pltpu.make_async_copy(value_ref.at[:, cols], value_buf.at[k], sems.at[1, k]),
            )
        )
        for copy in copies[-1]:
            copy.start()
    for k in range(count):
        for copy in copies[k]:
            copy.wait()
        product = key_buf[k].astype(jnp.float32) * value_buf[k].astype(jnp.float32)
        outs[k][...] = product.astype(jnp.bfloat16)


def pieces(x, count):
    part = x.shape[1] // count
    return [lax.dynamic_slice_in_dim(x, partner(k) * part, part, axis=1) for k in range(count)]


def split(count, filter_store):
    width, columns = filter_store.shape
    part = columns // count
    if part % 128:
        return pieces(filter_store, count)
    return pl.pallas_call(
        functools.partial(split_kernel, count, part),
        out_shape=[jax.ShapeDtypeStruct((width, part), jnp.bfloat16)] * count,
        in_specs=[IN_HBM],
        out_specs=[WHOLE] * count,
        scratch_shapes=[pltpu.SemaphoreType.DMA((count,))],
        compiler_params=pltpu.CompilerParams(vmem_limit_bytes=BIG),
        cost_estimate=pl.CostEstimate(flops=0, bytes_accessed=4 * width * columns, transcendentals=0),
    )(filter_store)


def gate(count, key_in, value_in):
    width, columns = key_in.shape
    part = columns // count
    if part % 128:
        gated = (key_in.astype(jnp.float32) * value_in.astype(jnp.float32)).astype(jnp.bfloat16)
        return pieces(gated, count)
    block = pltpu.VMEM((count, width, part), jnp.bfloat16)
    return pl.pallas_call(
        functools.partial(gate_kernel, count, part),
        out_shape=[jax.ShapeDtypeStruct((width, part), jnp.bfloat16)] * count,
        in_specs=[IN_HBM] * 2,
        out_specs=[WHOLE] * count,
        scratch_shapes=[block, block, pltpu.SemaphoreType.DMA((2, count))],
        compiler_params=pltpu.CompilerParams(vmem_limit_bytes=BIG),
        cost_estimate=pl.CostEstimate(flops=width * columns, bytes_accessed=6 * width * columns, transcendentals=0),
    )(key_in, value_in)


def conv_kernel(count, width, lag_ref, fh_ref, fl_ref, ih_ref, il_ref, *refs):
    filts, gates, outs, (fs, gs, ss) = refs[:count], refs[count : 2 * count], refs[2 * count : 3 * count], refs[3 * count :]
    dot = functools.partial(jnp.dot, preferred_element_type=jnp.float32)
    for k in range(count):
        filt, gated = filts[k][...], gates[k][...]
        fs[lag_ref[partner(k)]] = dot(fh_ref[...], filt) + dot(fl_ref[...], filt)
        gs[partner(k)] = dot(fh_ref[...], gated) + dot(fl_ref[...], gated)
    columns = filts[0].shape[1]
    lane = min(128, columns)

    def products(row, sign):
        re_rows = pl.ds(pl.multiple_of(row * 8, 8), 8)
        im_rows = pl.ds(pl.multiple_of(row * 8 + width, 8), 8)
        for at in range(0, columns, lane):
            lanes = pl.ds(at, lane)
            f_re = [fs[i, re_rows, lanes] for i in range(count)]
            f_im = [fs[i, im_rows, lanes] for i in range(count)]
            h_re, h_im = [], []
            for i in range(count):
                g_re, g_im = gs[i, re_rows, lanes], gs[i, im_rows, lanes]
                if i == 0:
                    h_re.append(g_re)
                    h_im.append(g_im)
                elif sign > 0:
                    h_re.append(g_re - last_im)
                    h_im.append(g_im + last_re)
                else:
                    h_re.append(g_re + last_im)
                    h_im.append(g_im - last_re)
                last_re, last_im = g_re, g_im
            for j in range(count):
                s_re = f_re[0] * h_re[j] - f_im[0] * h_im[j]
                s_im = f_re[0] * h_im[j] + f_im[0] * h_re[j]
                for i in range(1, j + 1):
                    s_re = s_re + f_re[i] * h_re[j - i] - f_im[i] * h_im[j - i]
                    s_im = s_im + f_re[i] * h_im[j - i] + f_im[i] * h_re[j - i]
                ss[j, re_rows, lanes] = s_re
                ss[j, im_rows, lanes] = s_im

    half = width // 16

    @pl.loop(0, half)
    def _(row):
        products(row, 1)

    @pl.loop(half, 2 * half)
    def _(row):
        products(row, -1)

    for k in range(count):
        total = ss[partner(k)]
        high = total.astype(jnp.bfloat16)
        low = (total - high.astype(jnp.float32)).astype(jnp.bfloat16)
        outs[k][...] = (dot(ih_ref[...], high) + dot(ih_ref[...], low) + dot(il_ref[...], high)).astype(jnp.bfloat16)


def block_conv(lag_of_block, filts, gates):
    count = len(filts)
    width, columns = filts[0].shape
    tabs = [jnp.asarray(t) for t in tables(width)]
    spectra = pltpu.VMEM((count, 2 * width, columns), jnp.float32)
    return pl.pallas_call(
        functools.partial(conv_kernel, count, width),
        out_shape=[jax.ShapeDtypeStruct((width, columns), jnp.bfloat16)] * count,
        in_specs=[pl.BlockSpec(memory_space=pltpu.SMEM)] + [WHOLE] * (4 + 2 * count),
        out_specs=[WHOLE] * count,
        scratch_shapes=[spectra, spectra, spectra],
        compiler_params=pltpu.CompilerParams(vmem_limit_bytes=32 * MIB),
        cost_estimate=pl.CostEstimate(
            flops=2 * count * width * 2 * width * columns * 7,
            bytes_accessed=6 * count * width * columns,
            transcendentals=0,
        ),
    )(lag_of_block, *tabs, *filts, *gates)


def pre_kernel(count, query_ref, skip_ref, *refs):
    convs, gates, (pre_ref, square_ref) = refs[:count], refs[count : 2 * count], refs[2 * count :]
    width, part = convs[0].shape
    total = jnp.zeros((width, 128), jnp.float32)
    for k in range(count):
        start = partner(k) * part if count > 1 else 0
        for at in range(0, part, 128):
            lanes, cols = pl.ds(at, 128), pl.ds(pl.multiple_of(start + at, 128), 128)
            gated = gates[k][:, lanes].astype(jnp.float32)
            conv = convs[k][:, lanes].astype(jnp.float32)
            pre = query_ref[:, cols].astype(jnp.float32) * (conv + skip_ref[:, cols] * gated)
            pre_ref[:, cols] = pre
            total = total + pre * pre
    square_ref[...] = jnp.sum(total.T, axis=0, keepdims=True)


def together(blocks):
    count = len(blocks)
    order = jnp.arange(count, dtype=jnp.int32) ^ lax.axis_index("tok")
    stacked = jnp.take(jnp.stack(blocks), order, axis=0)
    return [stacked.transpose(1, 0, 2).reshape(blocks[0].shape[0], -1)]


def gated_output(query, skip, convs, gates):
    width, columns = query.shape
    if convs[0].shape[1] % 128:
        convs, gates = together(convs), together(gates)
    count = len(convs)
    return pl.pallas_call(
        functools.partial(pre_kernel, count),
        out_shape=(
            jax.ShapeDtypeStruct((width, columns), jnp.float32),
            jax.ShapeDtypeStruct((1, width), jnp.float32),
        ),
        in_specs=[WHOLE] * (2 + 2 * count),
        out_specs=(WHOLE, WHOLE),
        compiler_params=pltpu.CompilerParams(vmem_limit_bytes=16 * MIB),
        cost_estimate=pl.CostEstimate(flops=6 * width * columns, bytes_accessed=10 * width * columns, transcendentals=0),
    )(query, skip, *convs, *gates)


def scale_kernel(channels, steps, pre_ref, square_ref, gain_ref, out_ref, buf, sems):
    width = pre_ref.shape[0]
    rows = width // steps
    scale = lax.rsqrt(square_ref[...] * (1.0 / channels) + 1e-06)
    scale = jnp.broadcast_to(scale, (128, width)).T
    copies = []
    for s in range(steps):
        for at in range(0, pre_ref.shape[1], 128):
            cols = pl.ds(at, 128)
            here = scale[s * rows : (s + 1) * rows, :]
            buf[pl.ds(s * rows, rows), cols] = gain_ref[:, cols] * pre_ref[pl.ds(s * rows, rows), cols] * here
        window = pl.ds(s * rows, rows)
        copies.append(pltpu.make_async_copy(buf.at[window, :], out_ref.at[window, :], sems.at[s]))
        copies[-1].start()
    for copy in copies:
        copy.wait()


def scaled(channels, pre, square, out_gain):
    width, columns = pre.shape
    steps = 8
    return pl.pallas_call(
        functools.partial(scale_kernel, channels, steps),
        out_shape=jax.ShapeDtypeStruct((width, columns), jnp.float32),
        in_specs=[WHOLE] * 3,
        out_specs=IN_HBM,
        scratch_shapes=[pltpu.VMEM((width, columns), jnp.float32), pltpu.SemaphoreType.DMA((steps,))],
        compiler_params=pltpu.CompilerParams(vmem_limit_bytes=16 * MIB),
        cost_estimate=pl.CostEstimate(flops=2 * width * columns, bytes_accessed=8 * width * columns, transcendentals=0),
    )(pre, square, out_gain)


def local(query, key_in, value_in, filter_store, lag_of_block, skip, out_gain):
    width, columns = query.shape
    count = lax.axis_size("tok")
    filts = exchange(split(count, filter_store))
    mine = gate(count, key_in, value_in)
    convs = exchange(block_conv(lag_of_block, filts, exchange(mine)))
    pre, square = gated_output(query, skip[None, :], convs, mine)
    square = lax.psum(square, "chan")
    return scaled(columns * lax.axis_size("chan"), pre, square, out_gain[None, :])


def solution(mesh):
    in_specs = (
        P("tok", "chan"),
        P("tok", "chan"),
        P("tok", "chan"),
        P("tok", "chan"),
        P(),
        P("chan"),
        P("chan"),
    )
    return jax.shard_map(local, mesh=mesh, in_specs=in_specs, out_specs=P("tok", "chan"), check_vma=False)
```

```python
import functools
import math

import jax
import jax.numpy as jnp
import ml_dtypes
import numpy as np
from jax import lax
from jax.experimental import pallas as pl
from jax.experimental.pallas import tpu as pltpu
from jax.sharding import PartitionSpec as P

MIB = 1024 * 1024
BIG = 48 * MIB
WHOLE = pl.BlockSpec(memory_space=pltpu.VMEM)
IN_HBM = pl.BlockSpec(memory_space=pltpu.HBM)


def split_bf16(table):
    high = table.astype(ml_dtypes.bfloat16)
    low = (table - high.astype(np.float64)).astype(ml_dtypes.bfloat16)
    return high, low


def tables(width):
    freq = np.concatenate([np.arange(0, width, 2), np.arange(1, width, 2)])
    place = np.arange(width)
    steps = ((2 * freq[:, None] + 1) * place[None, :]) % (4 * width)
    angle = math.pi / (2 * width) * steps
    forward = np.concatenate([np.cos(angle), -np.sin(angle)], axis=0)
    inverse = forward.T / width
    return split_bf16(forward) + split_bf16(inverse)


def partner(step):
    return lax.axis_index("tok") ^ step


def send(block, step, count):
    return lax.ppermute(block, "tok", [(d, d ^ step) for d in range(count)])


def far_first(count):
    half = count // 2
    far = list(range(half, count, 2)) + list(range(half + 1, count, 2))
    near = list(range(2, half)) + [1]
    return far, near


def columns_of(step, part):
    return pl.ds(pl.multiple_of(partner(step) * part, 128), part)


def split_kernel(count, part, filt_ref, *refs):
    outs, sems = refs[:count], refs[count]
    copies = []
    for k in range(count):
        copies.append(pltpu.make_async_copy(filt_ref.at[:, columns_of(k, part)], outs[k], sems.at[k]))
        copies[-1].start()
    for copy in copies:
        copy.wait()


def gate_kernel(count, part, key_ref, value_ref, *refs):
    outs, (key_buf, value_buf, sems) = refs[:count], refs[count:]
    copies = []
    for k in range(count):
        cols = columns_of(k, part)
        copies.append(
            (
                pltpu.make_async_copy(key_ref.at[:, cols], key_buf.at[k], sems.at[0, k]),
                pltpu.make_async_copy(value_ref.at[:, cols], value_buf.at[k], sems.at[1, k]),
            )
        )
        for copy in copies[-1]:
            copy.start()
    for k in range(count):
        for copy in copies[k]:
            copy.wait()
        product = key_buf[k].astype(jnp.float32) * value_buf[k].astype(jnp.float32)
        outs[k][...] = product.astype(jnp.bfloat16)


def pieces(x, count):
    part = x.shape[1] // count
    return [lax.dynamic_slice_in_dim(x, partner(k) * part, part, axis=1) for k in range(count)]


def split(count, filter_store):
    width, columns = filter_store.shape
    part = columns // count
    if part % 128:
        return pieces(filter_store, count)
    return pl.pallas_call(
        functools.partial(split_kernel, count, part),
        out_shape=[jax.ShapeDtypeStruct((width, part), jnp.bfloat16)] * count,
        in_specs=[IN_HBM],
        out_specs=[WHOLE] * count,
        scratch_shapes=[pltpu.SemaphoreType.DMA((count,))],
        compiler_params=pltpu.CompilerParams(vmem_limit_bytes=BIG),
        cost_estimate=pl.CostEstimate(flops=0, bytes_accessed=4 * width * columns, transcendentals=0),
    )(filter_store)


def gate(count, key_in, value_in):
    width, columns = key_in.shape
    part = columns // count
    if part % 128:
        gated = (key_in.astype(jnp.float32) * value_in.astype(jnp.float32)).astype(jnp.bfloat16)
        return pieces(gated, count)
    block = pltpu.VMEM((count, width, part), jnp.bfloat16)
    return pl.pallas_call(
        functools.partial(gate_kernel, count, part),
        out_shape=[jax.ShapeDtypeStruct((width, part), jnp.bfloat16)] * count,
        in_specs=[IN_HBM] * 2,
        out_specs=[WHOLE] * count,
        scratch_shapes=[block, block, pltpu.SemaphoreType.DMA((2, count))],
        compiler_params=pltpu.CompilerParams(vmem_limit_bytes=BIG),
        cost_estimate=pl.CostEstimate(flops=width * columns, bytes_accessed=6 * width * columns, transcendentals=0),
    )(key_in, value_in)


def dot(x, y):
    return jnp.dot(x, y, preferred_element_type=jnp.float32)


def transform(high, low, block):
    return dot(high, block) + dot(low, block)


def filter_kernel(steps, lag_ref, high_ref, low_ref, *refs):
    blocks, out = refs[:-1], refs[-1]
    for k, block in zip(steps, blocks):
        out[lag_ref[partner(k)]] = transform(high_ref[...], low_ref[...], block[...])


def gated_kernel(steps, high_ref, low_ref, *refs):
    blocks, out = refs[:-1], refs[-1]
    for k, block in zip(steps, blocks):
        out[partner(k)] = transform(high_ref[...], low_ref[...], block[...])


def spectra_shape(count, block):
    width, columns = block.shape
    return jax.ShapeDtypeStruct((count, 2 * width, columns), jnp.float32)


def transform_cost(count, block, passes):
    width, columns = block.shape
    return pl.CostEstimate(
        flops=4 * passes * count * width * width * columns,
        bytes_accessed=10 * count * width * columns,
        transcendentals=0,
    )


def filter_spectra(lag_of_block, high, low, blocks):
    steps = list(blocks)
    return pl.pallas_call(
        functools.partial(filter_kernel, steps),
        out_shape=spectra_shape(len(steps), blocks[steps[0]]),
        in_specs=[pl.BlockSpec(memory_space=pltpu.SMEM)] + [WHOLE] * (2 + len(steps)),
        out_specs=WHOLE,
        compiler_params=pltpu.CompilerParams(vmem_limit_bytes=16 * MIB),
        cost_estimate=transform_cost(len(steps), blocks[steps[0]], 2),
    )(lag_of_block, high, low, *[blocks[k] for k in steps])


def gated_spectra(count, high, low, blocks):
    steps = list(blocks)
    return pl.pallas_call(
        functools.partial(gated_kernel, steps),
        out_shape=spectra_shape(count, blocks[steps[0]]),
        in_specs=[WHOLE] * (2 + len(steps)),
        out_specs=WHOLE,
        compiler_params=pltpu.CompilerParams(vmem_limit_bytes=16 * MIB),
        cost_estimate=transform_cost(len(steps), blocks[steps[0]], 2),
    )(high, low, *[blocks[k] for k in steps])


def product_kernel(count, steps, first, fh_ref, fl_ref, ih_ref, il_ref, fs, gs, *refs):
    blocks, (gs, sh, sl), outs, ss = refs[: len(steps)], refs[len(steps) : len(steps) + 3], refs[len(steps) + 3 : -1], refs[-1]
    width, columns = outs[0].shape
    for k, block in zip(steps, blocks):
        gs[partner(k)] = transform(fh_ref[...], fl_ref[...], block[...])
    lane = min(128, columns)

    def products(row, sign):
        re_rows = pl.ds(pl.multiple_of(row * 8, 8), 8)
        im_rows = pl.ds(pl.multiple_of(row * 8 + width, 8), 8)
        for at in range(0, columns, lane):
            lanes = pl.ds(at, lane)
            f_re = [fs[i, re_rows, lanes] for i in range(count)]
            f_im = [fs[i, im_rows, lanes] for i in range(count)]
            h_re, h_im = [], []
            for i in range(count):
                g_re, g_im = gs[i, re_rows, lanes], gs[i, im_rows, lanes]
                if i == 0:
                    h_re.append(g_re)
                    h_im.append(g_im)
                elif sign > 0:
                    h_re.append(g_re - last_im)
                    h_im.append(g_im + last_re)
                else:
                    h_re.append(g_re + last_im)
                    h_im.append(g_im - last_re)
                last_re, last_im = g_re, g_im
            for j in range(count):
                s_re = f_re[0] * h_re[j] - f_im[0] * h_im[j]
                s_im = f_re[0] * h_im[j] + f_im[0] * h_re[j]
                for i in range(1, j + 1):
                    s_re = s_re + f_re[i] * h_re[j - i] - f_im[i] * h_im[j - i]
                    s_im = s_im + f_re[i] * h_im[j - i] + f_im[i] * h_re[j - i]
                ss[j, re_rows, lanes] = s_re
                ss[j, im_rows, lanes] = s_im

    half = width // 16

    @pl.loop(0, half)
    def _(row):
        products(row, 1)

    @pl.loop(half, 2 * half)
    def _(row):
        products(row, -1)

    for at, k in enumerate(first + [k for k in range(count) if k not in first]):
        total = ss[partner(k)]
        high = total.astype(jnp.bfloat16)
        low = (total - high.astype(jnp.float32)).astype(jnp.bfloat16)
        if k in first:
            outs[at][...] = inverse(ih_ref[...], il_ref[...], high, low)
        else:
            sh[partner(k)] = high
            sl[partner(k)] = low


def inverse(table_high, table_low, high, low):
    return (dot(table_high, high) + dot(table_high, low) + dot(table_low, high)).astype(jnp.bfloat16)


def products(count, first, tabs, filt, gated, blocks):
    steps = list(blocks)
    width, columns = blocks[steps[0]].shape
    half = jax.ShapeDtypeStruct((count, 2 * width, columns), jnp.bfloat16)
    found = pl.pallas_call(
        functools.partial(product_kernel, count, steps, first),
        out_shape=[jax.ShapeDtypeStruct(gated.shape, jnp.float32), half, half]
        + [jax.ShapeDtypeStruct((width, columns), jnp.bfloat16)] * len(first),
        in_specs=[WHOLE] * (6 + len(steps)),
        out_specs=[WHOLE] * (3 + len(first)),
        scratch_shapes=[pltpu.VMEM(gated.shape, jnp.float32)],
        input_output_aliases={5: 0},
        compiler_params=pltpu.CompilerParams(vmem_limit_bytes=20 * MIB),
        cost_estimate=transform_cost(count, blocks[steps[0]], 7),
    )(*tabs, filt, gated, *[blocks[k] for k in steps])
    return found[1], found[2], dict(zip(first, found[3:]))


def inverse_kernel(steps, ih_ref, il_ref, sh, sl, *outs):
    for k, out in zip(steps, outs):
        out[...] = inverse(ih_ref[...], il_ref[...], sh[partner(k)], sl[partner(k)])


def inverses(steps, tabs, high, low):
    count, twice, columns = high.shape
    block = jax.ShapeDtypeStruct((twice // 2, columns), jnp.bfloat16)
    found = pl.pallas_call(
        functools.partial(inverse_kernel, steps),
        out_shape=[block] * len(steps),
        in_specs=[WHOLE] * 4,
        out_specs=[WHOLE] * len(steps),
        compiler_params=pltpu.CompilerParams(vmem_limit_bytes=16 * MIB),
        cost_estimate=transform_cost(len(steps), block, 3),
    )(*tabs[2:], high, low)
    return dict(zip(steps, found))


def pre_kernel(steps, query_ref, skip_ref, *refs):
    count = len(steps)
    convs, gates, (pre_ref, square_ref) = refs[:count], refs[count : 2 * count], refs[2 * count :]
    width, part = convs[0].shape
    total = jnp.zeros((width, 128), jnp.float32)
    for at_k, k in enumerate(steps):
        start = partner(k) * part if count > 1 else 0
        for at in range(0, part, 128):
            lanes, cols = pl.ds(at, 128), pl.ds(pl.multiple_of(start + at, 128), 128)
            gated = gates[at_k][:, lanes].astype(jnp.float32)
            conv = convs[at_k][:, lanes].astype(jnp.float32)
            pre = query_ref[:, cols].astype(jnp.float32) * (conv + skip_ref[:, cols] * gated)
            pre_ref[:, cols] = pre
            total = total + pre * pre
    square_ref[...] = jnp.sum(total.T, axis=0, keepdims=True)


def together(blocks):
    blocks = [blocks[k] for k in range(len(blocks))]
    count = len(blocks)
    order = jnp.arange(count, dtype=jnp.int32) ^ lax.axis_index("tok")
    stacked = jnp.take(jnp.stack(blocks), order, axis=0)
    return {0: stacked.transpose(1, 0, 2).reshape(blocks[0].shape[0], -1)}


def gated_output(query, skip, convs, gates):
    width, columns = query.shape
    steps = list(convs)
    if convs[0].shape[1] % 128:
        convs, gates, steps = together(convs), together(gates), [0]
    count = len(steps)
    return pl.pallas_call(
        functools.partial(pre_kernel, steps),
        out_shape=(
            jax.ShapeDtypeStruct((width, columns), jnp.float32),
            jax.ShapeDtypeStruct((1, width), jnp.float32),
        ),
        in_specs=[WHOLE] * (2 + 2 * count),
        out_specs=(WHOLE, WHOLE),
        compiler_params=pltpu.CompilerParams(vmem_limit_bytes=16 * MIB),
        cost_estimate=pl.CostEstimate(flops=6 * width * columns, bytes_accessed=10 * width * columns, transcendentals=0),
    )(query, skip, *[convs[k] for k in steps], *[gates[k] for k in steps])


def scale_kernel(channels, steps, pre_ref, square_ref, gain_ref, out_ref, buf, sems):
    width = pre_ref.shape[0]
    rows = width // steps
    scale = lax.rsqrt(square_ref[...] * (1.0 / channels) + 1e-06)
    scale = jnp.broadcast_to(scale, (128, width)).T
    copies = []
    for s in range(steps):
        for at in range(0, pre_ref.shape[1], 128):
            cols = pl.ds(at, 128)
            here = scale[s * rows : (s + 1) * rows, :]
            buf[pl.ds(s * rows, rows), cols] = gain_ref[:, cols] * pre_ref[pl.ds(s * rows, rows), cols] * here
        window = pl.ds(s * rows, rows)
        copies.append(pltpu.make_async_copy(buf.at[window, :], out_ref.at[window, :], sems.at[s]))
        copies[-1].start()
    for copy in copies:
        copy.wait()


def scaled(channels, pre, square, out_gain):
    width, columns = pre.shape
    steps = 8
    return pl.pallas_call(
        functools.partial(scale_kernel, channels, steps),
        out_shape=jax.ShapeDtypeStruct((width, columns), jnp.float32),
        in_specs=[WHOLE] * 3,
        out_specs=IN_HBM,
        scratch_shapes=[pltpu.VMEM((width, columns), jnp.float32), pltpu.SemaphoreType.DMA((steps,))],
        compiler_params=pltpu.CompilerParams(vmem_limit_bytes=16 * MIB),
        cost_estimate=pl.CostEstimate(flops=2 * width * columns, bytes_accessed=8 * width * columns, transcendentals=0),
    )(pre, square, out_gain)


def local(query, key_in, value_in, filter_store, lag_of_block, skip, out_gain):
    width, columns = query.shape
    count = lax.axis_size("tok")
    tabs = [jnp.asarray(t) for t in tables(width)]
    own = split(count, filter_store)
    held, key_in, value_in = lax.optimization_barrier((own[0], key_in, value_in))
    mine = gate(count, key_in, value_in)
    far, near = far_first(count)
    filts, gates, convs = {}, {}, {}
    for k in far + near:
        filts[k] = send(own[k], k, count)
    gated_order = []
    for at in range(max(len(far), len(near))):
        gated_order += far[at : at + 1] + near[at : at + 1]
    for k in gated_order:
        gates[k] = send(mine[k], k, count)
    filts[0], gates[0] = held, mine[0]
    filt = filter_spectra(lag_of_block, *tabs[:2], filts)
    early = gated_order[: count // 2] + [0]
    gated = gated_spectra(count, *tabs[:2], {k: gates[k] for k in early})
    first = far[:2]
    high, low, found = products(count, first, tabs, filt, gated, {k: gates[k] for k in gates if k not in early})
    rest = [k for k in far + near if k not in first] + [0]
    found.update(inverses(rest, tabs, high, low))
    for k in far + near:
        convs[k] = send(found[k], k, count)
    convs[0] = found[0]
    pre, square = gated_output(query, skip[None, :], convs, mine)
    square = lax.psum(square, "chan")
    return scaled(columns * lax.axis_size("chan"), pre, square, out_gain[None, :])


def solution(mesh):
    in_specs = (
        P("tok", "chan"),
        P("tok", "chan"),
        P("tok", "chan"),
        P("tok", "chan"),
        P(),
        P("chan"),
        P("chan"),
    )
    return jax.shard_map(local, mesh=mesh, in_specs=in_specs, out_specs=P("tok", "chan"), check_vma=False)
```

```python
import functools
import math

import jax
import jax.numpy as jnp
import ml_dtypes
import numpy as np
from jax import lax
from jax.experimental import pallas as pl
from jax.experimental.pallas import tpu as pltpu
from jax.sharding import PartitionSpec as P

MIB = 1024 * 1024
BIG = 48 * MIB
WHOLE = pl.BlockSpec(memory_space=pltpu.VMEM)
IN_HBM = pl.BlockSpec(memory_space=pltpu.HBM)


def split_bf16(table):
    high = table.astype(ml_dtypes.bfloat16)
    low = (table - high.astype(np.float64)).astype(ml_dtypes.bfloat16)
    return high, low


def tables(width):
    freq = np.concatenate([np.arange(0, width, 2), np.arange(1, width, 2)])
    place = np.arange(width)
    steps = ((2 * freq[:, None] + 1) * place[None, :]) % (4 * width)
    angle = math.pi / (2 * width) * steps
    forward = np.concatenate([np.cos(angle), -np.sin(angle)], axis=0)
    inverse = forward.T / width
    return split_bf16(forward) + split_bf16(inverse)


def partner(step):
    return lax.axis_index("tok") ^ step


def send(block, step, count):
    return lax.ppermute(block, "tok", [(d, d ^ step) for d in range(count)])


def sending_order(count):
    half = count // 2
    far = list(range(half, count, 2)) + list(range(half + 1, count, 2))
    near = list(range(2, half)) + [1]
    order = []
    for at in range(half - 1):
        order += [far[at], near[at]]
    return order[:-1] + far[-1:] + order[-1:]


def columns_of(step, part):
    return pl.ds(pl.multiple_of(partner(step) * part, 128), part)


def split_kernel(count, part, filt_ref, *refs):
    outs, sems = refs[:count], refs[count]
    copies = []
    for k in range(count):
        copies.append(pltpu.make_async_copy(filt_ref.at[:, columns_of(k, part)], outs[k], sems.at[k]))
        copies[-1].start()
    for copy in copies:
        copy.wait()


def gate_kernel(count, part, key_ref, value_ref, *refs):
    outs, (key_buf, value_buf, sems) = refs[:count], refs[count:]
    copies = []
    for k in range(count):
        cols = columns_of(k, part)
        copies.append(
            (
                pltpu.make_async_copy(key_ref.at[:, cols], key_buf.at[k], sems.at[0, k]),
                pltpu.make_async_copy(value_ref.at[:, cols], value_buf.at[k], sems.at[1, k]),
            )
        )
        for copy in copies[-1]:
            copy.start()
    for k in range(count):
        for copy in copies[k]:
            copy.wait()
        product = key_buf[k].astype(jnp.float32) * value_buf[k].astype(jnp.float32)
        outs[k][...] = product.astype(jnp.bfloat16)


def pieces(x, count):
    part = x.shape[1] // count
    return [lax.dynamic_slice_in_dim(x, partner(k) * part, part, axis=1) for k in range(count)]


def split(count, filter_store):
    width, columns = filter_store.shape
    part = columns // count
    if part % 128:
        return pieces(filter_store, count)
    return pl.pallas_call(
        functools.partial(split_kernel, count, part),
        out_shape=[jax.ShapeDtypeStruct((width, part), jnp.bfloat16)] * count,
        in_specs=[IN_HBM],
        out_specs=[WHOLE] * count,
        scratch_shapes=[pltpu.SemaphoreType.DMA((count,))],
        compiler_params=pltpu.CompilerParams(vmem_limit_bytes=BIG),
        cost_estimate=pl.CostEstimate(flops=0, bytes_accessed=4 * width * columns, transcendentals=0),
    )(filter_store)


def gate(count, key_in, value_in):
    width, columns = key_in.shape
    part = columns // count
    if part % 128:
        gated = (key_in.astype(jnp.float32) * value_in.astype(jnp.float32)).astype(jnp.bfloat16)
        return pieces(gated, count)
    block = pltpu.VMEM((count, width, part), jnp.bfloat16)
    return pl.pallas_call(
        functools.partial(gate_kernel, count, part),
        out_shape=[jax.ShapeDtypeStruct((width, part), jnp.bfloat16)] * count,
        in_specs=[IN_HBM] * 2,
        out_specs=[WHOLE] * count,
        scratch_shapes=[block, block, pltpu.SemaphoreType.DMA((2, count))],
        compiler_params=pltpu.CompilerParams(vmem_limit_bytes=BIG),
        cost_estimate=pl.CostEstimate(flops=width * columns, bytes_accessed=6 * width * columns, transcendentals=0),
    )(key_in, value_in)


def dot(x, y):
    return jnp.dot(x, y, preferred_element_type=jnp.float32)


def transform(high, low, block):
    return dot(high, block) + dot(low, block)


def filter_kernel(steps, lag_ref, high_ref, low_ref, *refs):
    blocks, out = refs[:-1], refs[-1]
    for k, block in zip(steps, blocks):
        out[lag_ref[partner(k)]] = transform(high_ref[...], low_ref[...], block[...])


def gated_kernel(steps, high_ref, low_ref, *refs):
    blocks, out = refs[:-1], refs[-1]
    for k, block in zip(steps, blocks):
        out[partner(k)] = transform(high_ref[...], low_ref[...], block[...])


def spectra_shape(count, block):
    width, columns = block.shape
    return jax.ShapeDtypeStruct((count, 2 * width, columns), jnp.float32)


def transform_cost(count, block, passes):
    width, columns = block.shape
    return pl.CostEstimate(
        flops=4 * passes * count * width * width * columns,
        bytes_accessed=10 * count * width * columns,
        transcendentals=0,
    )


def filter_spectra(lag_of_block, high, low, blocks):
    steps = list(blocks)
    return pl.pallas_call(
        functools.partial(filter_kernel, steps),
        out_shape=spectra_shape(len(steps), blocks[steps[0]]),
        in_specs=[pl.BlockSpec(memory_space=pltpu.SMEM)] + [WHOLE] * (2 + len(steps)),
        out_specs=WHOLE,
        compiler_params=pltpu.CompilerParams(vmem_limit_bytes=16 * MIB),
        cost_estimate=transform_cost(len(steps), blocks[steps[0]], 2),
    )(lag_of_block, high, low, *[blocks[k] for k in steps])


def gated_spectra(count, high, low, blocks):
    steps = list(blocks)
    return pl.pallas_call(
        functools.partial(gated_kernel, steps),
        out_shape=spectra_shape(count, blocks[steps[0]]),
        in_specs=[WHOLE] * (2 + len(steps)),
        out_specs=WHOLE,
        compiler_params=pltpu.CompilerParams(vmem_limit_bytes=16 * MIB),
        cost_estimate=transform_cost(len(steps), blocks[steps[0]], 2),
    )(high, low, *[blocks[k] for k in steps])


def product_kernel(count, steps, first, fh_ref, fl_ref, ih_ref, il_ref, fs, gs, *refs):
    blocks, (gs, sh, sl), outs, ss = refs[: len(steps)], refs[len(steps) : len(steps) + 3], refs[len(steps) + 3 : -1], refs[-1]
    width, columns = outs[0].shape
    for k, block in zip(steps, blocks):
        gs[partner(k)] = transform(fh_ref[...], fl_ref[...], block[...])
    lane = min(128, columns)

    def products(row, sign):
        re_rows = pl.ds(pl.multiple_of(row * 8, 8), 8)
        im_rows = pl.ds(pl.multiple_of(row * 8 + width, 8), 8)
        for at in range(0, columns, lane):
            lanes = pl.ds(at, lane)
            f_re = [fs[i, re_rows, lanes] for i in range(count)]
            f_im = [fs[i, im_rows, lanes] for i in range(count)]
            h_re, h_im = [], []
            for i in range(count):
                g_re, g_im = gs[i, re_rows, lanes], gs[i, im_rows, lanes]
                if i == 0:
                    h_re.append(g_re)
                    h_im.append(g_im)
                elif sign > 0:
                    h_re.append(g_re - last_im)
                    h_im.append(g_im + last_re)
                else:
                    h_re.append(g_re + last_im)
                    h_im.append(g_im - last_re)
                last_re, last_im = g_re, g_im
            for j in range(count):
                s_re = f_re[0] * h_re[j] - f_im[0] * h_im[j]
                s_im = f_re[0] * h_im[j] + f_im[0] * h_re[j]
                for i in range(1, j + 1):
                    s_re = s_re + f_re[i] * h_re[j - i] - f_im[i] * h_im[j - i]
                    s_im = s_im + f_re[i] * h_im[j - i] + f_im[i] * h_re[j - i]
                ss[j, re_rows, lanes] = s_re
                ss[j, im_rows, lanes] = s_im

    half = width // 16

    @pl.loop(0, half)
    def _(row):
        products(row, 1)

    @pl.loop(half, 2 * half)
    def _(row):
        products(row, -1)

    for at, k in enumerate(first + [k for k in range(count) if k not in first]):
        total = ss[partner(k)]
        high = total.astype(jnp.bfloat16)
        low = (total - high.astype(jnp.float32)).astype(jnp.bfloat16)
        if k in first:
            outs[at][...] = inverse(ih_ref[...], il_ref[...], high, low)
        else:
            sh[partner(k)] = high
            sl[partner(k)] = low


def inverse(table_high, table_low, high, low):
    return (dot(table_high, high) + dot(table_high, low) + dot(table_low, high)).astype(jnp.bfloat16)


def products(count, first, tabs, filt, gated, blocks):
    steps = list(blocks)
    width, columns = blocks[steps[0]].shape
    half = jax.ShapeDtypeStruct((count, 2 * width, columns), jnp.bfloat16)
    found = pl.pallas_call(
        functools.partial(product_kernel, count, steps, first),
        out_shape=[jax.ShapeDtypeStruct(gated.shape, jnp.float32), half, half]
        + [jax.ShapeDtypeStruct((width, columns), jnp.bfloat16)] * len(first),
        in_specs=[WHOLE] * (6 + len(steps)),
        out_specs=[WHOLE] * (3 + len(first)),
        scratch_shapes=[pltpu.VMEM(gated.shape, jnp.float32)],
        input_output_aliases={5: 0},
        compiler_params=pltpu.CompilerParams(vmem_limit_bytes=20 * MIB),
        cost_estimate=transform_cost(count, blocks[steps[0]], 7),
    )(*tabs, filt, gated, *[blocks[k] for k in steps])
    return found[1], found[2], dict(zip(first, found[3:]))


def inverse_kernel(steps, ih_ref, il_ref, sh, sl, *outs):
    for k, out in zip(steps, outs):
        out[...] = inverse(ih_ref[...], il_ref[...], sh[partner(k)], sl[partner(k)])


def inverses(steps, tabs, high, low):
    count, twice, columns = high.shape
    block = jax.ShapeDtypeStruct((twice // 2, columns), jnp.bfloat16)
    found = pl.pallas_call(
        functools.partial(inverse_kernel, steps),
        out_shape=[block] * len(steps),
        in_specs=[WHOLE] * 4,
        out_specs=[WHOLE] * len(steps),
        compiler_params=pltpu.CompilerParams(vmem_limit_bytes=16 * MIB),
        cost_estimate=transform_cost(len(steps), block, 3),
    )(*tabs[2:], high, low)
    return dict(zip(steps, found))


def pre_kernel(steps, query_ref, skip_ref, *refs):
    count = len(steps)
    convs, gates, (pre_ref, square_ref) = refs[:count], refs[count : 2 * count], refs[2 * count :]
    width, part = convs[0].shape
    total = jnp.zeros((width, 128), jnp.float32)
    for at_k, k in enumerate(steps):
        start = partner(k) * part if count > 1 else 0
        for at in range(0, part, 128):
            lanes, cols = pl.ds(at, 128), pl.ds(pl.multiple_of(start + at, 128), 128)
            gated = gates[at_k][:, lanes].astype(jnp.float32)
            conv = convs[at_k][:, lanes].astype(jnp.float32)
            pre = query_ref[:, cols].astype(jnp.float32) * (conv + skip_ref[:, cols] * gated)
            pre_ref[:, cols] = pre
            total = total + pre * pre
    square_ref[...] = jnp.sum(total.T, axis=0, keepdims=True)


def together(blocks):
    blocks = [blocks[k] for k in range(len(blocks))]
    count = len(blocks)
    order = jnp.arange(count, dtype=jnp.int32) ^ lax.axis_index("tok")
    stacked = jnp.take(jnp.stack(blocks), order, axis=0)
    return {0: stacked.transpose(1, 0, 2).reshape(blocks[0].shape[0], -1)}


def gated_output(query, skip, convs, gates):
    width, columns = query.shape
    steps = list(convs)
    if convs[0].shape[1] % 128:
        convs, gates, steps = together(convs), together(gates), [0]
    count = len(steps)
    return pl.pallas_call(
        functools.partial(pre_kernel, steps),
        out_shape=(
            jax.ShapeDtypeStruct((width, columns), jnp.float32),
            jax.ShapeDtypeStruct((1, width), jnp.float32),
        ),
        in_specs=[WHOLE] * (2 + 2 * count),
        out_specs=(WHOLE, WHOLE),
        compiler_params=pltpu.CompilerParams(vmem_limit_bytes=16 * MIB),
        cost_estimate=pl.CostEstimate(flops=6 * width * columns, bytes_accessed=10 * width * columns, transcendentals=0),
    )(query, skip, *[convs[k] for k in steps], *[gates[k] for k in steps])


def scale_kernel(channels, steps, pre_ref, square_ref, gain_ref, out_ref, buf, sems):
    width = pre_ref.shape[0]
    rows = width // steps
    scale = lax.rsqrt(square_ref[...] * (1.0 / channels) + 1e-06)
    scale = jnp.broadcast_to(scale, (128, width)).T
    copies = []
    for s in range(steps):
        for at in range(0, pre_ref.shape[1], 128):
            cols = pl.ds(at, 128)
            here = scale[s * rows : (s + 1) * rows, :]
            buf[pl.ds(s * rows, rows), cols] = gain_ref[:, cols] * pre_ref[pl.ds(s * rows, rows), cols] * here
        window = pl.ds(s * rows, rows)
        copies.append(pltpu.make_async_copy(buf.at[window, :], out_ref.at[window, :], sems.at[s]))
        copies[-1].start()
    for copy in copies:
        copy.wait()


def scaled(channels, pre, square, out_gain):
    width, columns = pre.shape
    steps = 8
    return pl.pallas_call(
        functools.partial(scale_kernel, channels, steps),
        out_shape=jax.ShapeDtypeStruct((width, columns), jnp.float32),
        in_specs=[WHOLE] * 3,
        out_specs=IN_HBM,
        scratch_shapes=[pltpu.VMEM((width, columns), jnp.float32), pltpu.SemaphoreType.DMA((steps,))],
        compiler_params=pltpu.CompilerParams(vmem_limit_bytes=16 * MIB),
        cost_estimate=pl.CostEstimate(flops=2 * width * columns, bytes_accessed=8 * width * columns, transcendentals=0),
    )(pre, square, out_gain)


def local(query, key_in, value_in, filter_store, lag_of_block, skip, out_gain):
    width, columns = query.shape
    count = lax.axis_size("tok")
    tabs = [jnp.asarray(t) for t in tables(width)]
    own = split(count, filter_store)
    held, key_in, value_in = lax.optimization_barrier((own[0], key_in, value_in))
    mine = gate(count, key_in, value_in)
    order = sending_order(count)
    filts, gates, convs = {}, {}, {}
    for k in order:
        filts[k] = send(own[k], k, count)
    for k in order:
        gates[k] = send(mine[k], k, count)
    filts[0], gates[0] = held, mine[0]
    filt = filter_spectra(lag_of_block, *tabs[:2], filts)
    early = order[: count // 2] + [0]
    gated = gated_spectra(count, *tabs[:2], {k: gates[k] for k in early})
    first = order[:2]
    high, low, found = products(count, first, tabs, filt, gated, {k: gates[k] for k in gates if k not in early})
    rest = order[2:] + [0]
    found.update(inverses(rest, tabs, high, low))
    for k in order:
        convs[k] = send(found[k], k, count)
    convs[0] = found[0]
    pre, square = gated_output(query, skip[None, :], convs, mine)
    square = lax.psum(square, "chan")
    return scaled(columns * lax.axis_size("chan"), pre, square, out_gain[None, :])


def solution(mesh):
    in_specs = (
        P("tok", "chan"),
        P("tok", "chan"),
        P("tok", "chan"),
        P("tok", "chan"),
        P(),
        P("chan"),
        P("chan"),
    )
    return jax.shard_map(local, mesh=mesh, in_specs=in_specs, out_specs=P("tok", "chan"), check_vma=False)
```

```python
import functools
import math

import jax
import jax.numpy as jnp
import ml_dtypes
import numpy as np
from jax import lax
from jax.experimental import pallas as pl
from jax.experimental.pallas import tpu as pltpu
from jax.sharding import PartitionSpec as P

MIB = 1024 * 1024
WHOLE = pl.BlockSpec(memory_space=pltpu.VMEM)
IN_HBM = pl.BlockSpec(memory_space=pltpu.HBM)


def split_bf16(table):
    high = table.astype(ml_dtypes.bfloat16)
    low = (table - high.astype(np.float64)).astype(ml_dtypes.bfloat16)
    return high, low


def tables(width):
    freq = np.concatenate([np.arange(0, width, 2), np.arange(1, width, 2)])
    place = np.arange(width)
    steps = ((2 * freq[:, None] + 1) * place[None, :]) % (4 * width)
    angle = math.pi / (2 * width) * steps
    forward = np.concatenate([np.cos(angle), -np.sin(angle)], axis=0)
    inverse = forward.T / width
    return split_bf16(forward) + split_bf16(inverse)


def partner(step):
    return lax.axis_index("tok") ^ step


class Window:
    def __init__(self, count, size):
        self.count, self.size, self.arrived = count, size, []

    def send(self, block, step, after=None):
        if after is None:
            after = [len(self.arrived) - self.size] if len(self.arrived) >= self.size else []
        if after:
            held = lax.optimization_barrier((block, *[self.arrived[i] for i in after]))
            block = held[0]
            for i, value in zip(after, held[1:]):
                self.arrived[i] = value
        self.arrived.append(lax.ppermute(block, "tok", [(d, d ^ step) for d in range(self.count)]))
        return len(self.arrived) - 1


def sending_order(count):
    half = count // 2
    far = list(range(half, count, 2)) + list(range(half + 1, count, 2))
    near = list(range(2, half)) + [1]
    order = []
    for at in range(half - 1):
        order += [far[at], near[at]]
    return order[:-1] + far[-1:] + order[-1:]


def columns_of(step, part):
    return pl.ds(pl.multiple_of(partner(step) * part, 128), part)


def split_kernel(count, part, filt_ref, *refs):
    outs, sems = refs[:count], refs[count]
    copies = []
    for k in range(count):
        copies.append(pltpu.make_async_copy(filt_ref.at[:, columns_of(k, part)], outs[k], sems.at[k]))
        copies[-1].start()
    for copy in copies:
        copy.wait()


def chunks_of(part):
    return 2 if part % 256 == 0 else 1


def is_far(step, count):
    return step >= count // 2


def place(step, count, part):
    parts = chunks_of(part) if is_far(step, count) else 1
    return [(c * (part // parts), part // parts) for c in range(parts)]


def gate_kernel(count, part, key_ref, value_ref, *refs):
    outs, (key_buf, value_buf, sems) = list(refs[:-3]), refs[-3:]
    copies = []
    for k in range(count):
        cols = columns_of(k, part)
        copies.append(
            (
                pltpu.make_async_copy(key_ref.at[:, cols], key_buf.at[k], sems.at[0, k]),
                pltpu.make_async_copy(value_ref.at[:, cols], value_buf.at[k], sems.at[1, k]),
            )
        )
        for copy in copies[-1]:
            copy.start()
    for k in range(count):
        for copy in copies[k]:
            copy.wait()
        product = key_buf[k].astype(jnp.float32) * value_buf[k].astype(jnp.float32)
        product = product.astype(jnp.bfloat16)
        for at, size in place(k, count, part):
            outs.pop(0)[...] = product[:, at : at + size]


def pieces(x, count):
    part = x.shape[1] // count
    return [lax.dynamic_slice_in_dim(x, partner(k) * part, part, axis=1) for k in range(count)]


def split(count, filter_store):
    width, columns = filter_store.shape
    part = columns // count
    if part % 128:
        return pieces(filter_store, count)
    return pl.pallas_call(
        functools.partial(split_kernel, count, part),
        out_shape=[jax.ShapeDtypeStruct((width, part), jnp.bfloat16)] * count,
        in_specs=[IN_HBM],
        out_specs=[WHOLE] * count,
        scratch_shapes=[pltpu.SemaphoreType.DMA((count,))],
        compiler_params=pltpu.CompilerParams(vmem_limit_bytes=16 * MIB),
        cost_estimate=pl.CostEstimate(flops=0, bytes_accessed=4 * width * columns, transcendentals=0),
    )(filter_store)


def gate(count, key_in, value_in):
    width, columns = key_in.shape
    part = columns // count
    if part % 128:
        gated = (key_in.astype(jnp.float32) * value_in.astype(jnp.float32)).astype(jnp.bfloat16)
        return [[piece] for piece in pieces(gated, count)]
    block = pltpu.VMEM((count, width, part), jnp.bfloat16)
    places = [place(k, count, part) for k in range(count)]
    shapes = [jax.ShapeDtypeStruct((width, size), jnp.bfloat16) for sizes in places for _, size in sizes]
    found = list(
        pl.pallas_call(
            functools.partial(gate_kernel, count, part),
            out_shape=shapes,
            in_specs=[IN_HBM] * 2,
            out_specs=[WHOLE] * len(shapes),
            scratch_shapes=[block, block, pltpu.SemaphoreType.DMA((2, count))],
            compiler_params=pltpu.CompilerParams(vmem_limit_bytes=16 * MIB),
            cost_estimate=pl.CostEstimate(
                flops=width * columns, bytes_accessed=6 * width * columns, transcendentals=0
            ),
        )(key_in, value_in)
    )
    return [[found.pop(0) for _ in sizes] for sizes in places]


def dot(x, y):
    return jnp.dot(x, y, preferred_element_type=jnp.float32)


def transform(high, low, block):
    return dot(high, block) + dot(low, block)


def filter_kernel(steps, lag_ref, high_ref, low_ref, *refs):
    blocks, outs = refs[: len(steps)], refs[len(steps) :]
    chunk = outs[0].shape[2]
    for k, block in zip(steps, blocks):
        spectrum = transform(high_ref[...], low_ref[...], block[...])
        for c, out in enumerate(outs):
            out[lag_ref[partner(k)]] = spectrum[:, c * chunk : (c + 1) * chunk]


def filter_spectra(lag_of_block, high, low, blocks):
    steps = list(blocks)
    width, part = blocks[0].shape
    chunks = chunks_of(part)
    shape = jax.ShapeDtypeStruct((len(steps), 2 * width, part // chunks), jnp.float32)
    return pl.pallas_call(
        functools.partial(filter_kernel, steps),
        out_shape=[shape] * chunks,
        in_specs=[pl.BlockSpec(memory_space=pltpu.SMEM)] + [WHOLE] * (2 + len(steps)),
        out_specs=[WHOLE] * chunks,
        compiler_params=pltpu.CompilerParams(vmem_limit_bytes=16 * MIB),
        cost_estimate=pl.CostEstimate(
            flops=8 * len(steps) * width * width * part,
            bytes_accessed=10 * len(steps) * width * part,
            transcendentals=0,
        ),
    )(lag_of_block, high, low, *[blocks[k] for k in steps])


def multiply_spectra(count, width, columns, fs, gs, ss):
    lane = min(128, columns)

    def tile(row, sign):
        re_rows = pl.ds(pl.multiple_of(row * 8, 8), 8)
        im_rows = pl.ds(pl.multiple_of(row * 8 + width, 8), 8)
        for at in range(0, columns, lane):
            lanes = pl.ds(at, lane)
            f_re = [fs[i, re_rows, lanes] for i in range(count)]
            f_im = [fs[i, im_rows, lanes] for i in range(count)]
            h_re, h_im = [], []
            for i in range(count):
                g_re, g_im = gs[i, re_rows, lanes], gs[i, im_rows, lanes]
                if i == 0:
                    h_re.append(g_re)
                    h_im.append(g_im)
                elif sign > 0:
                    h_re.append(g_re - last_im)
                    h_im.append(g_im + last_re)
                else:
                    h_re.append(g_re + last_im)
                    h_im.append(g_im - last_re)
                last_re, last_im = g_re, g_im
            for j in range(count):
                s_re = f_re[0] * h_re[j] - f_im[0] * h_im[j]
                s_im = f_re[0] * h_im[j] + f_im[0] * h_re[j]
                for i in range(1, j + 1):
                    s_re = s_re + f_re[i] * h_re[j - i] - f_im[i] * h_im[j - i]
                    s_im = s_im + f_re[i] * h_im[j - i] + f_im[i] * h_re[j - i]
                ss[j, re_rows, lanes] = s_re
                ss[j, im_rows, lanes] = s_im

    half = width // 16

    @pl.loop(0, half)
    def _(row):
        tile(row, 1)

    @pl.loop(half, 2 * half)
    def _(row):
        tile(row, -1)


def pairs(items, columns):
    size = 2 if columns == 128 else 1
    return [items[at : at + size] for at in range(0, len(items), size)]


def conv_kernel(count, chunk, chunks, steps, ends, fh_ref, fl_ref, ih_ref, il_ref, fs, *refs):
    blocks, earlier, outs, (gs, ss) = (
        dict(zip(steps, refs[:count])),
        refs[count : count + ends[0]],
        refs[count + ends[0] : -2],
        refs[-2:],
    )
    width, columns = gs.shape[1] // 2, gs.shape[2]
    here = pl.ds(chunk * columns, columns)

    def block(k):
        ref = blocks[k]
        return ref[...] if ref.shape[1] == columns else ref[:, here]

    for group in pairs(steps, columns):
        found = transform(fh_ref[...], fl_ref[...], jnp.concatenate([block(k) for k in group], axis=1))
        for at, k in enumerate(group):
            gs[partner(k)] = found[:, at * columns : (at + 1) * columns]
    multiply_spectra(count, width, columns, fs, gs, ss)
    earlier = list(earlier)
    outs = dict(zip(steps, outs))
    for group in pairs(steps, columns):
        total = jnp.concatenate([ss[partner(k)] for k in group], axis=1)
        high = total.astype(jnp.bfloat16)
        low = (total - high.astype(jnp.float32)).astype(jnp.bfloat16)
        conv = dot(ih_ref[...], high) + dot(ih_ref[...], low) + dot(il_ref[...], high)
        conv = conv.astype(jnp.bfloat16)
        for at, k in enumerate(group):
            found = conv[:, at * columns : (at + 1) * columns]
            if outs[k].shape[1] == columns:
                outs[k][...] = found
            else:
                outs[k][:, : chunk * columns] = earlier.pop(0)[...]
                outs[k][:, here] = found


def block_conv(chunk, chunks, tabs, filt, blocks, earlier):
    count, twice, columns = filt.shape
    width = twice // 2
    steps = list(blocks)
    whole = [k for k in steps if not is_far(k, count)] if chunk == chunks - 1 else []
    before = [earlier[k] for k in whole] if earlier else []
    spectra = pltpu.VMEM((count, twice, columns), jnp.float32)
    sizes = [columns * chunks if k in whole else columns for k in steps]
    found = pl.pallas_call(
        functools.partial(conv_kernel, count, chunk, chunks, steps, [len(before)]),
        out_shape=[jax.ShapeDtypeStruct((width, size), jnp.bfloat16) for size in sizes],
        in_specs=[WHOLE] * (5 + count + len(before)),
        out_specs=[WHOLE] * count,
        scratch_shapes=[spectra, spectra],
        compiler_params=pltpu.CompilerParams(vmem_limit_bytes=20 * MIB),
        cost_estimate=pl.CostEstimate(
            flops=24 * count * width * width * columns,
            bytes_accessed=14 * count * width * columns,
            transcendentals=0,
        ),
    )(*tabs, filt, *[blocks[k] for k in steps], *before)
    return dict(zip(steps, found))


def pre_kernel(where, part, query_ref, skip_ref, *refs):
    count = len(where)
    convs, gates, (pre_ref, square_ref) = refs[:count], refs[count : 2 * count], refs[2 * count :]
    width = query_ref.shape[0]
    total = jnp.zeros((width, 128), jnp.float32)
    for (k, start), conv_ref, gated_ref in zip(where, convs, gates):
        start = partner(k) * part + start if part else start
        for at in range(0, conv_ref.shape[1], 128):
            lanes, cols = pl.ds(at, 128), pl.ds(pl.multiple_of(start + at, 128), 128)
            gated = gated_ref[:, lanes].astype(jnp.float32)
            conv = conv_ref[:, lanes].astype(jnp.float32)
            pre = query_ref[:, cols].astype(jnp.float32) * (conv + skip_ref[:, cols] * gated)
            pre_ref[:, cols] = pre
            total = total + pre * pre
    square_ref[...] = jnp.sum(total.T, axis=0, keepdims=True)


def together(blocks):
    count = len(blocks)
    order = jnp.arange(count, dtype=jnp.int32) ^ lax.axis_index("tok")
    stacked = jnp.take(jnp.stack([blocks[k] for k in range(count)]), order, axis=0)
    return stacked.transpose(1, 0, 2).reshape(blocks[0].shape[0], -1)


def gated_output(query, skip, part, convs, gates):
    width, columns = query.shape
    where = list(convs)
    if part % 128:
        convs = {(0, 0): together({k: piece for (k, _), piece in convs.items()})}
        gates = {(0, 0): together({k: piece for (k, _), piece in gates.items()})}
        where, part = [(0, 0)], 0
    return pl.pallas_call(
        functools.partial(pre_kernel, where, part),
        out_shape=(
            jax.ShapeDtypeStruct((width, columns), jnp.float32),
            jax.ShapeDtypeStruct((1, width), jnp.float32),
        ),
        in_specs=[WHOLE] * (2 + 2 * len(where)),
        out_specs=(WHOLE, WHOLE),
        compiler_params=pltpu.CompilerParams(vmem_limit_bytes=16 * MIB),
        cost_estimate=pl.CostEstimate(flops=6 * width * columns, bytes_accessed=10 * width * columns, transcendentals=0),
    )(query, skip, *[convs[w] for w in where], *[gates[w] for w in where])


def scale_kernel(channels, steps, pre_ref, square_ref, gain_ref, out_ref, buf, sems):
    width = pre_ref.shape[0]
    rows = width // steps
    scale = lax.rsqrt(square_ref[...] * (1.0 / channels) + 1e-06)
    scale = jnp.broadcast_to(scale, (128, width)).T
    copies = []
    for s in range(steps):
        for at in range(0, pre_ref.shape[1], 128):
            cols = pl.ds(at, 128)
            here = scale[s * rows : (s + 1) * rows, :]
            buf[pl.ds(s * rows, rows), cols] = gain_ref[:, cols] * pre_ref[pl.ds(s * rows, rows), cols] * here
        window = pl.ds(s * rows, rows)
        copies.append(pltpu.make_async_copy(buf.at[window, :], out_ref.at[window, :], sems.at[s]))
        copies[-1].start()
    for copy in copies:
        copy.wait()


def scaled(channels, pre, square, out_gain):
    width, columns = pre.shape
    steps = 8
    return pl.pallas_call(
        functools.partial(scale_kernel, channels, steps),
        out_shape=jax.ShapeDtypeStruct((width, columns), jnp.float32),
        in_specs=[WHOLE] * 3,
        out_specs=IN_HBM,
        scratch_shapes=[pltpu.VMEM((width, columns), jnp.float32), pltpu.SemaphoreType.DMA((steps,))],
        compiler_params=pltpu.CompilerParams(vmem_limit_bytes=16 * MIB),
        cost_estimate=pl.CostEstimate(flops=2 * width * columns, bytes_accessed=8 * width * columns, transcendentals=0),
    )(pre, square, out_gain)


def local(query, key_in, value_in, filter_store, lag_of_block, skip, out_gain):
    width, columns = query.shape
    count = lax.axis_size("tok")
    tabs = [jnp.asarray(t) for t in tables(width)]
    own = split(count, filter_store)
    held, key_in, value_in = lax.optimization_barrier((own[0], key_in, value_in))
    mine = gate(count, key_in, value_in)
    order = sending_order(count)
    part = columns // count
    chunks = chunks_of(part)
    window = Window(count, 5)
    filts = {k: window.send(own[k], k) for k in order}
    arrived = {}
    for c in range(chunks):
        for k in order:
            if c == 0 or is_far(k, count):
                arrived[k, c] = window.send(mine[k][c], k)
    filts = {k: window.arrived[i] for k, i in filts.items()}
    filts[0] = held
    filt = filter_spectra(lag_of_block, *tabs[:2], filts)
    convs, done = {}, {}
    for c in range(chunks):
        blocks = {k: window.arrived[arrived[k, c if is_far(k, count) else 0]] for k in order}
        blocks[0] = mine[0][0]
        done = block_conv(c, chunks, tabs, filt[c], blocks, done)
        begin = len(window.arrived)
        for k in order:
            if is_far(k, count) or c == chunks - 1:
                at = c * (part // chunks) if is_far(k, count) else 0
                sent = len(window.arrived)
                after = [sent - 5]
                if c and sent < begin + 3:
                    after = [begin - 4, begin - 3, begin - 2]
                convs[k, at] = window.send(done[k], k, after)
    convs = {w: window.arrived[i] for w, i in convs.items()}
    convs[0, 0] = done[0]
    gates = {(k, at): mine[k][c] for k in range(count) for c, (at, _) in enumerate(place(k, count, part))}
    pre, square = gated_output(query, skip[None, :], part, convs, gates)
    square = lax.psum(square, "chan")
    return scaled(columns * lax.axis_size("chan"), pre, square, out_gain[None, :])


def solution(mesh):
    in_specs = (
        P("tok", "chan"),
        P("tok", "chan"),
        P("tok", "chan"),
        P("tok", "chan"),
        P(),
        P("chan"),
        P("chan"),
    )
    return jax.shard_map(local, mesh=mesh, in_specs=in_specs, out_specs=P("tok", "chan"), check_vma=False)
```

```python
import functools
import math

import jax
import jax.numpy as jnp
import ml_dtypes
import numpy as np
from jax import lax
from jax.experimental import pallas as pl
from jax.experimental.pallas import tpu as pltpu
from jax.sharding import PartitionSpec as P

MIB = 1024 * 1024
EARLY = 3
WHOLE = pl.BlockSpec(memory_space=pltpu.VMEM)
IN_HBM = pl.BlockSpec(memory_space=pltpu.HBM)


def split_bf16(table):
    high = table.astype(ml_dtypes.bfloat16)
    low = (table - high.astype(np.float64)).astype(ml_dtypes.bfloat16)
    return high, low


def tables(width):
    freq = np.concatenate([np.arange(0, width, 2), np.arange(1, width, 2)])
    place = np.arange(width)
    steps = ((2 * freq[:, None] + 1) * place[None, :]) % (4 * width)
    angle = math.pi / (2 * width) * steps
    forward = np.concatenate([np.cos(angle), -np.sin(angle)], axis=0)
    inverse = forward.T / width
    return split_bf16(forward) + split_bf16(inverse)


def partner(step):
    return lax.axis_index("tok") ^ step


def after(value, *earlier):
    held = lax.optimization_barrier((value, *earlier))
    return held[0], list(held[1:])


def send(block, step, count):
    return lax.ppermute(block, "tok", [(d, d ^ step) for d in range(count)])


def spread(blocks):
    return lax.all_to_all(blocks, "tok", 0, 0, tiled=True)


def sending_order(count):
    half = count // 2
    far = list(range(half, count, 2)) + list(range(half + 1, count, 2))
    near = list(range(2, half)) + [1]
    order = []
    for at in range(half - 1):
        order += [far[at], near[at]]
    return order[:-1] + far[-1:] + order[-1:]


def columns_of(step, part):
    return pl.ds(pl.multiple_of(partner(step) * part, 128), part)


def split_kernel(count, part, filt_ref, out_ref, sems):
    copies = []
    for j in range(count):
        copies.append(pltpu.make_async_copy(filt_ref.at[:, pl.ds(j * part, part)], out_ref.at[j], sems.at[j]))
        copies[-1].start()
    for copy in copies:
        copy.wait()


def chunks_of(part):
    return 2 if part % 256 == 0 else 1


def gate_kernel(count, part, key_ref, value_ref, *refs):
    firsts, lasts, (key_buf, value_buf, sems) = refs[:count], refs[count:-3], refs[-3:]
    copies = []
    for k in range(count):
        cols = columns_of(k, part)
        copies.append(
            (
                pltpu.make_async_copy(key_ref.at[:, cols], key_buf.at[k], sems.at[0, k]),
                pltpu.make_async_copy(value_ref.at[:, cols], value_buf.at[k], sems.at[1, k]),
            )
        )
        for copy in copies[-1]:
            copy.start()
    for k in range(count):
        for copy in copies[k]:
            copy.wait()
        product = key_buf[k].astype(jnp.float32) * value_buf[k].astype(jnp.float32)
        product = product.astype(jnp.bfloat16)
        size = firsts[k].shape[1]
        firsts[k][...] = product[:, :size]
        if lasts:
            lasts[0][partner(k)] = product[:, size:]


def pieces(x, count):
    part = x.shape[1] // count
    return [lax.dynamic_slice_in_dim(x, partner(k) * part, part, axis=1) for k in range(count)]


def split(count, filter_store):
    width, columns = filter_store.shape
    part = columns // count
    if part % 128:
        return filter_store.reshape(width, count, part).transpose(1, 0, 2)
    return pl.pallas_call(
        functools.partial(split_kernel, count, part),
        out_shape=jax.ShapeDtypeStruct((count, width, part), jnp.bfloat16),
        in_specs=[IN_HBM],
        out_specs=WHOLE,
        scratch_shapes=[pltpu.SemaphoreType.DMA((count,))],
        compiler_params=pltpu.CompilerParams(vmem_limit_bytes=16 * MIB),
        cost_estimate=pl.CostEstimate(flops=0, bytes_accessed=4 * width * columns, transcendentals=0),
    )(filter_store)


def gate(count, key_in, value_in):
    width, columns = key_in.shape
    part = columns // count
    if part % 128:
        gated = (key_in.astype(jnp.float32) * value_in.astype(jnp.float32)).astype(jnp.bfloat16)
        return pieces(gated, count), []
    chunks = chunks_of(part)
    size = part // chunks
    block = pltpu.VMEM((count, width, part), jnp.bfloat16)
    shapes = [jax.ShapeDtypeStruct((width, size), jnp.bfloat16)] * count
    shapes += [jax.ShapeDtypeStruct((count, width, size), jnp.bfloat16)] * (chunks - 1)
    found = pl.pallas_call(
        functools.partial(gate_kernel, count, part),
        out_shape=shapes,
        in_specs=[IN_HBM] * 2,
        out_specs=[WHOLE] * len(shapes),
        scratch_shapes=[block, block, pltpu.SemaphoreType.DMA((2, count))],
        compiler_params=pltpu.CompilerParams(vmem_limit_bytes=16 * MIB),
        cost_estimate=pl.CostEstimate(flops=width * columns, bytes_accessed=6 * width * columns, transcendentals=0),
    )(key_in, value_in)
    return found[:count], found[count:]


def dot(x, y):
    return jnp.dot(x, y, preferred_element_type=jnp.float32)


def transform(high, low, block):
    return dot(high, block) + dot(low, block)


def filter_kernel(lag_ref, high_ref, low_ref, blocks, *outs):
    chunk = outs[0].shape[2]
    for i in range(blocks.shape[0]):
        spectrum = transform(high_ref[...], low_ref[...], blocks[i])
        for c, out in enumerate(outs):
            out[lag_ref[i]] = spectrum[:, c * chunk : (c + 1) * chunk]


def filter_spectra(lag_of_block, high, low, blocks):
    count, width, part = blocks.shape
    chunks = chunks_of(part)
    shape = jax.ShapeDtypeStruct((count, 2 * width, part // chunks), jnp.float32)
    return pl.pallas_call(
        filter_kernel,
        out_shape=[shape] * chunks,
        in_specs=[pl.BlockSpec(memory_space=pltpu.SMEM)] + [WHOLE] * 3,
        out_specs=[WHOLE] * chunks,
        compiler_params=pltpu.CompilerParams(vmem_limit_bytes=16 * MIB),
        cost_estimate=pl.CostEstimate(
            flops=8 * count * width * width * part,
            bytes_accessed=10 * count * width * part,
            transcendentals=0,
        ),
    )(lag_of_block, high, low, blocks)


def multiply_spectra(count, width, columns, fs, gs, ss):
    lane = min(128, columns)

    def tile(row, sign):
        re_rows = pl.ds(pl.multiple_of(row * 8, 8), 8)
        im_rows = pl.ds(pl.multiple_of(row * 8 + width, 8), 8)
        for at in range(0, columns, lane):
            lanes = pl.ds(at, lane)
            f_re = [fs[i, re_rows, lanes] for i in range(count)]
            f_im = [fs[i, im_rows, lanes] for i in range(count)]
            h_re, h_im = [], []
            for i in range(count):
                g_re, g_im = gs[i, re_rows, lanes], gs[i, im_rows, lanes]
                if i == 0:
                    h_re.append(g_re)
                    h_im.append(g_im)
                elif sign > 0:
                    h_re.append(g_re - last_im)
                    h_im.append(g_im + last_re)
                else:
                    h_re.append(g_re + last_im)
                    h_im.append(g_im - last_re)
                last_re, last_im = g_re, g_im
            for j in range(count):
                s_re = f_re[0] * h_re[j] - f_im[0] * h_im[j]
                s_im = f_re[0] * h_im[j] + f_im[0] * h_re[j]
                for i in range(1, j + 1):
                    s_re = s_re + f_re[i] * h_re[j - i] - f_im[i] * h_im[j - i]
                    s_im = s_im + f_re[i] * h_im[j - i] + f_im[i] * h_re[j - i]
                ss[j, re_rows, lanes] = s_re
                ss[j, im_rows, lanes] = s_im

    half = width // 16

    @pl.loop(0, half)
    def _(row):
        tile(row, 1)

    @pl.loop(half, 2 * half)
    def _(row):
        tile(row, -1)


def pairs(items, columns):
    size = 2 if columns == 128 else 1
    return [items[at : at + size] for at in range(0, len(items), size)]


def conv_kernel(steps, fh_ref, fl_ref, ih_ref, il_ref, fs, *refs):
    gs, ss = refs[-2:]
    count, columns = gs.shape[0], gs.shape[2]
    width = gs.shape[1] // 2
    if steps:
        blocks, outs = dict(zip(steps, refs[:count])), dict(zip(steps, refs[count:-2]))
        where = partner
    else:
        steps = list(range(count))
        blocks, outs = ({k: ref.at[k] for k in steps} for ref in refs[:2])
        where = int
    for group in pairs(steps, columns):
        found = transform(fh_ref[...], fl_ref[...], jnp.concatenate([blocks[k][...] for k in group], axis=1))
        for at, k in enumerate(group):
            gs[where(k)] = found[:, at * columns : (at + 1) * columns]
    multiply_spectra(count, width, columns, fs, gs, ss)
    for group in pairs(steps, columns):
        total = jnp.concatenate([ss[where(k)] for k in group], axis=1)
        high = total.astype(jnp.bfloat16)
        low = (total - high.astype(jnp.float32)).astype(jnp.bfloat16)
        conv = dot(ih_ref[...], high) + dot(ih_ref[...], low) + dot(il_ref[...], high)
        conv = conv.astype(jnp.bfloat16)
        for at, k in enumerate(group):
            outs[k][...] = conv[:, at * columns : (at + 1) * columns]


def block_conv(tabs, filt, steps, blocks):
    count, twice, columns = filt.shape
    width = twice // 2
    spectra = pltpu.VMEM((count, twice, columns), jnp.float32)
    return pl.pallas_call(
        functools.partial(conv_kernel, steps),
        out_shape=[jax.ShapeDtypeStruct(block.shape, jnp.bfloat16) for block in blocks],
        in_specs=[WHOLE] * (5 + len(blocks)),
        out_specs=[WHOLE] * len(blocks),
        scratch_shapes=[spectra, spectra],
        compiler_params=pltpu.CompilerParams(vmem_limit_bytes=20 * MIB),
        cost_estimate=pl.CostEstimate(
            flops=24 * count * width * width * columns,
            bytes_accessed=14 * count * width * columns,
            transcendentals=0,
        ),
    )(*tabs, filt, *blocks)


def pre_kernel(steps, part, query_ref, skip_ref, *refs):
    count = len(steps)
    pieces = len(refs) // 2 - 1
    convs, gates, (pre_ref, square_ref) = refs[:pieces], refs[pieces : 2 * pieces], refs[-2:]
    width = query_ref.shape[0]
    total = jnp.zeros((width, 128), jnp.float32)

    def add(total, start, conv_ref, gated_ref):
        for at in range(0, conv_ref.shape[1], 128):
            lanes, cols = pl.ds(at, 128), pl.ds(pl.multiple_of(start + at, 128), 128)
            gated = gated_ref[:, lanes].astype(jnp.float32)
            conv = conv_ref[:, lanes].astype(jnp.float32)
            pre = query_ref[:, cols].astype(jnp.float32) * (conv + skip_ref[:, cols] * gated)
            pre_ref[:, cols] = pre
            total = total + pre * pre
        return total

    for k, conv_ref, gated_ref in zip(steps, convs, gates):
        total = add(total, partner(k) * part if count > 1 else 0, conv_ref, gated_ref)
    if pieces > count:
        size = convs[-1].shape[2]
        for j in range(count):
            total = add(total, j * part + part - size, convs[-1].at[j], gates[-1].at[j])
    square_ref[...] = jnp.sum(total.T, axis=0, keepdims=True)


def together(blocks):
    count = len(blocks)
    order = jnp.arange(count, dtype=jnp.int32) ^ lax.axis_index("tok")
    stacked = jnp.take(jnp.stack([blocks[k] for k in range(count)]), order, axis=0)
    return stacked.transpose(1, 0, 2).reshape(blocks[0].shape[0], -1)


def gated_output(query, skip, steps, convs, gates):
    width, columns = query.shape
    part = columns // len(steps)
    if part % 128:
        convs, gates = ([together(dict(zip(steps, blocks)))] for blocks in (convs, gates))
        steps = [0]
    return pl.pallas_call(
        functools.partial(pre_kernel, steps, part),
        out_shape=(
            jax.ShapeDtypeStruct((width, columns), jnp.float32),
            jax.ShapeDtypeStruct((1, width), jnp.float32),
        ),
        in_specs=[WHOLE] * (2 + 2 * len(convs)),
        out_specs=(WHOLE, WHOLE),
        compiler_params=pltpu.CompilerParams(vmem_limit_bytes=16 * MIB),
        cost_estimate=pl.CostEstimate(flops=6 * width * columns, bytes_accessed=10 * width * columns, transcendentals=0),
    )(query, skip, *convs, *gates)


def scale_kernel(channels, steps, pre_ref, square_ref, gain_ref, out_ref, buf, sems):
    width = pre_ref.shape[0]
    rows = width // steps
    scale = lax.rsqrt(square_ref[...] * (1.0 / channels) + 1e-06)
    scale = jnp.broadcast_to(scale, (128, width)).T
    copies = []
    for s in range(steps):
        for at in range(0, pre_ref.shape[1], 128):
            cols = pl.ds(at, 128)
            here = scale[s * rows : (s + 1) * rows, :]
            buf[pl.ds(s * rows, rows), cols] = gain_ref[:, cols] * pre_ref[pl.ds(s * rows, rows), cols] * here
        window = pl.ds(s * rows, rows)
        copies.append(pltpu.make_async_copy(buf.at[window, :], out_ref.at[window, :], sems.at[s]))
        copies[-1].start()
    for copy in copies:
        copy.wait()


def scaled(channels, pre, square, out_gain):
    width, columns = pre.shape
    steps = 8
    return pl.pallas_call(
        functools.partial(scale_kernel, channels, steps),
        out_shape=jax.ShapeDtypeStruct((width, columns), jnp.float32),
        in_specs=[WHOLE] * 3,
        out_specs=IN_HBM,
        scratch_shapes=[pltpu.VMEM((width, columns), jnp.float32), pltpu.SemaphoreType.DMA((steps,))],
        compiler_params=pltpu.CompilerParams(vmem_limit_bytes=16 * MIB),
        cost_estimate=pl.CostEstimate(flops=2 * width * columns, bytes_accessed=8 * width * columns, transcendentals=0),
    )(pre, square, out_gain)


def local(query, key_in, value_in, filter_store, lag_of_block, skip, out_gain):
    width, columns = query.shape
    count = lax.axis_size("tok")
    tabs = [jnp.asarray(t) for t in tables(width)]
    own = split(count, filter_store)
    own, (key_in, value_in) = after(own, key_in, value_in)
    firsts, lasts = gate(count, key_in, value_in)
    order = sending_order(count)
    steps = order + [0]
    filt = filter_spectra(lag_of_block, *tabs[:2], spread(own))
    blocks = [send(firsts[k], k, count) for k in order] + [firsts[0]]
    lasts_all = [spread(last) for last in lasts]
    done = block_conv(tabs, filt[0], steps, blocks)
    convs = [send(done[at], k, count) for at, k in enumerate(order)] + [done[-1]]
    for filt_last, last in zip(filt[1:], lasts_all):
        (done,) = block_conv(tabs, filt_last, [], [last])
        done, convs[:EARLY] = after(done, *convs[:EARLY])
        convs.append(spread(done))
    gates = [firsts[k] for k in steps] + list(lasts)
    pre, square = gated_output(query, skip[None, :], steps, convs, gates)
    square = lax.psum(square, "chan")
    return scaled(columns * lax.axis_size("chan"), pre, square, out_gain[None, :])


def solution(mesh):
    in_specs = (
        P("tok", "chan"),
        P("tok", "chan"),
        P("tok", "chan"),
        P("tok", "chan"),
        P(),
        P("chan"),
        P("chan"),
    )
    return jax.shard_map(local, mesh=mesh, in_specs=in_specs, out_specs=P("tok", "chan"), check_vma=False)
```

```python
import functools
import math

import jax
import jax.numpy as jnp
import ml_dtypes
import numpy as np
from jax import lax
from jax.experimental import pallas as pl
from jax.experimental.pallas import tpu as pltpu
from jax.sharding import PartitionSpec as P

MIB = 1024 * 1024
WHOLE = pl.BlockSpec(memory_space=pltpu.VMEM)
IN_HBM = pl.BlockSpec(memory_space=pltpu.HBM)


def split_bf16(table):
    high = table.astype(ml_dtypes.bfloat16)
    low = (table - high.astype(np.float64)).astype(ml_dtypes.bfloat16)
    return high, low


def tables(width):
    freq = np.concatenate([np.arange(0, width, 2), np.arange(1, width, 2)])
    place = np.arange(width)
    steps = ((2 * freq[:, None] + 1) * place[None, :]) % (4 * width)
    angle = math.pi / (2 * width) * steps
    forward = np.concatenate([np.cos(angle), -np.sin(angle)], axis=0)
    inverse = forward.T / width
    return split_bf16(forward) + split_bf16(inverse)


def partner(step):
    return lax.axis_index("tok") ^ step


def after(value, *earlier):
    held = lax.optimization_barrier((value, *earlier))
    return held[0], list(held[1:])


def send(block, step, count):
    return lax.ppermute(block, "tok", [(d, d ^ step) for d in range(count)])


def spread(blocks):
    return lax.all_to_all(blocks, "tok", 0, 0, tiled=True)


def sending_order(count):
    half = count // 2
    far = list(range(half, count, 2)) + list(range(half + 1, count, 2))
    near = list(range(2, half)) + [1]
    order = []
    for at in range(half - 1):
        order += [far[at], near[at]]
    return order[:-1] + far[-1:] + order[-1:]


def columns_of(step, part):
    return pl.ds(pl.multiple_of(partner(step) * part, 128), part)


def split_kernel(count, part, filt_ref, *refs):
    outs, sems = refs[:count], refs[count]
    copies = []
    for k in range(count):
        copies.append(pltpu.make_async_copy(filt_ref.at[:, columns_of(k, part)], outs[k], sems.at[k]))
        copies[-1].start()
    for copy in copies:
        copy.wait()


def chunks_of(part):
    return 2 if part % 256 == 0 else 1


def gate_kernel(count, part, key_ref, value_ref, *refs):
    lasts, firsts, (key_buf, value_buf, sems) = refs[:count], refs[count:-3], refs[-3:]
    copies = []
    for k in range(count):
        cols = columns_of(k, part)
        copies.append(
            (
                pltpu.make_async_copy(key_ref.at[:, cols], key_buf.at[k], sems.at[0, k]),
                pltpu.make_async_copy(value_ref.at[:, cols], value_buf.at[k], sems.at[1, k]),
            )
        )
        for copy in copies[-1]:
            copy.start()
    for k in range(count):
        for copy in copies[k]:
            copy.wait()
        product = key_buf[k].astype(jnp.float32) * value_buf[k].astype(jnp.float32)
        product = product.astype(jnp.bfloat16)
        size = lasts[k].shape[1]
        lasts[k][...] = product[:, part - size :]
        if firsts:
            firsts[0][partner(k)] = product[:, : part - size]


def pieces(x, count):
    part = x.shape[1] // count
    return [lax.dynamic_slice_in_dim(x, partner(k) * part, part, axis=1) for k in range(count)]


def split(count, filter_store):
    width, columns = filter_store.shape
    part = columns // count
    if part % 128:
        return pieces(filter_store, count)
    return pl.pallas_call(
        functools.partial(split_kernel, count, part),
        out_shape=[jax.ShapeDtypeStruct((width, part), jnp.bfloat16)] * count,
        in_specs=[IN_HBM],
        out_specs=[WHOLE] * count,
        scratch_shapes=[pltpu.SemaphoreType.DMA((count,))],
        compiler_params=pltpu.CompilerParams(vmem_limit_bytes=16 * MIB),
        cost_estimate=pl.CostEstimate(flops=0, bytes_accessed=4 * width * columns, transcendentals=0),
    )(filter_store)


def gate(count, key_in, value_in):
    width, columns = key_in.shape
    part = columns // count
    if part % 128:
        gated = (key_in.astype(jnp.float32) * value_in.astype(jnp.float32)).astype(jnp.bfloat16)
        return pieces(gated, count), []
    chunks = chunks_of(part)
    size = part // chunks
    block = pltpu.VMEM((count, width, part), jnp.bfloat16)
    shapes = [jax.ShapeDtypeStruct((width, size), jnp.bfloat16)] * count
    shapes += [jax.ShapeDtypeStruct((count, width, size), jnp.bfloat16)] * (chunks - 1)
    found = pl.pallas_call(
        functools.partial(gate_kernel, count, part),
        out_shape=shapes,
        in_specs=[IN_HBM] * 2,
        out_specs=[WHOLE] * len(shapes),
        scratch_shapes=[block, block, pltpu.SemaphoreType.DMA((2, count))],
        compiler_params=pltpu.CompilerParams(vmem_limit_bytes=16 * MIB),
        cost_estimate=pl.CostEstimate(flops=width * columns, bytes_accessed=6 * width * columns, transcendentals=0),
    )(key_in, value_in)
    return found[:count], found[count:]


def dot(x, y):
    return jnp.dot(x, y, preferred_element_type=jnp.float32)


def transform(high, low, block):
    return dot(high, block) + dot(low, block)


def filter_kernel(steps, lag_ref, high_ref, low_ref, *refs):
    blocks, outs = refs[: len(steps)], refs[len(steps) :]
    chunk = outs[0].shape[2]
    for k, block in zip(steps, blocks):
        spectrum = transform(high_ref[...], low_ref[...], block[...])
        for c, out in enumerate(outs):
            out[lag_ref[partner(k)]] = spectrum[:, c * chunk : (c + 1) * chunk]


def filter_spectra(lag_of_block, high, low, blocks):
    steps = list(blocks)
    width, part = blocks[0].shape
    chunks = chunks_of(part)
    shape = jax.ShapeDtypeStruct((len(steps), 2 * width, part // chunks), jnp.float32)
    return pl.pallas_call(
        functools.partial(filter_kernel, steps),
        out_shape=[shape] * chunks,
        in_specs=[pl.BlockSpec(memory_space=pltpu.SMEM)] + [WHOLE] * (2 + len(steps)),
        out_specs=[WHOLE] * chunks,
        compiler_params=pltpu.CompilerParams(vmem_limit_bytes=16 * MIB),
        cost_estimate=pl.CostEstimate(
            flops=8 * len(steps) * width * width * part,
            bytes_accessed=10 * len(steps) * width * part,
            transcendentals=0,
        ),
    )(lag_of_block, high, low, *[blocks[k] for k in steps])


def multiply_spectra(count, width, columns, fs, gs, ss):
    lane = min(128, columns)

    def tile(row, sign):
        re_rows = pl.ds(pl.multiple_of(row * 8, 8), 8)
        im_rows = pl.ds(pl.multiple_of(row * 8 + width, 8), 8)
        for at in range(0, columns, lane):
            lanes = pl.ds(at, lane)
            f_re = [fs[i, re_rows, lanes] for i in range(count)]
            f_im = [fs[i, im_rows, lanes] for i in range(count)]
            h_re, h_im = [], []
            for i in range(count):
                g_re, g_im = gs[i, re_rows, lanes], gs[i, im_rows, lanes]
                if i == 0:
                    h_re.append(g_re)
                    h_im.append(g_im)
                elif sign > 0:
                    h_re.append(g_re - last_im)
                    h_im.append(g_im + last_re)
                else:
                    h_re.append(g_re + last_im)
                    h_im.append(g_im - last_re)
                last_re, last_im = g_re, g_im
            for j in range(count):
                s_re = f_re[0] * h_re[j] - f_im[0] * h_im[j]
                s_im = f_re[0] * h_im[j] + f_im[0] * h_re[j]
                for i in range(1, j + 1):
                    s_re = s_re + f_re[i] * h_re[j - i] - f_im[i] * h_im[j - i]
                    s_im = s_im + f_re[i] * h_im[j - i] + f_im[i] * h_re[j - i]
                ss[j, re_rows, lanes] = s_re
                ss[j, im_rows, lanes] = s_im

    half = width // 16

    @pl.loop(0, half)
    def _(row):
        tile(row, 1)

    @pl.loop(half, 2 * half)
    def _(row):
        tile(row, -1)


def pairs(items, columns):
    size = 2 if columns == 128 else 1
    return [items[at : at + size] for at in range(0, len(items), size)]


def conv_kernel(steps, fh_ref, fl_ref, ih_ref, il_ref, fs, *refs):
    gs, ss = refs[-2:]
    count, columns = gs.shape[0], gs.shape[2]
    width = gs.shape[1] // 2
    if steps:
        blocks, outs = dict(zip(steps, refs[:count])), dict(zip(steps, refs[count:-2]))
        where = partner
    else:
        steps = list(range(count))
        blocks, outs = ({k: ref.at[k] for k in steps} for ref in refs[:2])
        where = int
    for group in pairs(steps, columns):
        found = transform(fh_ref[...], fl_ref[...], jnp.concatenate([blocks[k][...] for k in group], axis=1))
        for at, k in enumerate(group):
            gs[where(k)] = found[:, at * columns : (at + 1) * columns]
    multiply_spectra(count, width, columns, fs, gs, ss)
    for group in pairs(steps, columns):
        total = jnp.concatenate([ss[where(k)] for k in group], axis=1)
        high = total.astype(jnp.bfloat16)
        low = (total - high.astype(jnp.float32)).astype(jnp.bfloat16)
        conv = dot(ih_ref[...], high) + dot(ih_ref[...], low) + dot(il_ref[...], high)
        conv = conv.astype(jnp.bfloat16)
        for at, k in enumerate(group):
            outs[k][...] = conv[:, at * columns : (at + 1) * columns]


def block_conv(tabs, filt, steps, blocks):
    count, twice, columns = filt.shape
    width = twice // 2
    spectra = pltpu.VMEM((count, twice, columns), jnp.float32)
    return pl.pallas_call(
        functools.partial(conv_kernel, steps),
        out_shape=[jax.ShapeDtypeStruct(block.shape, jnp.bfloat16) for block in blocks],
        in_specs=[WHOLE] * (5 + len(blocks)),
        out_specs=[WHOLE] * len(blocks),
        scratch_shapes=[spectra, spectra],
        compiler_params=pltpu.CompilerParams(vmem_limit_bytes=20 * MIB),
        cost_estimate=pl.CostEstimate(
            flops=24 * count * width * width * columns,
            bytes_accessed=14 * count * width * columns,
            transcendentals=0,
        ),
    )(*tabs, filt, *blocks)


def pre_kernel(steps, part, query_ref, skip_ref, *refs):
    count = len(steps)
    pieces = len(refs) // 2 - 1
    convs, gates, (pre_ref, square_ref) = refs[:pieces], refs[pieces : 2 * pieces], refs[-2:]
    width = query_ref.shape[0]
    total = jnp.zeros((width, 128), jnp.float32)

    def add(total, start, conv_ref, gated_ref):
        for at in range(0, conv_ref.shape[1], 128):
            lanes, cols = pl.ds(at, 128), pl.ds(pl.multiple_of(start + at, 128), 128)
            gated = gated_ref[:, lanes].astype(jnp.float32)
            conv = conv_ref[:, lanes].astype(jnp.float32)
            pre = query_ref[:, cols].astype(jnp.float32) * (conv + skip_ref[:, cols] * gated)
            pre_ref[:, cols] = pre
            total = total + pre * pre
        return total

    if pieces > count:
        for j in range(count):
            total = add(total, j * part, convs[-1].at[j], gates[-1].at[j])
    for k, conv_ref, gated_ref in zip(steps, convs, gates):
        start = partner(k) * part + part - conv_ref.shape[1] if count > 1 else 0
        total = add(total, start, conv_ref, gated_ref)
    square_ref[...] = jnp.sum(total.T, axis=0, keepdims=True)


def together(blocks):
    count = len(blocks)
    order = jnp.arange(count, dtype=jnp.int32) ^ lax.axis_index("tok")
    stacked = jnp.take(jnp.stack([blocks[k] for k in range(count)]), order, axis=0)
    return stacked.transpose(1, 0, 2).reshape(blocks[0].shape[0], -1)


def gated_output(query, skip, steps, convs, gates):
    width, columns = query.shape
    part = columns // len(steps)
    if part % 128:
        convs, gates = ([together(dict(zip(steps, blocks)))] for blocks in (convs, gates))
        steps = [0]
    return pl.pallas_call(
        functools.partial(pre_kernel, steps, part),
        out_shape=(
            jax.ShapeDtypeStruct((width, columns), jnp.float32),
            jax.ShapeDtypeStruct((1, width), jnp.float32),
        ),
        in_specs=[WHOLE] * (2 + 2 * len(convs)),
        out_specs=(WHOLE, WHOLE),
        compiler_params=pltpu.CompilerParams(vmem_limit_bytes=16 * MIB),
        cost_estimate=pl.CostEstimate(flops=6 * width * columns, bytes_accessed=10 * width * columns, transcendentals=0),
    )(query, skip, *convs, *gates)


def scale_kernel(channels, steps, pre_ref, square_ref, gain_ref, out_ref, buf, sems):
    width = pre_ref.shape[0]
    rows = width // steps
    scale = lax.rsqrt(square_ref[...] * (1.0 / channels) + 1e-06)
    scale = jnp.broadcast_to(scale, (128, width)).T
    copies = []
    for s in range(steps):
        for at in range(0, pre_ref.shape[1], 128):
            cols = pl.ds(at, 128)
            here = scale[s * rows : (s + 1) * rows, :]
            buf[pl.ds(s * rows, rows), cols] = gain_ref[:, cols] * pre_ref[pl.ds(s * rows, rows), cols] * here
        window = pl.ds(s * rows, rows)
        copies.append(pltpu.make_async_copy(buf.at[window, :], out_ref.at[window, :], sems.at[s]))
        copies[-1].start()
    for copy in copies:
        copy.wait()


def scaled(channels, pre, square, out_gain):
    width, columns = pre.shape
    steps = 8
    return pl.pallas_call(
        functools.partial(scale_kernel, channels, steps),
        out_shape=jax.ShapeDtypeStruct((width, columns), jnp.float32),
        in_specs=[WHOLE] * 3,
        out_specs=IN_HBM,
        scratch_shapes=[pltpu.VMEM((width, columns), jnp.float32), pltpu.SemaphoreType.DMA((steps,))],
        compiler_params=pltpu.CompilerParams(vmem_limit_bytes=16 * MIB),
        cost_estimate=pl.CostEstimate(flops=2 * width * columns, bytes_accessed=8 * width * columns, transcendentals=0),
    )(pre, square, out_gain)


def local(query, key_in, value_in, filter_store, lag_of_block, skip, out_gain):
    width, columns = query.shape
    count = lax.axis_size("tok")
    tabs = [jnp.asarray(t) for t in tables(width)]
    own = list(split(count, filter_store))
    own[0], (key_in, value_in) = after(own[0], key_in, value_in)
    lasts, firsts = gate(count, key_in, value_in)
    order = sending_order(count)
    steps = order + [0]
    filts = [send(own[k], k, count) for k in order]
    blocks = []
    for at, k in enumerate(order):
        block = lasts[k]
        if at + 2 < len(order):
            block, (filts[at + 2],) = after(block, filts[at + 2])
        blocks.append(send(block, k, count))
    filt = filter_spectra(lag_of_block, *tabs[:2], dict(zip(steps, filts + own[:1])))
    own_last = lasts[0]
    spread_convs = []
    for filt_first, first in zip(filt[:-1], firsts):
        (done,) = block_conv(tabs, filt_first, [], [spread(first)])
        own_last, (done,) = after(own_last, done)
        spread_convs.append(spread(done))
    done = block_conv(tabs, filt[-1], steps, blocks + [own_last])
    convs = [send(done[at], k, count) for at, k in enumerate(order)] + [done[-1]]
    gates = [lasts[k] for k in steps] + list(firsts)
    pre, square = gated_output(query, skip[None, :], steps, convs + spread_convs, gates)
    square = lax.psum(square, "chan")
    return scaled(columns * lax.axis_size("chan"), pre, square, out_gain[None, :])


def solution(mesh):
    in_specs = (
        P("tok", "chan"),
        P("tok", "chan"),
        P("tok", "chan"),
        P("tok", "chan"),
        P(),
        P("chan"),
        P("chan"),
    )
    return jax.shard_map(local, mesh=mesh, in_specs=in_specs, out_specs=P("tok", "chan"), check_vma=False)
```

```python
import functools
import math

import jax
import jax.numpy as jnp
import ml_dtypes
import numpy as np
from jax import lax
from jax.experimental import pallas as pl
from jax.experimental.pallas import tpu as pltpu
from jax.sharding import PartitionSpec as P

MIB = 1024 * 1024
BIG = 48 * MIB
WHOLE = pl.BlockSpec(memory_space=pltpu.VMEM)
IN_HBM = pl.BlockSpec(memory_space=pltpu.HBM)


def split_bf16(table):
    high = table.astype(ml_dtypes.bfloat16)
    low = (table - high.astype(np.float64)).astype(ml_dtypes.bfloat16)
    return high, low


def tables(width):
    freq = np.concatenate([np.arange(0, width, 2), np.arange(1, width, 2)])
    place = np.arange(width)
    steps = ((2 * freq[:, None] + 1) * place[None, :]) % (4 * width)
    angle = math.pi / (2 * width) * steps
    forward = np.concatenate([np.cos(angle), -np.sin(angle)], axis=0)
    inverse = forward.T / width
    return split_bf16(forward) + split_bf16(inverse)


def partner(step):
    return lax.axis_index("tok") ^ step


def send(block, step, count):
    return lax.ppermute(block, "tok", [(d, d ^ step) for d in range(count)])


def sending_order(count):
    half = count // 2
    far = list(range(half, count, 2)) + list(range(half + 1, count, 2))
    near = list(range(2, half)) + [1]
    order = []
    for at in range(half - 1):
        order += [far[at], near[at]]
    return order[:-1] + far[-1:] + order[-1:]


def columns_of(step, part):
    return pl.ds(pl.multiple_of(partner(step) * part, 128), part)


def piece(x, step, part):
    return lax.dynamic_slice_in_dim(x, partner(step) * part, part, axis=1)


def gate_kernel(alone, paired, part, filt_ref, key_ref, value_ref, *refs):
    width = key_ref.shape[0]
    outs, (key_buf, value_buf, sems) = list(refs[:-3]), refs[-3:]
    filts, gates = dict(zip(alone, outs)), dict(zip(alone + paired, outs[len(alone) :]))
    copies, stores = {}, []
    for k in alone + paired:
        cols = columns_of(k, part)
        copies[k] = (
            pltpu.make_async_copy(key_ref.at[:, cols], key_buf.at[k], sems.at[0, k]),
            pltpu.make_async_copy(value_ref.at[:, cols], value_buf.at[k], sems.at[1, k]),
        )
        for copy in copies[k]:
            copy.start()
    for k in alone + paired:
        to = filts[k] if k in filts else gates[k].at[pl.ds(0, width), :]
        stores.append(pltpu.make_async_copy(filt_ref.at[:, columns_of(k, part)], to, sems.at[2, k]))
        stores[-1].start()
    for k in alone + paired:
        for copy in copies[k]:
            copy.wait()
        product = key_buf[k].astype(jnp.float32) * value_buf[k].astype(jnp.float32)
        gates[k][pl.ds(0 if k in filts else width, width), :] = product.astype(jnp.bfloat16)
    for copy in stores:
        copy.wait()


def gate(count, alone, paired, filter_store, key_in, value_in):
    width, columns = key_in.shape
    part = columns // count
    if part % 128:
        gated = (key_in.astype(jnp.float32) * value_in.astype(jnp.float32)).astype(jnp.bfloat16)
        filts, gates = ({k: piece(x, k, part) for k in alone + paired} for x in (filter_store, gated))
        for k in paired:
            gates[k] = jnp.concatenate([filts.pop(k), gates[k]], axis=0)
        return filts, gates
    block = pltpu.VMEM((count, width, part), jnp.bfloat16)
    shapes = [jax.ShapeDtypeStruct((width, part), jnp.bfloat16)] * (2 * len(alone))
    shapes += [jax.ShapeDtypeStruct((2 * width, part), jnp.bfloat16)] * len(paired)
    found = pl.pallas_call(
        functools.partial(gate_kernel, alone, paired, part),
        out_shape=shapes,
        in_specs=[IN_HBM] * 3,
        out_specs=[WHOLE] * len(shapes),
        scratch_shapes=[block, block, pltpu.SemaphoreType.DMA((3, count))],
        compiler_params=pltpu.CompilerParams(vmem_limit_bytes=16 * MIB),
        cost_estimate=pl.CostEstimate(flops=width * columns, bytes_accessed=10 * width * columns, transcendentals=0),
    )(filter_store, key_in, value_in)
    return dict(zip(alone, found)), dict(zip(alone + paired, found[len(alone) :]))


def dot(x, y):
    return jnp.dot(x, y, preferred_element_type=jnp.float32)


def transform(high, low, block):
    return dot(high, block) + dot(low, block)


def filter_kernel(steps, lag_ref, high_ref, low_ref, *refs):
    blocks, out = refs[:-1], refs[-1]
    for k, block in zip(steps, blocks):
        rows = pl.ds(0, out.shape[1] // 2)
        out[lag_ref[partner(k)]] = transform(high_ref[...], low_ref[...], block[rows, :])


def gated_rows(block, width):
    return block[pl.ds(block.shape[0] - width, width), :]


def gated_kernel(steps, high_ref, low_ref, *refs):
    blocks, out = refs[:-1], refs[-1]
    for k, block in zip(steps, blocks):
        rows = gated_rows(block, out.shape[1] // 2)
        out[partner(k)] = transform(high_ref[...], low_ref[...], rows)


def spectra_shape(count, width, columns):
    return jax.ShapeDtypeStruct((count, 2 * width, columns), jnp.float32)


def transform_cost(count, width, columns, passes):
    return pl.CostEstimate(
        flops=4 * passes * count * width * width * columns,
        bytes_accessed=10 * count * width * columns,
        transcendentals=0,
    )


def filter_spectra(lag_of_block, high, low, blocks):
    steps = list(blocks)
    width, columns = blocks[0].shape
    return pl.pallas_call(
        functools.partial(filter_kernel, steps),
        out_shape=spectra_shape(len(steps), width, columns),
        in_specs=[pl.BlockSpec(memory_space=pltpu.SMEM)] + [WHOLE] * (2 + len(steps)),
        out_specs=WHOLE,
        compiler_params=pltpu.CompilerParams(vmem_limit_bytes=16 * MIB),
        cost_estimate=transform_cost(len(steps), width, columns, 2),
    )(lag_of_block, high, low, *[blocks[k] for k in steps])


def gated_spectra(count, high, low, blocks):
    steps = list(blocks)
    width, columns = blocks[0].shape
    return pl.pallas_call(
        functools.partial(gated_kernel, steps),
        out_shape=spectra_shape(count, width, columns),
        in_specs=[WHOLE] * (2 + len(steps)),
        out_specs=WHOLE,
        compiler_params=pltpu.CompilerParams(vmem_limit_bytes=16 * MIB),
        cost_estimate=transform_cost(len(steps), width, columns, 2),
    )(high, low, *[blocks[k] for k in steps])


def product_kernel(count, steps, first, fh_ref, fl_ref, ih_ref, il_ref, fs, gs, *refs):
    blocks, (gs, ss), outs = refs[: len(steps)], refs[len(steps) : len(steps) + 2], refs[len(steps) + 2 :]
    width, columns = outs[0].shape
    for k, block in zip(steps, blocks):
        gs[partner(k)] = transform(fh_ref[...], fl_ref[...], gated_rows(block, width))
    lane = min(128, columns)

    def products(row, sign):
        re_rows = pl.ds(pl.multiple_of(row * 8, 8), 8)
        im_rows = pl.ds(pl.multiple_of(row * 8 + width, 8), 8)
        for at in range(0, columns, lane):
            lanes = pl.ds(at, lane)
            f_re = [fs[i, re_rows, lanes] for i in range(count)]
            f_im = [fs[i, im_rows, lanes] for i in range(count)]
            h_re, h_im = [], []
            for i in range(count):
                g_re, g_im = gs[i, re_rows, lanes], gs[i, im_rows, lanes]
                if i == 0:
                    h_re.append(g_re)
                    h_im.append(g_im)
                elif sign > 0:
                    h_re.append(g_re - last_im)
                    h_im.append(g_im + last_re)
                else:
                    h_re.append(g_re + last_im)
                    h_im.append(g_im - last_re)
                last_re, last_im = g_re, g_im
            for j in range(count):
                s_re = f_re[0] * h_re[j] - f_im[0] * h_im[j]
                s_im = f_re[0] * h_im[j] + f_im[0] * h_re[j]
                for i in range(1, j + 1):
                    s_re = s_re + f_re[i] * h_re[j - i] - f_im[i] * h_im[j - i]
                    s_im = s_im + f_re[i] * h_im[j - i] + f_im[i] * h_re[j - i]
                ss[j, re_rows, lanes] = s_re
                ss[j, im_rows, lanes] = s_im

    half = width // 16

    @pl.loop(0, half)
    def _(row):
        products(row, 1)

    @pl.loop(half, 2 * half)
    def _(row):
        products(row, -1)

    for k, out in zip(first, outs):
        out[...] = inverse(ih_ref[...], il_ref[...], ss[partner(k)])


def inverse(table_high, table_low, total):
    high = total.astype(jnp.bfloat16)
    low = (total - high.astype(jnp.float32)).astype(jnp.bfloat16)
    return (dot(table_high, high) + dot(table_high, low) + dot(table_low, high)).astype(jnp.bfloat16)


def products(first, tabs, filt, gated, blocks):
    steps = list(blocks)
    count, twice, columns = gated.shape
    width = twice // 2
    found = pl.pallas_call(
        functools.partial(product_kernel, count, steps, first),
        out_shape=[jax.ShapeDtypeStruct(gated.shape, jnp.float32)] * 2
        + [jax.ShapeDtypeStruct((width, columns), jnp.bfloat16)] * len(first),
        in_specs=[WHOLE] * (6 + len(steps)),
        out_specs=[WHOLE] * (2 + len(first)),
        input_output_aliases={5: 0},
        compiler_params=pltpu.CompilerParams(vmem_limit_bytes=20 * MIB),
        cost_estimate=transform_cost(count, width, columns, 7),
    )(*tabs, filt, gated, *[blocks[k] for k in steps])
    return found[1], dict(zip(first, found[2:]))


def inverse_kernel(steps, ih_ref, il_ref, ss, *outs):
    for k, out in zip(steps, outs):
        out[...] = inverse(ih_ref[...], il_ref[...], ss[partner(k)])


def inverses(steps, tabs, sums):
    count, twice, columns = sums.shape
    width = twice // 2
    found = pl.pallas_call(
        functools.partial(inverse_kernel, steps),
        out_shape=[jax.ShapeDtypeStruct((width, columns), jnp.bfloat16)] * len(steps),
        in_specs=[WHOLE] * 3,
        out_specs=[WHOLE] * len(steps),
        compiler_params=pltpu.CompilerParams(vmem_limit_bytes=16 * MIB),
        cost_estimate=transform_cost(len(steps), width, columns, 3),
    )(*tabs[2:], sums)
    return dict(zip(steps, found))


def pre_kernel(steps, query_ref, skip_ref, *refs):
    count = len(steps)
    convs, gates, (pre_ref, square_ref) = refs[:count], refs[count : 2 * count], refs[2 * count :]
    width, part = convs[0].shape
    total = jnp.zeros((width, 128), jnp.float32)
    for at_k, k in enumerate(steps):
        start = partner(k) * part if count > 1 else 0
        for at in range(0, part, 128):
            lanes, cols = pl.ds(at, 128), pl.ds(pl.multiple_of(start + at, 128), 128)
            gated = gates[at_k][pl.ds(gates[at_k].shape[0] - width, width), lanes].astype(jnp.float32)
            conv = convs[at_k][:, lanes].astype(jnp.float32)
            pre = query_ref[:, cols].astype(jnp.float32) * (conv + skip_ref[:, cols] * gated)
            pre_ref[:, cols] = pre
            total = total + pre * pre
    square_ref[...] = jnp.sum(total.T, axis=0, keepdims=True)


def together(blocks, width):
    count = len(blocks)
    order = jnp.arange(count, dtype=jnp.int32) ^ lax.axis_index("tok")
    stacked = jnp.take(jnp.stack([blocks[k][-width:] for k in range(count)]), order, axis=0)
    return {0: stacked.transpose(1, 0, 2).reshape(width, -1)}


def gated_output(query, skip, convs, gates):
    width, columns = query.shape
    steps = list(convs)
    if convs[0].shape[1] % 128:
        convs, gates, steps = together(convs, width), together(gates, width), [0]
    count = len(steps)
    return pl.pallas_call(
        functools.partial(pre_kernel, steps),
        out_shape=(
            jax.ShapeDtypeStruct((width, columns), jnp.float32),
            jax.ShapeDtypeStruct((1, width), jnp.float32),
        ),
        in_specs=[WHOLE] * (2 + 2 * count),
        out_specs=(WHOLE, WHOLE),
        compiler_params=pltpu.CompilerParams(vmem_limit_bytes=16 * MIB),
        cost_estimate=pl.CostEstimate(flops=6 * width * columns, bytes_accessed=10 * width * columns, transcendentals=0),
    )(query, skip, *[convs[k] for k in steps], *[gates[k] for k in steps])


def scale_kernel(channels, steps, pre_ref, gain_ref, *refs):
    squares, (out_ref, buf, sems) = refs[:-3], refs[-3:]
    width = pre_ref.shape[0]
    rows = width // steps
    total = squares[0][...]
    for square in squares[1:]:
        total = total + square[...]
    scale = lax.rsqrt(total * (1.0 / channels) + 1e-06)
    scale = jnp.broadcast_to(scale, (128, width)).T
    copies = []
    for s in range(steps):
        for at in range(0, pre_ref.shape[1], 128):
            cols = pl.ds(at, 128)
            here = scale[s * rows : (s + 1) * rows, :]
            buf[pl.ds(s * rows, rows), cols] = gain_ref[:, cols] * pre_ref[pl.ds(s * rows, rows), cols] * here
        window = pl.ds(s * rows, rows)
        copies.append(pltpu.make_async_copy(buf.at[window, :], out_ref.at[window, :], sems.at[s]))
        copies[-1].start()
    for copy in copies:
        copy.wait()


def scaled(channels, pre, squares, out_gain):
    width, columns = pre.shape
    steps = 8
    return pl.pallas_call(
        functools.partial(scale_kernel, channels, steps),
        out_shape=jax.ShapeDtypeStruct((width, columns), jnp.float32),
        in_specs=[WHOLE] * (2 + len(squares)),
        out_specs=IN_HBM,
        scratch_shapes=[pltpu.VMEM((width, columns), jnp.float32), pltpu.SemaphoreType.DMA((steps,))],
        compiler_params=pltpu.CompilerParams(vmem_limit_bytes=16 * MIB),
        cost_estimate=pl.CostEstimate(flops=2 * width * columns, bytes_accessed=8 * width * columns, transcendentals=0),
    )(pre, out_gain, *squares)


def local(query, key_in, value_in, filter_store, lag_of_block, skip, out_gain):
    width, columns = query.shape
    count = lax.axis_size("tok")
    tabs = [jnp.asarray(t) for t in tables(width)]
    part = columns // count
    order = sending_order(count)
    at = count // 2
    ahead, alone, paired = order[:1], order[1:at], order[at:]
    filts = {k: send(piece(filter_store, k, part), k, count) for k in ahead}
    own_filts, mine = gate(count, alone + [0] + ahead, paired, filter_store, key_in, value_in)
    gates = {}
    for k in alone:
        filts[k] = send(own_filts[k], k, count)
    for k in paired:
        filts[k] = gates[k] = send(mine[k], k, count)
    for k in ahead + alone:
        gates[k] = send(mine[k], k, count)
    filts[0], gates[0] = own_filts[0], mine[0]
    late = (ahead + alone)[1:]
    early = paired + [ahead[0], 0]
    filt = filter_spectra(lag_of_block, *tabs[:2], filts)
    gated = gated_spectra(count, *tabs[:2], {k: gates[k] for k in early})
    first = order[:1]
    sums, found = products(first, tabs, filt, gated, {k: gates[k] for k in late})
    found.update(inverses(order[1:] + [0], tabs, sums))
    convs = {k: send(found[k], k, count) for k in order}
    convs[0] = found[0]
    pre, square = gated_output(query, skip[None, :], convs, mine)
    others = lax.axis_size("chan")
    squares = [square] + [
        lax.ppermute(square, "chan", [(d, d ^ step) for d in range(others)]) for step in reversed(range(1, others))
    ]
    return scaled(columns * others, pre, squares, out_gain[None, :])


def solution(mesh):
    in_specs = (
        P("tok", "chan"),
        P("tok", "chan"),
        P("tok", "chan"),
        P("tok", "chan"),
        P(),
        P("chan"),
        P("chan"),
    )
    return jax.shard_map(local, mesh=mesh, in_specs=in_specs, out_specs=P("tok", "chan"), check_vma=False)
```

```python
import functools
import math

import jax
import jax.numpy as jnp
import ml_dtypes
import numpy as np
from jax import lax
from jax.experimental import pallas as pl
from jax.experimental.pallas import tpu as pltpu
from jax.sharding import PartitionSpec as P

MIB = 1024 * 1024
BIG = 48 * MIB
WHOLE = pl.BlockSpec(memory_space=pltpu.VMEM)
IN_HBM = pl.BlockSpec(memory_space=pltpu.HBM)


def split_bf16(table):
    high = table.astype(ml_dtypes.bfloat16)
    low = (table - high.astype(np.float64)).astype(ml_dtypes.bfloat16)
    return high, low


def tables(width):
    freq = np.concatenate([np.arange(0, width, 2), np.arange(1, width, 2)])
    place = np.arange(width)
    steps = ((2 * freq[:, None] + 1) * place[None, :]) % (4 * width)
    angle = math.pi / (2 * width) * steps
    forward = np.concatenate([np.cos(angle), -np.sin(angle)], axis=0)
    inverse = forward.T / width
    return split_bf16(forward) + split_bf16(inverse)


def partner(step):
    return lax.axis_index("tok") ^ step


def send(block, step, count):
    return lax.ppermute(block, "tok", [(d, d ^ step) for d in range(count)])


def sending_order(count):
    half = count // 2
    far = list(range(half, count, 2)) + list(range(half + 1, count, 2))
    near = list(range(2, half)) + [1]
    order = []
    for at in range(half - 1):
        order += [far[at], near[at]]
    return order[:-1] + far[-1:] + order[-1:]


def columns_of(step, part):
    return pl.ds(pl.multiple_of(partner(step) * part, 128), part)


def piece(x, step, part):
    return lax.dynamic_slice_in_dim(x, partner(step) * part, part, axis=1)


def split_kernel(steps, part, filt_ref, *refs):
    outs, sems = refs[:-1], refs[-1]
    copies = []
    for at, k in enumerate(steps):
        copies.append(pltpu.make_async_copy(filt_ref.at[:, columns_of(k, part)], outs[at], sems.at[at]))
        copies[-1].start()
    for copy in copies:
        copy.wait()


def split(count, steps, filter_store):
    width, columns = filter_store.shape
    part = columns // count
    if part % 128:
        return {k: piece(filter_store, k, part) for k in steps}
    found = pl.pallas_call(
        functools.partial(split_kernel, steps, part),
        out_shape=[jax.ShapeDtypeStruct((width, part), jnp.bfloat16)] * len(steps),
        in_specs=[IN_HBM],
        out_specs=[WHOLE] * len(steps),
        scratch_shapes=[pltpu.SemaphoreType.DMA((len(steps),))],
        compiler_params=pltpu.CompilerParams(vmem_limit_bytes=16 * MIB),
        cost_estimate=pl.CostEstimate(flops=0, bytes_accessed=4 * width * columns, transcendentals=0),
    )(filter_store)
    return dict(zip(steps, found))


def gate_kernel(count, part, key_ref, value_ref, *refs):
    outs, (key_buf, value_buf, sems) = refs[:count], refs[count:]
    copies = []
    for k in range(count):
        cols = columns_of(k, part)
        copies.append(
            (
                pltpu.make_async_copy(key_ref.at[:, cols], key_buf.at[k], sems.at[0, k]),
                pltpu.make_async_copy(value_ref.at[:, cols], value_buf.at[k], sems.at[1, k]),
            )
        )
        for copy in copies[-1]:
            copy.start()
    for k in range(count):
        for copy in copies[k]:
            copy.wait()
        product = key_buf[k].astype(jnp.float32) * value_buf[k].astype(jnp.float32)
        outs[k][...] = product.astype(jnp.bfloat16)


def gate(count, key_in, value_in):
    width, columns = key_in.shape
    part = columns // count
    if part % 128:
        gated = (key_in.astype(jnp.float32) * value_in.astype(jnp.float32)).astype(jnp.bfloat16)
        return [piece(gated, k, part) for k in range(count)]
    block = pltpu.VMEM((count, width, part), jnp.bfloat16)
    return pl.pallas_call(
        functools.partial(gate_kernel, count, part),
        out_shape=[jax.ShapeDtypeStruct((width, part), jnp.bfloat16)] * count,
        in_specs=[IN_HBM] * 2,
        out_specs=[WHOLE] * count,
        scratch_shapes=[block, block, pltpu.SemaphoreType.DMA((2, count))],
        compiler_params=pltpu.CompilerParams(vmem_limit_bytes=16 * MIB),
        cost_estimate=pl.CostEstimate(flops=width * columns, bytes_accessed=6 * width * columns, transcendentals=0),
    )(key_in, value_in)


def dot(x, y):
    return jnp.dot(x, y, preferred_element_type=jnp.float32)


def transform(high, low, block):
    return dot(high, block) + dot(low, block)


def filter_kernel(steps, lag_ref, high_ref, low_ref, *refs):
    blocks, out = refs[:-1], refs[-1]
    count = len(steps)
    for at, (k, block) in enumerate(zip(steps, blocks)):
        out[at] = jnp.zeros(out.shape[1:], jnp.float32)
        out[count + lag_ref[partner(k)]] = transform(high_ref[...], low_ref[...], block[...])


def transform_cost(count, width, columns, passes):
    return pl.CostEstimate(
        flops=4 * passes * count * width * width * columns,
        bytes_accessed=10 * count * width * columns,
        transcendentals=0,
    )


def filter_spectra(lag_of_block, high, low, blocks):
    steps = list(blocks)
    count = len(steps)
    width, columns = blocks[0].shape
    return pl.pallas_call(
        functools.partial(filter_kernel, steps),
        out_shape=jax.ShapeDtypeStruct((2 * count, 2 * width, columns), jnp.float32),
        in_specs=[pl.BlockSpec(memory_space=pltpu.SMEM)] + [WHOLE] * (2 + count),
        out_specs=WHOLE,
        compiler_params=pltpu.CompilerParams(vmem_limit_bytes=16 * MIB),
        cost_estimate=transform_cost(count, width, columns, 2),
    )(lag_of_block, high, low, *[blocks[k] for k in steps])


def tiles(width, columns, tile):
    half = width // 16
    lane = min(128, columns)

    def run(row, sign):
        re_rows = pl.ds(pl.multiple_of(row * 8, 8), 8)
        im_rows = pl.ds(pl.multiple_of(row * 8 + width, 8), 8)
        for at in range(0, columns, lane):
            tile(re_rows, im_rows, pl.ds(at, lane), sign)

    @pl.loop(0, half)
    def _(row):
        run(row, 1)

    @pl.loop(half, 2 * half)
    def _(row):
        run(row, -1)


def early_kernel(count, steps, fh_ref, fl_ref, fs, *refs):
    blocks, (ss, gs) = refs[: len(steps)], refs[len(steps) :]
    width, columns = blocks[0].shape
    for k in range(count):
        if k not in steps:
            gs[partner(k)] = jnp.zeros(gs.shape[1:], jnp.float32)
    for k, block in zip(steps, blocks):
        gs[partner(k)] = transform(fh_ref[...], fl_ref[...], block[...])

    def tile(re_rows, im_rows, lanes, sign):
        f = [(fs[count + i, re_rows, lanes], fs[count + i, im_rows, lanes]) for i in range(count)]
        h, last = [], None
        for i in range(count):
            here = (gs[i, re_rows, lanes], gs[i, im_rows, lanes])
            if last is None:
                h.append(here)
            elif sign > 0:
                h.append((here[0] - last[1], here[1] + last[0]))
            else:
                h.append((here[0] + last[1], here[1] - last[0]))
            last = here
        for j in range(count):
            s_re = f[0][0] * h[j][0] - f[0][1] * h[j][1]
            s_im = f[0][0] * h[j][1] + f[0][1] * h[j][0]
            for i in range(1, j + 1):
                s_re = s_re + f[i][0] * h[j - i][0] - f[i][1] * h[j - i][1]
                s_im = s_im + f[i][0] * h[j - i][1] + f[i][1] * h[j - i][0]
            ss[j, re_rows, lanes] = s_re
            ss[j, im_rows, lanes] = s_im

    tiles(width, columns, tile)


def early_products(tabs, filt, blocks):
    steps = list(blocks)
    count = filt.shape[0] // 2
    width, columns = blocks[0].shape
    shape = (count, 2 * width, columns)
    return pl.pallas_call(
        functools.partial(early_kernel, count, steps),
        out_shape=jax.ShapeDtypeStruct(shape, jnp.float32),
        in_specs=[WHOLE] * (3 + len(steps)),
        out_specs=WHOLE,
        scratch_shapes=[pltpu.VMEM(shape, jnp.float32)],
        compiler_params=pltpu.CompilerParams(vmem_limit_bytes=16 * MIB),
        cost_estimate=transform_cost(count, width, columns, 4),
    )(*tabs[:2], filt, *[blocks[k] for k in steps])


def inverse(table_high, table_low, total):
    high = total.astype(jnp.bfloat16)
    low = (total - high.astype(jnp.float32)).astype(jnp.bfloat16)
    return (dot(table_high, high) + dot(table_high, low) + dot(table_low, high)).astype(jnp.bfloat16)


def late_kernel(count, steps, first, fh_ref, fl_ref, ih_ref, il_ref, fs, sums, *refs):
    blocks, ss, outs, gs = refs[: len(steps)], refs[len(steps)], refs[len(steps) + 1 : -1], refs[-1]
    width, columns = blocks[0].shape
    for at, block in enumerate(blocks):
        gs[at] = transform(fh_ref[...], fl_ref[...], block[...])
    starts = [count - partner(k) for k in steps]

    def tile(re_rows, im_rows, lanes, sign):
        g = [(gs[at, re_rows, lanes], gs[at, im_rows, lanes]) for at in range(len(steps))]
        last = None
        for j in range(count):
            d_re = d_im = None
            for start, (g_re, g_im) in zip(starts, g):
                f_re, f_im = fs[start + j, re_rows, lanes], fs[start + j, im_rows, lanes]
                p_re, p_im = f_re * g_re - f_im * g_im, f_re * g_im + f_im * g_re
                d_re, d_im = (p_re, p_im) if d_re is None else (d_re + p_re, d_im + p_im)
            s_re, s_im = ss[j, re_rows, lanes] + d_re, ss[j, im_rows, lanes] + d_im
            if last is not None and sign > 0:
                s_re, s_im = s_re - last[1], s_im + last[0]
            elif last is not None:
                s_re, s_im = s_re + last[1], s_im - last[0]
            ss[j, re_rows, lanes] = s_re
            ss[j, im_rows, lanes] = s_im
            last = (d_re, d_im)

    tiles(width, columns, tile)
    for k, out in zip(first, outs):
        out[...] = inverse(ih_ref[...], il_ref[...], ss[partner(k)])


def late_products(first, tabs, filt, sums, blocks):
    steps = list(blocks)
    count, twice, columns = sums.shape
    width = twice // 2
    found = pl.pallas_call(
        functools.partial(late_kernel, count, steps, first),
        out_shape=[jax.ShapeDtypeStruct(sums.shape, jnp.float32)]
        + [jax.ShapeDtypeStruct((width, columns), jnp.bfloat16)] * len(first),
        in_specs=[WHOLE] * (6 + len(steps)),
        out_specs=[WHOLE] * (1 + len(first)),
        scratch_shapes=[pltpu.VMEM((len(steps), twice, columns), jnp.float32)],
        input_output_aliases={5: 0},
        compiler_params=pltpu.CompilerParams(vmem_limit_bytes=16 * MIB),
        cost_estimate=transform_cost(count, width, columns, 3),
    )(*tabs, filt, sums, *[blocks[k] for k in steps])
    return found[0], dict(zip(first, found[1:]))


def inverse_kernel(steps, ih_ref, il_ref, ss, *outs):
    for k, out in zip(steps, outs):
        out[...] = inverse(ih_ref[...], il_ref[...], ss[partner(k)])


def inverses(steps, tabs, sums):
    count, twice, columns = sums.shape
    width = twice // 2
    found = pl.pallas_call(
        functools.partial(inverse_kernel, steps),
        out_shape=[jax.ShapeDtypeStruct((width, columns), jnp.bfloat16)] * len(steps),
        in_specs=[WHOLE] * 3,
        out_specs=[WHOLE] * len(steps),
        compiler_params=pltpu.CompilerParams(vmem_limit_bytes=16 * MIB),
        cost_estimate=transform_cost(len(steps), width, columns, 3),
    )(*tabs[2:], sums)
    return dict(zip(steps, found))


def pre_kernel(steps, before, after, query_ref, skip_ref, *refs):
    count = len(steps)
    refs = list(refs)
    total = jnp.zeros((query_ref.shape[0], 128), jnp.float32)
    if before:
        refs.pop(0)
        total = refs.pop(0)[...]
    convs, gates, (pre_ref, square_ref) = refs[:count], refs[count : 2 * count], refs[2 * count :]
    width, part = convs[0].shape
    for at_k, k in enumerate(steps):
        start = partner(k) * part if part < query_ref.shape[1] else 0
        for at in range(0, part, 128):
            lanes, cols = pl.ds(at, 128), pl.ds(pl.multiple_of(start + at, 128), 128)
            gated = gates[at_k][:, lanes].astype(jnp.float32)
            conv = convs[at_k][:, lanes].astype(jnp.float32)
            pre = query_ref[:, cols].astype(jnp.float32) * (conv + skip_ref[:, cols] * gated)
            pre_ref[:, cols] = pre
            total = total + pre * pre
    if after:
        square_ref[...] = total
    else:
        square_ref[...] = jnp.sum(total.T, axis=0, keepdims=True)


def together(blocks):
    count, width = len(blocks), blocks[0].shape[0]
    order = jnp.arange(count, dtype=jnp.int32) ^ lax.axis_index("tok")
    stacked = jnp.take(jnp.stack([blocks[k] for k in range(count)]), order, axis=0)
    return {0: stacked.transpose(1, 0, 2).reshape(width, -1)}


def gated_output(query, skip, early, convs, gates):
    width, columns = query.shape
    groups = [early, [k for k in convs if k not in early]]
    if convs[0].shape[1] % 128:
        convs, gates, groups = together(convs), together(gates), [[0]]
    found = []
    for at, steps in enumerate(groups):
        rest = at + 1 < len(groups)
        found = pl.pallas_call(
            functools.partial(pre_kernel, steps, at > 0, rest),
            out_shape=(
                jax.ShapeDtypeStruct((width, columns), jnp.float32),
                jax.ShapeDtypeStruct((width, 128) if rest else (1, width), jnp.float32),
            ),
            in_specs=[WHOLE] * (2 + len(found) + 2 * len(steps)),
            out_specs=(WHOLE, WHOLE),
            input_output_aliases={2: 0} if found else {},
            compiler_params=pltpu.CompilerParams(vmem_limit_bytes=16 * MIB),
            cost_estimate=pl.CostEstimate(
                flops=3 * width * columns, bytes_accessed=5 * width * columns, transcendentals=0
            ),
        )(query, skip, *found, *[convs[k] for k in steps], *[gates[k] for k in steps])
    return found


def scale_kernel(channels, steps, pre_ref, gain_ref, *refs):
    squares, (out_ref, buf, sems) = refs[:-3], refs[-3:]
    width = pre_ref.shape[0]
    rows = width // steps
    total = squares[0][...]
    for square in squares[1:]:
        total = total + square[...]
    scale = lax.rsqrt(total * (1.0 / channels) + 1e-06)
    scale = jnp.broadcast_to(scale, (128, width)).T
    copies = []
    for s in range(steps):
        for at in range(0, pre_ref.shape[1], 128):
            cols = pl.ds(at, 128)
            here = scale[s * rows : (s + 1) * rows, :]
            buf[pl.ds(s * rows, rows), cols] = gain_ref[:, cols] * pre_ref[pl.ds(s * rows, rows), cols] * here
        window = pl.ds(s * rows, rows)
        copies.append(pltpu.make_async_copy(buf.at[window, :], out_ref.at[window, :], sems.at[s]))
        copies[-1].start()
    for copy in copies:
        copy.wait()


def scaled(channels, pre, squares, out_gain):
    width, columns = pre.shape
    steps = 8
    return pl.pallas_call(
        functools.partial(scale_kernel, channels, steps),
        out_shape=jax.ShapeDtypeStruct((width, columns), jnp.float32),
        in_specs=[WHOLE] * (2 + len(squares)),
        out_specs=IN_HBM,
        scratch_shapes=[pltpu.VMEM((width, columns), jnp.float32), pltpu.SemaphoreType.DMA((steps,))],
        compiler_params=pltpu.CompilerParams(vmem_limit_bytes=16 * MIB),
        cost_estimate=pl.CostEstimate(flops=2 * width * columns, bytes_accessed=8 * width * columns, transcendentals=0),
    )(pre, out_gain, *squares)


def local(query, key_in, value_in, filter_store, lag_of_block, skip, out_gain):
    width, columns = query.shape
    count = lax.axis_size("tok")
    tabs = [jnp.asarray(t) for t in tables(width)]
    part = columns // count
    order = sending_order(count)
    gated_order = order[:-3] + order[-1:] + order[-3:-1]
    own = split(count, order[1:] + [0], filter_store)
    own[order[0]] = piece(filter_store, order[0], part)
    own[0], key_in, value_in = lax.optimization_barrier((own[0], key_in, value_in))
    mine = gate(count, key_in, value_in)
    filts = {k: send(own[k], k, count) for k in order}
    gates = {k: send(mine[k], k, count) for k in gated_order}
    filts[0], gates[0] = own[0], mine[0]
    late = gated_order[-2:]
    filt = filter_spectra(lag_of_block, *tabs[:2], filts)
    sums = early_products(tabs, filt, {k: gates[k] for k in gates if k not in late})
    sums, found = late_products(order[:1], tabs, filt, sums, {k: gates[k] for k in late})
    found.update(inverses(order[1:] + [0], tabs, sums))
    convs = {k: send(found[k], k, count) for k in order}
    convs[0] = found[0]
    pre, square = gated_output(query, skip[None, :], order[: count // 2] + [0], convs, mine)
    others = lax.axis_size("chan")
    squares = [square] + [
        lax.ppermute(square, "chan", [(d, d ^ step) for d in range(others)]) for step in reversed(range(1, others))
    ]
    return scaled(columns * others, pre, squares, out_gain[None, :])


def solution(mesh):
    in_specs = (
        P("tok", "chan"),
        P("tok", "chan"),
        P("tok", "chan"),
        P("tok", "chan"),
        P(),
        P("chan"),
        P("chan"),
    )
    return jax.shard_map(local, mesh=mesh, in_specs=in_specs, out_specs=P("tok", "chan"), check_vma=False)
```

```python
import functools
import math

import jax
import jax.numpy as jnp
import numpy as np
from jax import lax
from jax.experimental import pallas as pl
from jax.experimental.pallas import tpu as pltpu
from jax.sharding import PartitionSpec as P

MIB = 1024 * 1024
ALL = 56 * MIB
BIG = 48 * MIB
WHOLE = pl.BlockSpec(memory_space=pltpu.VMEM)
IN_HBM = pl.BlockSpec(memory_space=pltpu.HBM)


def tables(width):
    freq = np.concatenate([np.arange(0, width, 2), np.arange(1, width, 2)])
    place = np.arange(width)
    steps = ((2 * freq[:, None] + 1) * place[None, :]) % (4 * width)
    angle = math.pi / (2 * width) * steps
    forward = np.concatenate([np.cos(angle), -np.sin(angle)], axis=0)
    inverse = forward.T / width
    return forward.astype(np.float32), inverse.astype(np.float32)


def partner(step):
    return lax.axis_index("tok") ^ step


def send(block, step, count):
    return lax.ppermute(block, "tok", [(d, d ^ step) for d in range(count)])


def sending_order(count):
    half = count // 2
    far = list(range(half, count, 2)) + list(range(half + 1, count, 2))
    near = list(range(2, half)) + [1]
    order = []
    for at in range(half - 1):
        order += [far[at], near[at]]
    return order[:-1] + far[-1:] + order[-1:]


def columns_of(step, part):
    return pl.ds(pl.multiple_of(partner(step) * part, 128), part)


def piece(x, step, part):
    return lax.dynamic_slice_in_dim(x, partner(step) * part, part, axis=1)


def split_kernel(steps, part, filt_ref, *refs):
    outs, sems = refs[:-1], refs[-1]
    copies = []
    for at, k in enumerate(steps):
        copies.append(pltpu.make_async_copy(filt_ref.at[:, columns_of(k, part)], outs[at], sems.at[at]))
        copies[-1].start()
    for copy in copies:
        copy.wait()


def split(count, steps, filter_store):
    width, columns = filter_store.shape
    part = columns // count
    if part % 128:
        return {k: piece(filter_store, k, part) for k in steps}
    found = pl.pallas_call(
        functools.partial(split_kernel, steps, part),
        out_shape=[jax.ShapeDtypeStruct((width, part), jnp.bfloat16)] * len(steps),
        in_specs=[IN_HBM],
        out_specs=[IN_HBM] * len(steps),
        scratch_shapes=[pltpu.SemaphoreType.DMA((len(steps),))],
        compiler_params=pltpu.CompilerParams(vmem_limit_bytes=ALL),
        cost_estimate=pl.CostEstimate(flops=0, bytes_accessed=4 * width * columns, transcendentals=0),
    )(filter_store)
    return dict(zip(steps, found))


def gate_kernel(count, part, key_ref, value_ref, *refs):
    outs, (key_buf, value_buf, sems) = refs[:count], refs[count:]
    copies = []
    for k in range(count):
        cols = columns_of(k, part)
        copies.append(
            (
                pltpu.make_async_copy(key_ref.at[:, cols], key_buf.at[k], sems.at[0, k]),
                pltpu.make_async_copy(value_ref.at[:, cols], value_buf.at[k], sems.at[1, k]),
            )
        )
        for copy in copies[-1]:
            copy.start()
    stores = []
    for k in range(count):
        for copy in copies[k]:
            copy.wait()
        product = key_buf[k].astype(jnp.float32) * value_buf[k].astype(jnp.float32)
        key_buf[k] = product.astype(jnp.bfloat16)
        stores.append(pltpu.make_async_copy(key_buf.at[k], outs[k], sems.at[2, k]))
        stores[-1].start()
    for copy in stores:
        copy.wait()


def gate(count, key_in, value_in):
    width, columns = key_in.shape
    part = columns // count
    if part % 128:
        gated = (key_in.astype(jnp.float32) * value_in.astype(jnp.float32)).astype(jnp.bfloat16)
        return [piece(gated, k, part) for k in range(count)]
    block = pltpu.VMEM((count, width, part), jnp.bfloat16)
    return pl.pallas_call(
        functools.partial(gate_kernel, count, part),
        out_shape=[jax.ShapeDtypeStruct((width, part), jnp.bfloat16)] * count,
        in_specs=[IN_HBM] * 2,
        out_specs=[IN_HBM] * count,
        scratch_shapes=[block, block, pltpu.SemaphoreType.DMA((3, count))],
        compiler_params=pltpu.CompilerParams(vmem_limit_bytes=ALL),
        cost_estimate=pl.CostEstimate(flops=width * columns, bytes_accessed=6 * width * columns, transcendentals=0),
    )(key_in, value_in)


def dot(x, y):
    return jnp.dot(x, y, preferred_element_type=jnp.float32)


def transform(high, low, block):
    return dot(high, block) + dot(low, block)


def halves(value):
    high = value.astype(jnp.bfloat16)
    return high, (value - high.astype(jnp.float32)).astype(jnp.bfloat16)


def filter_kernel(steps, lag_ref, forward_ref, inverse_ref, *refs):
    count = len(steps)
    blocks, (out, fh_ref, fl_ref, ih_ref, il_ref) = refs[:count], refs[count:]
    fh_ref[...], fl_ref[...] = halves(forward_ref[...])
    ih_ref[...], il_ref[...] = halves(inverse_ref[...])
    for at, (k, block) in enumerate(zip(steps, blocks)):
        out[at] = jnp.zeros(out.shape[1:], jnp.float32)
        out[count + lag_ref[partner(k)]] = transform(fh_ref[...], fl_ref[...], block[...])


def transform_cost(count, width, columns, passes):
    return pl.CostEstimate(
        flops=4 * passes * count * width * width * columns,
        bytes_accessed=10 * count * width * columns,
        transcendentals=0,
    )


def filter_spectra(lag_of_block, blocks):
    steps = list(blocks)
    count = len(steps)
    width, columns = blocks[0].shape
    forward = jax.ShapeDtypeStruct((2 * width, width), jnp.bfloat16)
    backward = jax.ShapeDtypeStruct((width, 2 * width), jnp.bfloat16)
    found = pl.pallas_call(
        functools.partial(filter_kernel, steps),
        out_shape=[
            jax.ShapeDtypeStruct((2 * count, 2 * width, columns), jnp.float32),
            forward,
            forward,
            backward,
            backward,
        ],
        in_specs=[pl.BlockSpec(memory_space=pltpu.SMEM)] + [WHOLE] * (2 + count),
        out_specs=[WHOLE] * 5,
        compiler_params=pltpu.CompilerParams(vmem_limit_bytes=16 * MIB),
        cost_estimate=transform_cost(count, width, columns, 2),
    )(lag_of_block, *[jnp.asarray(table) for table in tables(width)], *[blocks[k] for k in steps])
    return found[0], found[1:]


def tiles(width, columns, tile):
    half = width // 16
    lane = min(128, columns)

    def run(row, sign):
        re_rows = pl.ds(pl.multiple_of(row * 8, 8), 8)
        im_rows = pl.ds(pl.multiple_of(row * 8 + width, 8), 8)
        for at in range(0, columns, lane):
            tile(re_rows, im_rows, pl.ds(at, lane), sign)

    @pl.loop(0, half)
    def _(row):
        run(row, 1)

    @pl.loop(half, 2 * half)
    def _(row):
        run(row, -1)


def early_kernel(count, steps, fh_ref, fl_ref, fs, *refs):
    blocks, (ss, gs) = refs[: len(steps)], refs[len(steps) :]
    width, columns = blocks[0].shape
    for k in range(count):
        if k not in steps:
            gs[partner(k)] = jnp.zeros(gs.shape[1:], jnp.float32)
    for k, block in zip(steps, blocks):
        gs[partner(k)] = transform(fh_ref[...], fl_ref[...], block[...])

    def tile(re_rows, im_rows, lanes, sign):
        f = [(fs[count + i, re_rows, lanes], fs[count + i, im_rows, lanes]) for i in range(count)]
        h, last = [], None
        for i in range(count):
            here = (gs[i, re_rows, lanes], gs[i, im_rows, lanes])
            if last is None:
                h.append(here)
            elif sign > 0:
                h.append((here[0] - last[1], here[1] + last[0]))
            else:
                h.append((here[0] + last[1], here[1] - last[0]))
            last = here
        for j in range(count):
            s_re = f[0][0] * h[j][0] - f[0][1] * h[j][1]
            s_im = f[0][0] * h[j][1] + f[0][1] * h[j][0]
            for i in range(1, j + 1):
                s_re = s_re + f[i][0] * h[j - i][0] - f[i][1] * h[j - i][1]
                s_im = s_im + f[i][0] * h[j - i][1] + f[i][1] * h[j - i][0]
            ss[j, re_rows, lanes] = s_re
            ss[j, im_rows, lanes] = s_im

    tiles(width, columns, tile)


def early_products(tabs, filt, blocks):
    steps = list(blocks)
    count = filt.shape[0] // 2
    width, columns = blocks[0].shape
    shape = (count, 2 * width, columns)
    return pl.pallas_call(
        functools.partial(early_kernel, count, steps),
        out_shape=jax.ShapeDtypeStruct(shape, jnp.float32),
        in_specs=[WHOLE] * (3 + len(steps)),
        out_specs=WHOLE,
        scratch_shapes=[pltpu.VMEM(shape, jnp.float32)],
        compiler_params=pltpu.CompilerParams(vmem_limit_bytes=16 * MIB),
        cost_estimate=transform_cost(count, width, columns, 4),
    )(*tabs[:2], filt, *[blocks[k] for k in steps])


def inverse(table_high, table_low, total):
    high, low = halves(total)
    return (dot(table_high, high) + dot(table_high, low) + dot(table_low, high)).astype(jnp.bfloat16)


def late_kernel(count, steps, first, fh_ref, fl_ref, ih_ref, il_ref, fs, sums, *refs):
    blocks, ss, outs, gs = refs[: len(steps)], refs[len(steps)], refs[len(steps) + 1 : -1], refs[-1]
    width, columns = blocks[0].shape
    for at, block in enumerate(blocks):
        gs[at] = transform(fh_ref[...], fl_ref[...], block[...])
    starts = [count - partner(k) for k in steps]

    def tile(re_rows, im_rows, lanes, sign):
        def both(ref, i):
            return ref[i, re_rows, lanes], ref[i, im_rows, lanes]

        g = [both(gs, at) for at in range(len(steps))]
        f = [[both(fs, start + j) for start in starts] for j in range(count)]
        s = [both(ss, j) for j in range(count)]
        d = []
        for j in range(count):
            d_re = d_im = None
            for (f_re, f_im), (g_re, g_im) in zip(f[j], g):
                p_re, p_im = f_re * g_re - f_im * g_im, f_re * g_im + f_im * g_re
                d_re, d_im = (p_re, p_im) if d_re is None else (d_re + p_re, d_im + p_im)
            d.append((d_re, d_im))
        for j in range(count):
            s_re, s_im = s[j][0] + d[j][0], s[j][1] + d[j][1]
            if j and sign > 0:
                s_re, s_im = s_re - d[j - 1][1], s_im + d[j - 1][0]
            elif j:
                s_re, s_im = s_re + d[j - 1][1], s_im - d[j - 1][0]
            ss[j, re_rows, lanes] = s_re
            ss[j, im_rows, lanes] = s_im

    tiles(width, columns, tile)
    for k, out in zip(first, outs):
        out[...] = inverse(ih_ref[...], il_ref[...], ss[partner(k)])


def late_products(first, tabs, filt, sums, blocks):
    steps = list(blocks)
    count, twice, columns = sums.shape
    width = twice // 2
    found = pl.pallas_call(
        functools.partial(late_kernel, count, steps, first),
        out_shape=[jax.ShapeDtypeStruct(sums.shape, jnp.float32)]
        + [jax.ShapeDtypeStruct((width, columns), jnp.bfloat16)] * len(first),
        in_specs=[WHOLE] * (6 + len(steps)),
        out_specs=[WHOLE] * (1 + len(first)),
        scratch_shapes=[pltpu.VMEM((len(steps), twice, columns), jnp.float32)],
        input_output_aliases={5: 0},
        compiler_params=pltpu.CompilerParams(vmem_limit_bytes=16 * MIB),
        cost_estimate=transform_cost(count, width, columns, 3),
    )(*tabs, filt, sums, *[blocks[k] for k in steps])
    return found[0], dict(zip(first, found[1:]))


def inverse_kernel(steps, ih_ref, il_ref, ss, *outs):
    for k, out in zip(steps, outs):
        out[...] = inverse(ih_ref[...], il_ref[...], ss[partner(k)])


def inverses(steps, tabs, sums):
    count, twice, columns = sums.shape
    width = twice // 2
    found = pl.pallas_call(
        functools.partial(inverse_kernel, steps),
        out_shape=[jax.ShapeDtypeStruct((width, columns), jnp.bfloat16)] * len(steps),
        in_specs=[WHOLE] * 3,
        out_specs=[WHOLE] * len(steps),
        compiler_params=pltpu.CompilerParams(vmem_limit_bytes=16 * MIB),
        cost_estimate=transform_cost(len(steps), width, columns, 3),
    )(*tabs[2:], sums)
    return dict(zip(steps, found))


def pre_kernel(steps, before, after, query_ref, skip_ref, *refs):
    count = len(steps)
    refs = list(refs)
    total = jnp.zeros((query_ref.shape[0], 128), jnp.float32)
    if before:
        refs.pop(0)
        total = refs.pop(0)[...]
    convs, gates, (pre_ref, square_ref) = refs[:count], refs[count : 2 * count], refs[2 * count :]
    width, part = convs[0].shape
    for at_k, k in enumerate(steps):
        start = partner(k) * part if part < query_ref.shape[1] else 0
        for at in range(0, part, 128):
            lanes, cols = pl.ds(at, 128), pl.ds(pl.multiple_of(start + at, 128), 128)
            gated = gates[at_k][:, lanes].astype(jnp.float32)
            conv = convs[at_k][:, lanes].astype(jnp.float32)
            pre = query_ref[:, cols].astype(jnp.float32) * (conv + skip_ref[:, cols] * gated)
            pre_ref[:, cols] = pre
            total = total + pre * pre
    if after:
        square_ref[...] = total
    else:
        square_ref[...] = jnp.sum(total.T, axis=0, keepdims=True)


def together(blocks):
    count, width = len(blocks), blocks[0].shape[0]
    order = jnp.arange(count, dtype=jnp.int32) ^ lax.axis_index("tok")
    stacked = jnp.take(jnp.stack([blocks[k] for k in range(count)]), order, axis=0)
    return {0: stacked.transpose(1, 0, 2).reshape(width, -1)}


def gated_output(query, skip, early, convs, gates):
    width, columns = query.shape
    groups = [early, [k for k in convs if k not in early]]
    if convs[0].shape[1] % 128:
        convs, gates, groups = together(convs), together(gates), [[0]]
    found = []
    for at, steps in enumerate(groups):
        rest = at + 1 < len(groups)
        found = pl.pallas_call(
            functools.partial(pre_kernel, steps, at > 0, rest),
            out_shape=(
                jax.ShapeDtypeStruct((width, columns), jnp.float32),
                jax.ShapeDtypeStruct((width, 128) if rest else (1, width), jnp.float32),
            ),
            in_specs=[WHOLE] * (2 + len(found) + 2 * len(steps)),
            out_specs=(WHOLE, WHOLE),
            input_output_aliases={2: 0} if found else {},
            compiler_params=pltpu.CompilerParams(vmem_limit_bytes=16 * MIB),
            cost_estimate=pl.CostEstimate(
                flops=3 * width * columns, bytes_accessed=5 * width * columns, transcendentals=0
            ),
        )(query, skip, *found, *[convs[k] for k in steps], *[gates[k] for k in steps])
    return found


def scale_kernel(channels, steps, pre_ref, gain_ref, *refs):
    squares, (out_ref, buf, sems) = refs[:-3], refs[-3:]
    width = pre_ref.shape[0]
    rows = width // steps
    total = squares[0][...]
    for square in squares[1:]:
        total = total + square[...]
    scale = lax.rsqrt(total * (1.0 / channels) + 1e-06)
    scale = jnp.broadcast_to(scale, (128, width)).T
    copies = []
    for s in range(steps):
        for at in range(0, pre_ref.shape[1], 128):
            cols = pl.ds(at, 128)
            here = scale[s * rows : (s + 1) * rows, :]
            buf[pl.ds(s * rows, rows), cols] = gain_ref[:, cols] * pre_ref[pl.ds(s * rows, rows), cols] * here
        window = pl.ds(s * rows, rows)
        copies.append(pltpu.make_async_copy(buf.at[window, :], out_ref.at[window, :], sems.at[s]))
        copies[-1].start()
    for copy in copies:
        copy.wait()


def scaled(channels, pre, squares, out_gain):
    width, columns = pre.shape
    steps = 8
    return pl.pallas_call(
        functools.partial(scale_kernel, channels, steps),
        out_shape=jax.ShapeDtypeStruct((width, columns), jnp.float32),
        in_specs=[WHOLE] * (2 + len(squares)),
        out_specs=IN_HBM,
        scratch_shapes=[pltpu.VMEM((width, columns), jnp.float32), pltpu.SemaphoreType.DMA((steps,))],
        compiler_params=pltpu.CompilerParams(vmem_limit_bytes=16 * MIB),
        cost_estimate=pl.CostEstimate(flops=2 * width * columns, bytes_accessed=8 * width * columns, transcendentals=0),
    )(pre, out_gain, *squares)


def local(query, key_in, value_in, filter_store, lag_of_block, skip, out_gain):
    width, columns = query.shape
    count = lax.axis_size("tok")
    part = columns // count
    order = sending_order(count)
    gated_order = order[:-3] + order[-1:] + order[-3:-1]
    own = split(count, order + [0], filter_store)
    own[0], key_in, value_in = lax.optimization_barrier((own[0], key_in, value_in))
    mine = gate(count, key_in, value_in)
    filts = {k: send(own[k], k, count) for k in order}
    gates = {k: send(mine[k], k, count) for k in gated_order}
    filts[0], gates[0] = own[0], mine[0]
    held = gated_order[:2]
    filts[0], *arrived = lax.optimization_barrier((filts[0], *[gates[k] for k in held]))
    gates.update(zip(held, arrived))
    late = gated_order[-2:]
    filt, tabs = filter_spectra(lag_of_block, filts)
    sums = early_products(tabs, filt, {k: gates[k] for k in gates if k not in late})
    sums, found = late_products(order[:1], tabs, filt, sums, {k: gates[k] for k in late})
    found.update(inverses(order[1:] + [0], tabs, sums))
    convs = {k: send(found[k], k, count) for k in order}
    convs[0] = found[0]
    pre, square = gated_output(query, skip[None, :], order[: count // 2] + [0], convs, mine)
    others = lax.axis_size("chan")
    squares = [square] + [
        lax.ppermute(square, "chan", [(d, d ^ step) for d in range(others)]) for step in reversed(range(1, others))
    ]
    return scaled(columns * others, pre, squares, out_gain[None, :])


def solution(mesh):
    in_specs = (
        P("tok", "chan"),
        P("tok", "chan"),
        P("tok", "chan"),
        P("tok", "chan"),
        P(),
        P("chan"),
        P("chan"),
    )
    return jax.shard_map(local, mesh=mesh, in_specs=in_specs, out_specs=P("tok", "chan"), check_vma=False)
```

```python
import functools
import math

import jax
import jax.numpy as jnp
import ml_dtypes
import numpy as np
from jax import lax
from jax.experimental import pallas as pl
from jax.experimental.pallas import tpu as pltpu
from jax.sharding import PartitionSpec as P

MIB = 1024 * 1024
BIG = 48 * MIB
WHOLE = pl.BlockSpec(memory_space=pltpu.VMEM)
IN_HBM = pl.BlockSpec(memory_space=pltpu.HBM)


def split_bf16(table):
    high = table.astype(ml_dtypes.bfloat16)
    low = (table - high.astype(np.float64)).astype(ml_dtypes.bfloat16)
    return high, low


def tables(width):
    freq = np.concatenate([np.arange(0, width, 2), np.arange(1, width, 2)])
    place = np.arange(width)
    steps = ((2 * freq[:, None] + 1) * place[None, :]) % (4 * width)
    angle = math.pi / (2 * width) * steps
    forward = np.concatenate([np.cos(angle), -np.sin(angle)], axis=0)
    inverse = forward.T / width
    return split_bf16(forward) + split_bf16(inverse)


def partner(step):
    return lax.axis_index("tok") ^ step


def send(block, step, count):
    return lax.ppermute(block, "tok", [(d, d ^ step) for d in range(count)])


def sending_order(count):
    half = count // 2
    far = list(range(half, count, 2)) + list(range(half + 1, count, 2))
    near = list(range(2, half)) + [1]
    order = []
    for at in range(half - 1):
        order += [far[at], near[at]]
    return order[:-1] + far[-1:] + order[-1:]


def columns_of(step, part):
    return pl.ds(pl.multiple_of(partner(step) * part, 128), part)


def split_kernel(count, part, filt_ref, *refs):
    outs, sems = refs[:count], refs[count]
    copies = []
    for k in range(count):
        copies.append(pltpu.make_async_copy(filt_ref.at[:, columns_of(k, part)], outs[k], sems.at[k]))
        copies[-1].start()
    for copy in copies:
        copy.wait()


def gate_kernel(count, part, key_ref, value_ref, *refs):
    outs, (key_buf, value_buf, sems) = refs[:count], refs[count:]
    copies = []
    for k in range(count):
        cols = columns_of(k, part)
        copies.append(
            (
                pltpu.make_async_copy(key_ref.at[:, cols], key_buf.at[k], sems.at[0, k]),
                pltpu.make_async_copy(value_ref.at[:, cols], value_buf.at[k], sems.at[1, k]),
            )
        )
        for copy in copies[-1]:
            copy.start()
    for k in range(count):
        for copy in copies[k]:
            copy.wait()
        product = key_buf[k].astype(jnp.float32) * value_buf[k].astype(jnp.float32)
        outs[k][...] = product.astype(jnp.bfloat16)


def pieces(x, count):
    part = x.shape[1] // count
    return [lax.dynamic_slice_in_dim(x, partner(k) * part, part, axis=1) for k in range(count)]


def split(count, filter_store):
    width, columns = filter_store.shape
    part = columns // count
    if part % 128:
        return pieces(filter_store, count)
    return pl.pallas_call(
        functools.partial(split_kernel, count, part),
        out_shape=[jax.ShapeDtypeStruct((width, part), jnp.bfloat16)] * count,
        in_specs=[IN_HBM],
        out_specs=[WHOLE] * count,
        scratch_shapes=[pltpu.SemaphoreType.DMA((count,))],
        compiler_params=pltpu.CompilerParams(vmem_limit_bytes=BIG),
        cost_estimate=pl.CostEstimate(flops=0, bytes_accessed=4 * width * columns, transcendentals=0),
    )(filter_store)


def gate(count, key_in, value_in):
    width, columns = key_in.shape
    part = columns // count
    if part % 128:
        gated = (key_in.astype(jnp.float32) * value_in.astype(jnp.float32)).astype(jnp.bfloat16)
        return pieces(gated, count)
    block = pltpu.VMEM((count, width, part), jnp.bfloat16)
    return pl.pallas_call(
        functools.partial(gate_kernel, count, part),
        out_shape=[jax.ShapeDtypeStruct((width, part), jnp.bfloat16)] * count,
        in_specs=[IN_HBM] * 2,
        out_specs=[WHOLE] * count,
        scratch_shapes=[block, block, pltpu.SemaphoreType.DMA((2, count))],
        compiler_params=pltpu.CompilerParams(vmem_limit_bytes=BIG),
        cost_estimate=pl.CostEstimate(flops=width * columns, bytes_accessed=6 * width * columns, transcendentals=0),
    )(key_in, value_in)


def dot(x, y):
    return jnp.dot(x, y, preferred_element_type=jnp.float32)


def transform(high, low, block):
    return dot(high, block) + dot(low, block)


def filter_kernel(steps, lag_ref, high_ref, low_ref, *refs):
    blocks, out = refs[:-1], refs[-1]
    for k, block in zip(steps, blocks):
        out[lag_ref[partner(k)]] = transform(high_ref[...], low_ref[...], block[...])


def gated_kernel(steps, high_ref, low_ref, *refs):
    blocks, out = refs[:-1], refs[-1]
    for k, block in zip(steps, blocks):
        out[partner(k)] = transform(high_ref[...], low_ref[...], block[...])


def spectra_shape(count, block):
    width, columns = block.shape
    return jax.ShapeDtypeStruct((count, 2 * width, columns), jnp.float32)


def transform_cost(count, block, passes):
    width, columns = block.shape
    return pl.CostEstimate(
        flops=4 * passes * count * width * width * columns,
        bytes_accessed=10 * count * width * columns,
        transcendentals=0,
    )


def filter_spectra(lag_of_block, high, low, blocks):
    steps = list(blocks)
    return pl.pallas_call(
        functools.partial(filter_kernel, steps),
        out_shape=spectra_shape(len(steps), blocks[steps[0]]),
        in_specs=[pl.BlockSpec(memory_space=pltpu.SMEM)] + [WHOLE] * (2 + len(steps)),
        out_specs=WHOLE,
        compiler_params=pltpu.CompilerParams(vmem_limit_bytes=16 * MIB),
        cost_estimate=transform_cost(len(steps), blocks[steps[0]], 2),
    )(lag_of_block, high, low, *[blocks[k] for k in steps])


def gated_spectra(count, high, low, blocks):
    steps = list(blocks)
    return pl.pallas_call(
        functools.partial(gated_kernel, steps),
        out_shape=spectra_shape(count, blocks[steps[0]]),
        in_specs=[WHOLE] * (2 + len(steps)),
        out_specs=WHOLE,
        compiler_params=pltpu.CompilerParams(vmem_limit_bytes=16 * MIB),
        cost_estimate=transform_cost(len(steps), blocks[steps[0]], 2),
    )(high, low, *[blocks[k] for k in steps])


def product_kernel(count, steps, first, fh_ref, fl_ref, ih_ref, il_ref, fs, gs, *refs):
    blocks, (gs, ss), outs = refs[: len(steps)], refs[len(steps) : len(steps) + 2], refs[len(steps) + 2 :]
    width, columns = outs[0].shape
    for k, block in zip(steps, blocks):
        gs[partner(k)] = transform(fh_ref[...], fl_ref[...], block[...])
    lane = min(128, columns)

    def products(row, sign):
        re_rows = pl.ds(pl.multiple_of(row * 8, 8), 8)
        im_rows = pl.ds(pl.multiple_of(row * 8 + width, 8), 8)
        for at in range(0, columns, lane):
            lanes = pl.ds(at, lane)
            f_re = [fs[i, re_rows, lanes] for i in range(count)]
            f_im = [fs[i, im_rows, lanes] for i in range(count)]
            h_re, h_im = [], []
            for i in range(count):
                g_re, g_im = gs[i, re_rows, lanes], gs[i, im_rows, lanes]
                if i == 0:
                    h_re.append(g_re)
                    h_im.append(g_im)
                elif sign > 0:
                    h_re.append(g_re - last_im)
                    h_im.append(g_im + last_re)
                else:
                    h_re.append(g_re + last_im)
                    h_im.append(g_im - last_re)
                last_re, last_im = g_re, g_im
            for j in range(count):
                s_re = f_re[0] * h_re[j] - f_im[0] * h_im[j]
                s_im = f_re[0] * h_im[j] + f_im[0] * h_re[j]
                for i in range(1, j + 1):
                    s_re = s_re + f_re[i] * h_re[j - i] - f_im[i] * h_im[j - i]
                    s_im = s_im + f_re[i] * h_im[j - i] + f_im[i] * h_re[j - i]
                ss[j, re_rows, lanes] = s_re
                ss[j, im_rows, lanes] = s_im

    half = width // 16

    @pl.loop(0, half)
    def _(row):
        products(row, 1)

    @pl.loop(half, 2 * half)
    def _(row):
        products(row, -1)

    for k, out in zip(first, outs):
        out[...] = inverse(ih_ref[...], il_ref[...], ss[partner(k)])


def inverse(table_high, table_low, total):
    high = total.astype(jnp.bfloat16)
    low = (total - high.astype(jnp.float32)).astype(jnp.bfloat16)
    return (dot(table_high, high) + dot(table_high, low) + dot(table_low, high)).astype(jnp.bfloat16)


def products(first, tabs, filt, gated, blocks):
    steps = list(blocks)
    count, twice, columns = gated.shape
    width = twice // 2
    found = pl.pallas_call(
        functools.partial(product_kernel, count, steps, first),
        out_shape=[jax.ShapeDtypeStruct(gated.shape, jnp.float32)] * 2
        + [jax.ShapeDtypeStruct((width, columns), jnp.bfloat16)] * len(first),
        in_specs=[WHOLE] * (6 + len(steps)),
        out_specs=[WHOLE] * (2 + len(first)),
        input_output_aliases={5: 0},
        compiler_params=pltpu.CompilerParams(vmem_limit_bytes=20 * MIB),
        cost_estimate=transform_cost(count, blocks[steps[0]], 7),
    )(*tabs, filt, gated, *[blocks[k] for k in steps])
    return found[1], dict(zip(first, found[2:]))


def inverse_kernel(steps, ih_ref, il_ref, ss, *outs):
    for k, out in zip(steps, outs):
        out[...] = inverse(ih_ref[...], il_ref[...], ss[partner(k)])


def inverses(steps, tabs, sums):
    count, twice, columns = sums.shape
    width = twice // 2
    found = pl.pallas_call(
        functools.partial(inverse_kernel, steps),
        out_shape=[jax.ShapeDtypeStruct((width, columns), jnp.bfloat16)] * len(steps),
        in_specs=[WHOLE] * 3,
        out_specs=[WHOLE] * len(steps),
        compiler_params=pltpu.CompilerParams(vmem_limit_bytes=16 * MIB),
        cost_estimate=transform_cost(len(steps), jax.ShapeDtypeStruct((width, columns), jnp.bfloat16), 3),
    )(*tabs[2:], sums)
    return dict(zip(steps, found))


def pre_kernel(steps, before, after, query_ref, skip_ref, *refs):
    count = len(steps)
    refs = list(refs)
    total = jnp.zeros((query_ref.shape[0], 128), jnp.float32)
    if before:
        refs.pop(0)
        total = refs.pop(0)[...]
    convs, gates, (pre_ref, square_ref) = refs[:count], refs[count : 2 * count], refs[2 * count :]
    width, part = convs[0].shape
    for at_k, k in enumerate(steps):
        start = partner(k) * part if part < query_ref.shape[1] else 0
        for at in range(0, part, 128):
            lanes, cols = pl.ds(at, 128), pl.ds(pl.multiple_of(start + at, 128), 128)
            gated = gates[at_k][:, lanes].astype(jnp.float32)
            conv = convs[at_k][:, lanes].astype(jnp.float32)
            pre = query_ref[:, cols].astype(jnp.float32) * (conv + skip_ref[:, cols] * gated)
            pre_ref[:, cols] = pre
            total = total + pre * pre
    if after:
        square_ref[...] = total
    else:
        square_ref[...] = jnp.sum(total.T, axis=0, keepdims=True)


def together(blocks):
    count, width = len(blocks), blocks[0].shape[0]
    order = jnp.arange(count, dtype=jnp.int32) ^ lax.axis_index("tok")
    stacked = jnp.take(jnp.stack([blocks[k] for k in range(count)]), order, axis=0)
    return {0: stacked.transpose(1, 0, 2).reshape(width, -1)}


def gated_output(query, skip, early, convs, gates):
    width, columns = query.shape
    groups = [early, [k for k in convs if k not in early]]
    if convs[0].shape[1] % 128:
        convs, gates, groups = together(convs), together(gates), [[0]]
    found = []
    for at, steps in enumerate(groups):
        rest = at + 1 < len(groups)
        found = pl.pallas_call(
            functools.partial(pre_kernel, steps, at > 0, rest),
            out_shape=(
                jax.ShapeDtypeStruct((width, columns), jnp.float32),
                jax.ShapeDtypeStruct((width, 128) if rest else (1, width), jnp.float32),
            ),
            in_specs=[WHOLE] * (2 + len(found) + 2 * len(steps)),
            out_specs=(WHOLE, WHOLE),
            input_output_aliases={2: 0} if found else {},
            compiler_params=pltpu.CompilerParams(vmem_limit_bytes=16 * MIB),
            cost_estimate=pl.CostEstimate(
                flops=3 * width * columns, bytes_accessed=5 * width * columns, transcendentals=0
            ),
        )(query, skip, *found, *[convs[k] for k in steps], *[gates[k] for k in steps])
    return found


def scale_kernel(channels, steps, pre_ref, gain_ref, *refs):
    squares, (out_ref, buf, sems) = refs[:-3], refs[-3:]
    width = pre_ref.shape[0]
    rows = width // steps
    total = squares[0][...]
    for square in squares[1:]:
        total = total + square[...]
    scale = lax.rsqrt(total * (1.0 / channels) + 1e-06)
    scale = jnp.broadcast_to(scale, (128, width)).T
    copies = []
    for s in range(steps):
        for at in range(0, pre_ref.shape[1], 128):
            cols = pl.ds(at, 128)
            here = scale[s * rows : (s + 1) * rows, :]
            buf[pl.ds(s * rows, rows), cols] = gain_ref[:, cols] * pre_ref[pl.ds(s * rows, rows), cols] * here
        window = pl.ds(s * rows, rows)
        copies.append(pltpu.make_async_copy(buf.at[window, :], out_ref.at[window, :], sems.at[s]))
        copies[-1].start()
    for copy in copies:
        copy.wait()


def scaled(channels, pre, squares, out_gain):
    width, columns = pre.shape
    steps = 8
    return pl.pallas_call(
        functools.partial(scale_kernel, channels, steps),
        out_shape=jax.ShapeDtypeStruct((width, columns), jnp.float32),
        in_specs=[WHOLE] * (2 + len(squares)),
        out_specs=IN_HBM,
        scratch_shapes=[pltpu.VMEM((width, columns), jnp.float32), pltpu.SemaphoreType.DMA((steps,))],
        compiler_params=pltpu.CompilerParams(vmem_limit_bytes=16 * MIB),
        cost_estimate=pl.CostEstimate(flops=2 * width * columns, bytes_accessed=8 * width * columns, transcendentals=0),
    )(pre, out_gain, *squares)


def local(query, key_in, value_in, filter_store, lag_of_block, skip, out_gain):
    width, columns = query.shape
    count = lax.axis_size("tok")
    tabs = [jnp.asarray(t) for t in tables(width)]
    own = split(count, filter_store)
    held, key_in, value_in = lax.optimization_barrier((own[0], key_in, value_in))
    mine = gate(count, key_in, value_in)
    order = sending_order(count)
    filts, gates, convs = {}, {}, {}
    for k in order:
        filts[k] = send(own[k], k, count)
    for k in order:
        gates[k] = send(mine[k], k, count)
    filts[0], gates[0] = held, mine[0]
    filt = filter_spectra(lag_of_block, *tabs[:2], filts)
    early = order[: count // 2] + [0]
    gated = gated_spectra(count, *tabs[:2], {k: gates[k] for k in early})
    first = order[:1]
    sums, found = products(first, tabs, filt, gated, {k: gates[k] for k in gates if k not in early})
    found.update(inverses(order[1:] + [0], tabs, sums))
    for k in order:
        convs[k] = send(found[k], k, count)
    convs[0] = found[0]
    pre, square = gated_output(query, skip[None, :], order[: count // 2] + [0], convs, mine)
    others = lax.axis_size("chan")
    squares = [square] + [
        lax.ppermute(square, "chan", [(d, d ^ step) for d in range(others)]) for step in reversed(range(1, others))
    ]
    return scaled(columns * others, pre, squares, out_gain[None, :])


def solution(mesh):
    in_specs = (
        P("tok", "chan"),
        P("tok", "chan"),
        P("tok", "chan"),
        P("tok", "chan"),
        P(),
        P("chan"),
        P("chan"),
    )
    return jax.shard_map(local, mesh=mesh, in_specs=in_specs, out_specs=P("tok", "chan"), check_vma=False)
```

```python
import functools
import math

import jax
import jax.numpy as jnp
import ml_dtypes
import numpy as np
from jax import lax
from jax.experimental import pallas as pl
from jax.experimental.pallas import tpu as pltpu
from jax.sharding import PartitionSpec as P

MIB = 1024 * 1024
BIG = 48 * MIB
WHOLE = pl.BlockSpec(memory_space=pltpu.VMEM)
IN_HBM = pl.BlockSpec(memory_space=pltpu.HBM)


def split_bf16(table):
    high = table.astype(ml_dtypes.bfloat16)
    low = (table - high.astype(np.float64)).astype(ml_dtypes.bfloat16)
    return high, low


def tables(width):
    freq = np.concatenate([np.arange(0, width, 2), np.arange(1, width, 2)])
    place = np.arange(width)
    steps = ((2 * freq[:, None] + 1) * place[None, :]) % (4 * width)
    angle = math.pi / (2 * width) * steps
    forward = np.concatenate([np.cos(angle), -np.sin(angle)], axis=0)
    inverse = forward.T / width
    return split_bf16(forward) + split_bf16(inverse)


def partner(step):
    return lax.axis_index("tok") ^ step


def send(block, step, count):
    return lax.ppermute(block, "tok", [(d, d ^ step) for d in range(count)])


def sending_order(count):
    half = count // 2
    far = list(range(half, count, 2)) + list(range(half + 1, count, 2))
    near = list(range(2, half)) + [1]
    order = []
    for at in range(half - 1):
        order += [far[at], near[at]]
    return order[:-1] + far[-1:] + order[-1:]


def columns_of(step, part):
    return pl.ds(pl.multiple_of(partner(step) * part, 128), part)


def split_kernel(count, part, filt_ref, *refs):
    outs, sems = refs[:count], refs[count]
    copies = []
    for k in range(count):
        copies.append(pltpu.make_async_copy(filt_ref.at[:, columns_of(k, part)], outs[k], sems.at[k]))
        copies[-1].start()
    for copy in copies:
        copy.wait()


def gate_kernel(count, part, key_ref, value_ref, *refs):
    outs, (key_buf, value_buf, sems) = refs[:count], refs[count:]
    copies = []
    for k in range(count):
        cols = columns_of(k, part)
        copies.append(
            (
                pltpu.make_async_copy(key_ref.at[:, cols], key_buf.at[k], sems.at[0, k]),
                pltpu.make_async_copy(value_ref.at[:, cols], value_buf.at[k], sems.at[1, k]),
            )
        )
        for copy in copies[-1]:
            copy.start()
    for k in range(count):
        for copy in copies[k]:
            copy.wait()
        product = key_buf[k].astype(jnp.float32) * value_buf[k].astype(jnp.float32)
        outs[k][...] = product.astype(jnp.bfloat16)


def pieces(x, count):
    part = x.shape[1] // count
    return [lax.dynamic_slice_in_dim(x, partner(k) * part, part, axis=1) for k in range(count)]


def split(count, filter_store):
    width, columns = filter_store.shape
    part = columns // count
    if part % 128:
        return pieces(filter_store, count)
    return pl.pallas_call(
        functools.partial(split_kernel, count, part),
        out_shape=[jax.ShapeDtypeStruct((width, part), jnp.bfloat16)] * count,
        in_specs=[IN_HBM],
        out_specs=[WHOLE] * count,
        scratch_shapes=[pltpu.SemaphoreType.DMA((count,))],
        compiler_params=pltpu.CompilerParams(vmem_limit_bytes=BIG),
        cost_estimate=pl.CostEstimate(flops=0, bytes_accessed=4 * width * columns, transcendentals=0),
    )(filter_store)


def gate(count, key_in, value_in):
    width, columns = key_in.shape
    part = columns // count
    if part % 128:
        gated = (key_in.astype(jnp.float32) * value_in.astype(jnp.float32)).astype(jnp.bfloat16)
        return pieces(gated, count)
    block = pltpu.VMEM((count, width, part), jnp.bfloat16)
    return pl.pallas_call(
        functools.partial(gate_kernel, count, part),
        out_shape=[jax.ShapeDtypeStruct((width, part), jnp.bfloat16)] * count,
        in_specs=[IN_HBM] * 2,
        out_specs=[WHOLE] * count,
        scratch_shapes=[block, block, pltpu.SemaphoreType.DMA((2, count))],
        compiler_params=pltpu.CompilerParams(vmem_limit_bytes=BIG),
        cost_estimate=pl.CostEstimate(flops=width * columns, bytes_accessed=6 * width * columns, transcendentals=0),
    )(key_in, value_in)


def dot(x, y):
    return jnp.dot(x, y, preferred_element_type=jnp.float32)


def transform(high, low, block):
    return dot(high, block) + dot(low, block)


def transform_cost(count, width, columns, passes):
    return pl.CostEstimate(
        flops=4 * passes * count * width * width * columns,
        bytes_accessed=10 * count * width * columns,
        transcendentals=0,
    )


def tiles(width, columns, tile):
    half = width // 16
    lane = min(128, columns)

    def run(row, sign):
        re_rows = pl.ds(pl.multiple_of(row * 8, 8), 8)
        im_rows = pl.ds(pl.multiple_of(row * 8 + width, 8), 8)
        for at in range(0, columns, lane):
            tile(re_rows, im_rows, pl.ds(at, lane), sign)

    @pl.loop(0, half)
    def _(row):
        run(row, 1)

    @pl.loop(half, 2 * half)
    def _(row):
        run(row, -1)


def gated_kernel(steps, high_ref, low_ref, *refs):
    blocks, out = refs[:-1], refs[-1]
    for k in range(out.shape[0]):
        if k not in steps:
            out[partner(k)] = jnp.zeros(out.shape[1:], jnp.float32)
    for k, block in zip(steps, blocks):
        out[partner(k)] = transform(high_ref[...], low_ref[...], block[...])


def gated_spectra(count, high, low, blocks):
    steps = list(blocks)
    width, columns = blocks[0].shape
    return pl.pallas_call(
        functools.partial(gated_kernel, steps),
        out_shape=jax.ShapeDtypeStruct((count, 2 * width, columns), jnp.float32),
        in_specs=[WHOLE] * (2 + len(steps)),
        out_specs=WHOLE,
        compiler_params=pltpu.CompilerParams(vmem_limit_bytes=16 * MIB),
        cost_estimate=transform_cost(len(steps), width, columns, 2),
    )(high, low, *[blocks[k] for k in steps])


def early_kernel(count, steps, lag_ref, high_ref, low_ref, *refs):
    blocks, (gs, fs, ss) = refs[:count], refs[count:]
    width, columns = gs.shape[1] // 2, gs.shape[2]
    for at, (k, block) in enumerate(zip(steps, blocks)):
        fs[at] = jnp.zeros(fs.shape[1:], jnp.float32)
        fs[count + lag_ref[partner(k)]] = transform(high_ref[...], low_ref[...], block[...])

    def tile(re_rows, im_rows, lanes, sign):
        f = [(fs[count + i, re_rows, lanes], fs[count + i, im_rows, lanes]) for i in range(count)]
        h, last = [], None
        for i in range(count):
            here = (gs[i, re_rows, lanes], gs[i, im_rows, lanes])
            if last is None:
                h.append(here)
            elif sign > 0:
                h.append((here[0] - last[1], here[1] + last[0]))
            else:
                h.append((here[0] + last[1], here[1] - last[0]))
            last = here
        for j in range(count):
            s_re = f[0][0] * h[j][0] - f[0][1] * h[j][1]
            s_im = f[0][0] * h[j][1] + f[0][1] * h[j][0]
            for i in range(1, j + 1):
                s_re = s_re + f[i][0] * h[j - i][0] - f[i][1] * h[j - i][1]
                s_im = s_im + f[i][0] * h[j - i][1] + f[i][1] * h[j - i][0]
            ss[j, re_rows, lanes] = s_re
            ss[j, im_rows, lanes] = s_im

    tiles(width, columns, tile)


def early_products(lag_of_block, high, low, blocks, gated):
    steps = list(blocks)
    count, twice, columns = gated.shape
    return pl.pallas_call(
        functools.partial(early_kernel, count, steps),
        out_shape=[
            jax.ShapeDtypeStruct((2 * count, twice, columns), jnp.float32),
            jax.ShapeDtypeStruct(gated.shape, jnp.float32),
        ],
        in_specs=[pl.BlockSpec(memory_space=pltpu.SMEM)] + [WHOLE] * (3 + count),
        out_specs=[WHOLE, WHOLE],
        compiler_params=pltpu.CompilerParams(vmem_limit_bytes=16 * MIB),
        cost_estimate=transform_cost(count, twice // 2, columns, 2),
    )(lag_of_block, high, low, *[blocks[k] for k in steps], gated)


def inverse(table_high, table_low, total):
    high = total.astype(jnp.bfloat16)
    low = (total - high.astype(jnp.float32)).astype(jnp.bfloat16)
    return (dot(table_high, high) + dot(table_high, low) + dot(table_low, high)).astype(jnp.bfloat16)


def late_kernel(count, steps, first, fh_ref, fl_ref, ih_ref, il_ref, fs, sums, *refs):
    blocks, ss, outs, gs = refs[: len(steps)], refs[len(steps)], refs[len(steps) + 1 : -1], refs[-1]
    width, columns = blocks[0].shape
    for at, block in enumerate(blocks):
        gs[at] = transform(fh_ref[...], fl_ref[...], block[...])
    shifted = [fs.at[pl.ds(count - partner(k), count)] for k in steps]

    def tile(re_rows, im_rows, lanes, sign):
        def both(ref, i):
            return ref[i, re_rows, lanes], ref[i, im_rows, lanes]

        g = [both(gs, at) for at in range(len(steps))]
        f = [[both(view, j) for view in shifted] for j in range(count)]
        s = [both(ss, j) for j in range(count)]
        d = []
        for j in range(count):
            d_re = d_im = None
            for (f_re, f_im), (g_re, g_im) in zip(f[j], g):
                p_re, p_im = f_re * g_re - f_im * g_im, f_re * g_im + f_im * g_re
                d_re, d_im = (p_re, p_im) if d_re is None else (d_re + p_re, d_im + p_im)
            d.append((d_re, d_im))
        for j in range(count):
            s_re, s_im = s[j][0] + d[j][0], s[j][1] + d[j][1]
            if j and sign > 0:
                s_re, s_im = s_re - d[j - 1][1], s_im + d[j - 1][0]
            elif j:
                s_re, s_im = s_re + d[j - 1][1], s_im - d[j - 1][0]
            ss[j, re_rows, lanes] = s_re
            ss[j, im_rows, lanes] = s_im

    tiles(width, columns, tile)
    for k, out in zip(first, outs):
        out[...] = inverse(ih_ref[...], il_ref[...], ss[partner(k)])


def late_products(first, tabs, filt, sums, blocks):
    steps = list(blocks)
    count, twice, columns = sums.shape
    width = twice // 2
    found = pl.pallas_call(
        functools.partial(late_kernel, count, steps, first),
        out_shape=[jax.ShapeDtypeStruct(sums.shape, jnp.float32)]
        + [jax.ShapeDtypeStruct((width, columns), jnp.bfloat16)] * len(first),
        in_specs=[WHOLE] * (6 + len(steps)),
        out_specs=[WHOLE] * (1 + len(first)),
        scratch_shapes=[pltpu.VMEM((len(steps), twice, columns), jnp.float32)],
        input_output_aliases={5: 0},
        compiler_params=pltpu.CompilerParams(vmem_limit_bytes=16 * MIB),
        cost_estimate=transform_cost(count, width, columns, 3),
    )(*tabs, filt, sums, *[blocks[k] for k in steps])
    return found[0], dict(zip(first, found[1:]))


def inverse_kernel(steps, ih_ref, il_ref, ss, *outs):
    for k, out in zip(steps, outs):
        out[...] = inverse(ih_ref[...], il_ref[...], ss[partner(k)])


def inverses(steps, tabs, sums):
    count, twice, columns = sums.shape
    width = twice // 2
    found = pl.pallas_call(
        functools.partial(inverse_kernel, steps),
        out_shape=[jax.ShapeDtypeStruct((width, columns), jnp.bfloat16)] * len(steps),
        in_specs=[WHOLE] * 3,
        out_specs=[WHOLE] * len(steps),
        compiler_params=pltpu.CompilerParams(vmem_limit_bytes=16 * MIB),
        cost_estimate=transform_cost(len(steps), width, columns, 3),
    )(*tabs[2:], sums)
    return dict(zip(steps, found))


def pre_kernel(steps, before, after, query_ref, skip_ref, *refs):
    count = len(steps)
    refs = list(refs)
    total = jnp.zeros((query_ref.shape[0], 128), jnp.float32)
    if before:
        refs.pop(0)
        total = refs.pop(0)[...]
    convs, gates, (pre_ref, square_ref) = refs[:count], refs[count : 2 * count], refs[2 * count :]
    width, part = convs[0].shape
    for at_k, k in enumerate(steps):
        start = partner(k) * part if part < query_ref.shape[1] else 0
        for at in range(0, part, 128):
            lanes, cols = pl.ds(at, 128), pl.ds(pl.multiple_of(start + at, 128), 128)
            gated = gates[at_k][:, lanes].astype(jnp.float32)
            conv = convs[at_k][:, lanes].astype(jnp.float32)
            pre = query_ref[:, cols].astype(jnp.float32) * (conv + skip_ref[:, cols] * gated)
            pre_ref[:, cols] = pre
            total = total + pre * pre
    if after:
        square_ref[...] = total
    else:
        square_ref[...] = jnp.sum(total.T, axis=0, keepdims=True)


def together(blocks):
    count, width = len(blocks), blocks[0].shape[0]
    order = jnp.arange(count, dtype=jnp.int32) ^ lax.axis_index("tok")
    stacked = jnp.take(jnp.stack([blocks[k] for k in range(count)]), order, axis=0)
    return {0: stacked.transpose(1, 0, 2).reshape(width, -1)}


def gated_output(query, skip, early, convs, gates):
    width, columns = query.shape
    groups = [early, [k for k in convs if k not in early]]
    if convs[0].shape[1] % 128:
        convs, gates, groups = together(convs), together(gates), [[0]]
    found = []
    for at, steps in enumerate(groups):
        rest = at + 1 < len(groups)
        found = pl.pallas_call(
            functools.partial(pre_kernel, steps, at > 0, rest),
            out_shape=(
                jax.ShapeDtypeStruct((width, columns), jnp.float32),
                jax.ShapeDtypeStruct((width, 128) if rest else (1, width), jnp.float32),
            ),
            in_specs=[WHOLE] * (2 + len(found) + 2 * len(steps)),
            out_specs=(WHOLE, WHOLE),
            input_output_aliases={2: 0} if found else {},
            compiler_params=pltpu.CompilerParams(vmem_limit_bytes=16 * MIB),
            cost_estimate=pl.CostEstimate(
                flops=3 * width * columns, bytes_accessed=5 * width * columns, transcendentals=0
            ),
        )(query, skip, *found, *[convs[k] for k in steps], *[gates[k] for k in steps])
    return found


def scale_kernel(channels, steps, pre_ref, gain_ref, *refs):
    squares, (out_ref, buf, sems) = refs[:-3], refs[-3:]
    width = pre_ref.shape[0]
    rows = width // steps
    total = squares[0][...]
    for square in squares[1:]:
        total = total + square[...]
    scale = lax.rsqrt(total * (1.0 / channels) + 1e-06)
    scale = jnp.broadcast_to(scale, (128, width)).T
    copies = []
    for s in range(steps):
        for at in range(0, pre_ref.shape[1], 128):
            cols = pl.ds(at, 128)
            here = scale[s * rows : (s + 1) * rows, :]
            buf[pl.ds(s * rows, rows), cols] = gain_ref[:, cols] * pre_ref[pl.ds(s * rows, rows), cols] * here
        window = pl.ds(s * rows, rows)
        copies.append(pltpu.make_async_copy(buf.at[window, :], out_ref.at[window, :], sems.at[s]))
        copies[-1].start()
    for copy in copies:
        copy.wait()


def scaled(channels, pre, squares, out_gain):
    width, columns = pre.shape
    steps = 8
    return pl.pallas_call(
        functools.partial(scale_kernel, channels, steps),
        out_shape=jax.ShapeDtypeStruct((width, columns), jnp.float32),
        in_specs=[WHOLE] * (2 + len(squares)),
        out_specs=IN_HBM,
        scratch_shapes=[pltpu.VMEM((width, columns), jnp.float32), pltpu.SemaphoreType.DMA((steps,))],
        compiler_params=pltpu.CompilerParams(vmem_limit_bytes=16 * MIB),
        cost_estimate=pl.CostEstimate(flops=2 * width * columns, bytes_accessed=8 * width * columns, transcendentals=0),
    )(pre, out_gain, *squares)


def local(query, key_in, value_in, filter_store, lag_of_block, skip, out_gain):
    width, columns = query.shape
    count = lax.axis_size("tok")
    tabs = [jnp.asarray(t) for t in tables(width)]
    own = split(count, filter_store)
    order = sending_order(count)
    gates, convs = {}, {}
    filts = {k: send(own[k], k, count) for k in order}
    filts[order[0]], key_in, value_in = lax.optimization_barrier((filts[order[0]], key_in, value_in))
    mine = gate(count, key_in, value_in)
    for k in order:
        gates[k] = send(mine[k], k, count)
    filts[0], gates[0] = own[0], mine[0]
    early = order[: count // 2] + [0]
    gated = gated_spectra(count, *tabs[:2], {k: gates[k] for k in early})
    filt, sums = early_products(lag_of_block, *tabs[:2], filts, gated)
    sums, found = late_products(order[:1], tabs, filt, sums, {k: gates[k] for k in gates if k not in early})
    found.update(inverses(order[1:] + [0], tabs, sums))
    for at, k in enumerate(order):
        block = found[k]
        if at == 6:
            block, convs[order[0]] = lax.optimization_barrier((block, convs[order[0]]))
        convs[k] = send(block, k, count)
    convs[0] = found[0]
    pre, square = gated_output(query, skip[None, :], order[: count // 2] + [0], convs, mine)
    others = lax.axis_size("chan")
    squares = [square] + [
        lax.ppermute(square, "chan", [(d, d ^ step) for d in range(others)]) for step in reversed(range(1, others))
    ]
    return scaled(columns * others, pre, squares, out_gain[None, :])


def solution(mesh):
    in_specs = (
        P("tok", "chan"),
        P("tok", "chan"),
        P("tok", "chan"),
        P("tok", "chan"),
        P(),
        P("chan"),
        P("chan"),
    )
    return jax.shard_map(local, mesh=mesh, in_specs=in_specs, out_specs=P("tok", "chan"), check_vma=False)
```

```python
import functools
import math

import jax
import jax.numpy as jnp
import ml_dtypes
import numpy as np
from jax import lax
from jax.experimental import pallas as pl
from jax.experimental.pallas import tpu as pltpu
from jax.sharding import PartitionSpec as P

MIB = 1024 * 1024
BIG = 48 * MIB
WHOLE = pl.BlockSpec(memory_space=pltpu.VMEM)
IN_HBM = pl.BlockSpec(memory_space=pltpu.HBM)


def split_bf16(table):
    high = table.astype(ml_dtypes.bfloat16)
    low = (table - high.astype(np.float64)).astype(ml_dtypes.bfloat16)
    return high, low


def tables(width):
    freq = np.concatenate([np.arange(0, width, 2), np.arange(1, width, 2)])
    place = np.arange(width)
    steps = ((2 * freq[:, None] + 1) * place[None, :]) % (4 * width)
    angle = math.pi / (2 * width) * steps
    forward = np.concatenate([np.cos(angle), -np.sin(angle)], axis=0)
    inverse = forward.T / width
    return split_bf16(forward) + split_bf16(inverse)


def partner(step):
    return lax.axis_index("tok") ^ step


def send(block, step, count):
    return lax.ppermute(block, "tok", [(d, d ^ step) for d in range(count)])


def sending_order(count):
    half = count // 2
    far = list(range(half, count, 2)) + list(range(half + 1, count, 2))
    near = list(range(2, half)) + [1]
    order = []
    for at in range(half - 1):
        order += [far[at], near[at]]
    return order[:-1] + far[-1:] + order[-1:]


def columns_of(step, part):
    return pl.ds(pl.multiple_of(partner(step) * part, 128), part)


def split_kernel(count, part, filt_ref, *refs):
    outs, sems = refs[:count], refs[count]
    copies = []
    for k in range(count):
        copies.append(pltpu.make_async_copy(filt_ref.at[:, columns_of(k, part)], outs[k], sems.at[k]))
        copies[-1].start()
    for copy in copies:
        copy.wait()


def gate_kernel(count, part, key_ref, value_ref, *refs):
    outs, (key_buf, value_buf, sems) = refs[:count], refs[count:]
    copies = []
    for k in range(count):
        cols = columns_of(k, part)
        copies.append(
            (
                pltpu.make_async_copy(key_ref.at[:, cols], key_buf.at[k], sems.at[0, k]),
                pltpu.make_async_copy(value_ref.at[:, cols], value_buf.at[k], sems.at[1, k]),
            )
        )
        for copy in copies[-1]:
            copy.start()
    for k in range(count):
        for copy in copies[k]:
            copy.wait()
        product = key_buf[k].astype(jnp.float32) * value_buf[k].astype(jnp.float32)
        outs[k][...] = product.astype(jnp.bfloat16)


def pieces(x, count):
    part = x.shape[1] // count
    return [lax.dynamic_slice_in_dim(x, partner(k) * part, part, axis=1) for k in range(count)]


def split(count, filter_store):
    width, columns = filter_store.shape
    part = columns // count
    if part % 128:
        return pieces(filter_store, count)
    return pl.pallas_call(
        functools.partial(split_kernel, count, part),
        out_shape=[jax.ShapeDtypeStruct((width, part), jnp.bfloat16)] * count,
        in_specs=[IN_HBM],
        out_specs=[WHOLE] * count,
        scratch_shapes=[pltpu.SemaphoreType.DMA((count,))],
        compiler_params=pltpu.CompilerParams(vmem_limit_bytes=BIG),
        cost_estimate=pl.CostEstimate(flops=0, bytes_accessed=4 * width * columns, transcendentals=0),
    )(filter_store)


def gate(count, key_in, value_in):
    width, columns = key_in.shape
    part = columns // count
    if part % 128:
        gated = (key_in.astype(jnp.float32) * value_in.astype(jnp.float32)).astype(jnp.bfloat16)
        return pieces(gated, count)
    block = pltpu.VMEM((count, width, part), jnp.bfloat16)
    return pl.pallas_call(
        functools.partial(gate_kernel, count, part),
        out_shape=[jax.ShapeDtypeStruct((width, part), jnp.bfloat16)] * count,
        in_specs=[IN_HBM] * 2,
        out_specs=[WHOLE] * count,
        scratch_shapes=[block, block, pltpu.SemaphoreType.DMA((2, count))],
        compiler_params=pltpu.CompilerParams(vmem_limit_bytes=BIG),
        cost_estimate=pl.CostEstimate(flops=width * columns, bytes_accessed=6 * width * columns, transcendentals=0),
    )(key_in, value_in)


def dot(x, y):
    return jnp.dot(x, y, preferred_element_type=jnp.float32)


def transform(high, low, block):
    return dot(high, block) + dot(low, block)


def filter_kernel(steps, lag_ref, high_ref, low_ref, *refs):
    blocks, out = refs[:-1], refs[-1]
    for k, block in zip(steps, blocks):
        out[lag_ref[partner(k)]] = transform(high_ref[...], low_ref[...], block[...])


def gated_kernel(steps, high_ref, low_ref, *refs):
    blocks, out = refs[:-1], refs[-1]
    for k, block in zip(steps, blocks):
        out[partner(k)] = transform(high_ref[...], low_ref[...], block[...])


def spectra_shape(count, block):
    width, columns = block.shape
    return jax.ShapeDtypeStruct((count, 2 * width, columns), jnp.float32)


def transform_cost(count, block, passes):
    width, columns = block.shape
    return pl.CostEstimate(
        flops=4 * passes * count * width * width * columns,
        bytes_accessed=10 * count * width * columns,
        transcendentals=0,
    )


def filter_spectra(lag_of_block, high, low, blocks):
    steps = list(blocks)
    return pl.pallas_call(
        functools.partial(filter_kernel, steps),
        out_shape=spectra_shape(len(steps), blocks[steps[0]]),
        in_specs=[pl.BlockSpec(memory_space=pltpu.SMEM)] + [WHOLE] * (2 + len(steps)),
        out_specs=WHOLE,
        compiler_params=pltpu.CompilerParams(vmem_limit_bytes=16 * MIB),
        cost_estimate=transform_cost(len(steps), blocks[steps[0]], 2),
    )(lag_of_block, high, low, *[blocks[k] for k in steps])


def gated_spectra(count, high, low, blocks):
    steps = list(blocks)
    return pl.pallas_call(
        functools.partial(gated_kernel, steps),
        out_shape=spectra_shape(count, blocks[steps[0]]),
        in_specs=[WHOLE] * (2 + len(steps)),
        out_specs=WHOLE,
        compiler_params=pltpu.CompilerParams(vmem_limit_bytes=16 * MIB),
        cost_estimate=transform_cost(len(steps), blocks[steps[0]], 2),
    )(high, low, *[blocks[k] for k in steps])


def product_kernel(count, steps, first, fh_ref, fl_ref, ih_ref, il_ref, fs, gs, *refs):
    blocks, (gs, ss), outs = refs[: len(steps)], refs[len(steps) : len(steps) + 2], refs[len(steps) + 2 :]
    width, columns = outs[0].shape
    for k, block in zip(steps, blocks):
        gs[partner(k)] = transform(fh_ref[...], fl_ref[...], block[...])
    lane = min(128, columns)

    def products(row, sign):
        re_rows = pl.ds(pl.multiple_of(row * 8, 8), 8)
        im_rows = pl.ds(pl.multiple_of(row * 8 + width, 8), 8)
        for at in range(0, columns, lane):
            lanes = pl.ds(at, lane)
            f_re = [fs[i, re_rows, lanes] for i in range(count)]
            f_im = [fs[i, im_rows, lanes] for i in range(count)]
            h_re, h_im = [], []
            for i in range(count):
                g_re, g_im = gs[i, re_rows, lanes], gs[i, im_rows, lanes]
                if i == 0:
                    h_re.append(g_re)
                    h_im.append(g_im)
                elif sign > 0:
                    h_re.append(g_re - last_im)
                    h_im.append(g_im + last_re)
                else:
                    h_re.append(g_re + last_im)
                    h_im.append(g_im - last_re)
                last_re, last_im = g_re, g_im
            for j in range(count):
                s_re = f_re[0] * h_re[j] - f_im[0] * h_im[j]
                s_im = f_re[0] * h_im[j] + f_im[0] * h_re[j]
                for i in range(1, j + 1):
                    s_re = s_re + f_re[i] * h_re[j - i] - f_im[i] * h_im[j - i]
                    s_im = s_im + f_re[i] * h_im[j - i] + f_im[i] * h_re[j - i]
                ss[j, re_rows, lanes] = s_re
                ss[j, im_rows, lanes] = s_im

    half = width // 16

    @pl.loop(0, half)
    def _(row):
        products(row, 1)

    @pl.loop(half, 2 * half)
    def _(row):
        products(row, -1)

    for k, out in zip(first, outs):
        out[...] = inverse(ih_ref[...], il_ref[...], ss[partner(k)])


def inverse(table_high, table_low, total):
    high = total.astype(jnp.bfloat16)
    low = (total - high.astype(jnp.float32)).astype(jnp.bfloat16)
    return (dot(table_high, high) + dot(table_high, low) + dot(table_low, high)).astype(jnp.bfloat16)


def products(first, tabs, filt, gated, blocks):
    steps = list(blocks)
    count, twice, columns = gated.shape
    width = twice // 2
    found = pl.pallas_call(
        functools.partial(product_kernel, count, steps, first),
        out_shape=[jax.ShapeDtypeStruct(gated.shape, jnp.float32)] * 2
        + [jax.ShapeDtypeStruct((width, columns), jnp.bfloat16)] * len(first),
        in_specs=[WHOLE] * (6 + len(steps)),
        out_specs=[WHOLE] * (2 + len(first)),
        input_output_aliases={5: 0},
        compiler_params=pltpu.CompilerParams(vmem_limit_bytes=20 * MIB),
        cost_estimate=transform_cost(count, blocks[steps[0]], 7),
    )(*tabs, filt, gated, *[blocks[k] for k in steps])
    return found[1], dict(zip(first, found[2:]))


def inverse_kernel(steps, ih_ref, il_ref, ss, *outs):
    for k, out in zip(steps, outs):
        out[...] = inverse(ih_ref[...], il_ref[...], ss[partner(k)])


def inverses(steps, tabs, sums):
    count, twice, columns = sums.shape
    width = twice // 2
    found = pl.pallas_call(
        functools.partial(inverse_kernel, steps),
        out_shape=[jax.ShapeDtypeStruct((width, columns), jnp.bfloat16)] * len(steps),
        in_specs=[WHOLE] * 3,
        out_specs=[WHOLE] * len(steps),
        compiler_params=pltpu.CompilerParams(vmem_limit_bytes=16 * MIB),
        cost_estimate=transform_cost(len(steps), jax.ShapeDtypeStruct((width, columns), jnp.bfloat16), 3),
    )(*tabs[2:], sums)
    return dict(zip(steps, found))


def pre_kernel(steps, before, after, query_ref, skip_ref, *refs):
    count = len(steps)
    refs = list(refs)
    total = jnp.zeros((query_ref.shape[0], 128), jnp.float32)
    if before:
        refs.pop(0)
        total = refs.pop(0)[...]
    convs, gates, (pre_ref, square_ref) = refs[:count], refs[count : 2 * count], refs[2 * count :]
    width, part = convs[0].shape
    for at_k, k in enumerate(steps):
        start = partner(k) * part if part < query_ref.shape[1] else 0
        for at in range(0, part, 128):
            lanes, cols = pl.ds(at, 128), pl.ds(pl.multiple_of(start + at, 128), 128)
            gated = gates[at_k][:, lanes].astype(jnp.float32)
            conv = convs[at_k][:, lanes].astype(jnp.float32)
            pre = query_ref[:, cols].astype(jnp.float32) * (conv + skip_ref[:, cols] * gated)
            pre_ref[:, cols] = pre
            total = total + pre * pre
    if after:
        square_ref[...] = total
    else:
        square_ref[...] = jnp.sum(total.T, axis=0, keepdims=True)


def together(blocks):
    count, width = len(blocks), blocks[0].shape[0]
    order = jnp.arange(count, dtype=jnp.int32) ^ lax.axis_index("tok")
    stacked = jnp.take(jnp.stack([blocks[k] for k in range(count)]), order, axis=0)
    return {0: stacked.transpose(1, 0, 2).reshape(width, -1)}


def gated_output(query, skip, early, convs, gates):
    width, columns = query.shape
    groups = [early, [k for k in convs if k not in early]]
    if convs[0].shape[1] % 128:
        convs, gates, groups = together(convs), together(gates), [[0]]
    found = []
    for at, steps in enumerate(groups):
        rest = at + 1 < len(groups)
        found = pl.pallas_call(
            functools.partial(pre_kernel, steps, at > 0, rest),
            out_shape=(
                jax.ShapeDtypeStruct((width, columns), jnp.float32),
                jax.ShapeDtypeStruct((width, 128) if rest else (1, width), jnp.float32),
            ),
            in_specs=[WHOLE] * (2 + len(found) + 2 * len(steps)),
            out_specs=(WHOLE, WHOLE),
            input_output_aliases={2: 0} if found else {},
            compiler_params=pltpu.CompilerParams(vmem_limit_bytes=16 * MIB),
            cost_estimate=pl.CostEstimate(
                flops=3 * width * columns, bytes_accessed=5 * width * columns, transcendentals=0
            ),
        )(query, skip, *found, *[convs[k] for k in steps], *[gates[k] for k in steps])
    return found


def scale_kernel(channels, steps, pre_ref, gain_ref, *refs):
    squares, (out_ref, buf, sems) = refs[:-3], refs[-3:]
    width = pre_ref.shape[0]
    rows = width // steps
    total = squares[0][...]
    for square in squares[1:]:
        total = total + square[...]
    scale = lax.rsqrt(total * (1.0 / channels) + 1e-06)
    scale = jnp.broadcast_to(scale, (128, width)).T
    copies = []
    for s in range(steps):
        for at in range(0, pre_ref.shape[1], 128):
            cols = pl.ds(at, 128)
            here = scale[s * rows : (s + 1) * rows, :]
            buf[pl.ds(s * rows, rows), cols] = gain_ref[:, cols] * pre_ref[pl.ds(s * rows, rows), cols] * here
        window = pl.ds(s * rows, rows)
        copies.append(pltpu.make_async_copy(buf.at[window, :], out_ref.at[window, :], sems.at[s]))
        copies[-1].start()
    for copy in copies:
        copy.wait()


def scaled(channels, pre, squares, out_gain):
    width, columns = pre.shape
    steps = 8
    return pl.pallas_call(
        functools.partial(scale_kernel, channels, steps),
        out_shape=jax.ShapeDtypeStruct((width, columns), jnp.float32),
        in_specs=[WHOLE] * (2 + len(squares)),
        out_specs=IN_HBM,
        scratch_shapes=[pltpu.VMEM((width, columns), jnp.float32), pltpu.SemaphoreType.DMA((steps,))],
        compiler_params=pltpu.CompilerParams(vmem_limit_bytes=16 * MIB),
        cost_estimate=pl.CostEstimate(flops=2 * width * columns, bytes_accessed=8 * width * columns, transcendentals=0),
    )(pre, out_gain, *squares)


def local(query, key_in, value_in, filter_store, lag_of_block, skip, out_gain):
    width, columns = query.shape
    count = lax.axis_size("tok")
    tabs = [jnp.asarray(t) for t in tables(width)]
    own = split(count, filter_store)
    held, key_in, value_in = lax.optimization_barrier((own[0], key_in, value_in))
    mine = gate(count, key_in, value_in)
    order = sending_order(count)
    filts, gates, convs = {}, {}, {}
    for k in order:
        filts[k] = send(own[k], k, count)
    gated_order = order[:2] + [order[3], order[2]] + order[4:]
    for k in gated_order:
        gates[k] = send(mine[k], k, count)
    filts[0], gates[0] = held, mine[0]
    filt = filter_spectra(lag_of_block, *tabs[:2], filts)
    early = gated_order[: count // 2] + [0]
    gated = gated_spectra(count, *tabs[:2], {k: gates[k] for k in early})
    first = order[:1]
    sums, found = products(first, tabs, filt, gated, {k: gates[k] for k in gates if k not in early})
    found.update(inverses(order[1:] + [0], tabs, sums))
    for k in order:
        convs[k] = send(found[k], k, count)
    convs[0] = found[0]
    pre, square = gated_output(query, skip[None, :], order[: count // 2] + [0], convs, mine)
    others = lax.axis_size("chan")
    squares = [square] + [
        lax.ppermute(square, "chan", [(d, d ^ step) for d in range(others)]) for step in reversed(range(1, others))
    ]
    return scaled(columns * others, pre, squares, out_gain[None, :])


def solution(mesh):
    in_specs = (
        P("tok", "chan"),
        P("tok", "chan"),
        P("tok", "chan"),
        P("tok", "chan"),
        P(),
        P("chan"),
        P("chan"),
    )
    return jax.shard_map(local, mesh=mesh, in_specs=in_specs, out_specs=P("tok", "chan"), check_vma=False)
```

```python
import functools
import math

import jax
import jax.numpy as jnp
import ml_dtypes
import numpy as np
from jax import lax
from jax.experimental import pallas as pl
from jax.experimental.pallas import tpu as pltpu
from jax.sharding import PartitionSpec as P

MIB = 1024 * 1024
BIG = 48 * MIB
WHOLE = pl.BlockSpec(memory_space=pltpu.VMEM)
IN_HBM = pl.BlockSpec(memory_space=pltpu.HBM)


def split_bf16(table):
    high = table.astype(ml_dtypes.bfloat16)
    low = (table - high.astype(np.float64)).astype(ml_dtypes.bfloat16)
    return high, low


def tables(width):
    freq = np.concatenate([np.arange(0, width, 2), np.arange(1, width, 2)])
    place = np.arange(width)
    steps = ((2 * freq[:, None] + 1) * place[None, :]) % (4 * width)
    angle = math.pi / (2 * width) * steps
    forward = np.concatenate([np.cos(angle), -np.sin(angle)], axis=0)
    inverse = forward.T / width
    return split_bf16(forward) + split_bf16(inverse)


def partner(step):
    return lax.axis_index("tok") ^ step


def send(block, step, count):
    return lax.ppermute(block, "tok", [(d, d ^ step) for d in range(count)])


def sending_order(count):
    half = count // 2
    far = list(range(half, count, 2)) + list(range(half + 1, count, 2))
    near = list(range(2, half)) + [1]
    order = []
    for at in range(half - 1):
        order += [far[at], near[at]]
    return order[:-1] + far[-1:] + order[-1:]


def columns_of(step, part):
    return pl.ds(pl.multiple_of(partner(step) * part, 128), part)


def split_kernel(count, part, filt_ref, *refs):
    outs, sems = refs[:count], refs[count]
    copies = []
    for k in range(count):
        copies.append(pltpu.make_async_copy(filt_ref.at[:, columns_of(k, part)], outs[k], sems.at[k]))
        copies[-1].start()
    for copy in copies:
        copy.wait()


def gate_kernel(count, part, key_ref, value_ref, *refs):
    outs, (key_buf, value_buf, sems) = refs[:count], refs[count:]
    copies = []
    for k in range(count):
        cols = columns_of(k, part)
        copies.append(
            (
                pltpu.make_async_copy(key_ref.at[:, cols], key_buf.at[k], sems.at[0, k]),
                pltpu.make_async_copy(value_ref.at[:, cols], value_buf.at[k], sems.at[1, k]),
            )
        )
        for copy in copies[-1]:
            copy.start()
    for k in range(count):
        for copy in copies[k]:
            copy.wait()
        product = key_buf[k].astype(jnp.float32) * value_buf[k].astype(jnp.float32)
        outs[k][...] = product.astype(jnp.bfloat16)


def pieces(x, count):
    part = x.shape[1] // count
    return [lax.dynamic_slice_in_dim(x, partner(k) * part, part, axis=1) for k in range(count)]


def split(count, filter_store):
    width, columns = filter_store.shape
    part = columns // count
    if part % 128:
        return pieces(filter_store, count)
    return pl.pallas_call(
        functools.partial(split_kernel, count, part),
        out_shape=[jax.ShapeDtypeStruct((width, part), jnp.bfloat16)] * count,
        in_specs=[IN_HBM],
        out_specs=[WHOLE] * count,
        scratch_shapes=[pltpu.SemaphoreType.DMA((count,))],
        compiler_params=pltpu.CompilerParams(vmem_limit_bytes=BIG),
        cost_estimate=pl.CostEstimate(flops=0, bytes_accessed=4 * width * columns, transcendentals=0),
    )(filter_store)


def gate(count, key_in, value_in):
    width, columns = key_in.shape
    part = columns // count
    if part % 128:
        gated = (key_in.astype(jnp.float32) * value_in.astype(jnp.float32)).astype(jnp.bfloat16)
        return pieces(gated, count)
    block = pltpu.VMEM((count, width, part), jnp.bfloat16)
    return pl.pallas_call(
        functools.partial(gate_kernel, count, part),
        out_shape=[jax.ShapeDtypeStruct((width, part), jnp.bfloat16)] * count,
        in_specs=[IN_HBM] * 2,
        out_specs=[WHOLE] * count,
        scratch_shapes=[block, block, pltpu.SemaphoreType.DMA((2, count))],
        compiler_params=pltpu.CompilerParams(vmem_limit_bytes=BIG),
        cost_estimate=pl.CostEstimate(flops=width * columns, bytes_accessed=6 * width * columns, transcendentals=0),
    )(key_in, value_in)


def dot(x, y):
    return jnp.dot(x, y, preferred_element_type=jnp.float32)


def transform(high, low, block):
    return dot(high, block) + dot(low, block)


def transform_cost(count, width, columns, passes):
    return pl.CostEstimate(
        flops=4 * passes * count * width * width * columns,
        bytes_accessed=10 * count * width * columns,
        transcendentals=0,
    )


def tiles(width, columns, tile):
    half = width // 16
    lane = min(128, columns)

    def run(row, sign):
        re_rows = pl.ds(pl.multiple_of(row * 8, 8), 8)
        im_rows = pl.ds(pl.multiple_of(row * 8 + width, 8), 8)
        for at in range(0, columns, lane):
            tile(re_rows, im_rows, pl.ds(at, lane), sign)

    @pl.loop(0, half)
    def _(row):
        run(row, 1)

    @pl.loop(half, 2 * half)
    def _(row):
        run(row, -1)


def gated_kernel(steps, high_ref, low_ref, *refs):
    blocks, out = refs[:-1], refs[-1]
    for k in range(out.shape[0]):
        if k not in steps:
            out[partner(k)] = jnp.zeros(out.shape[1:], jnp.float32)
    for k, block in zip(steps, blocks):
        out[partner(k)] = transform(high_ref[...], low_ref[...], block[...])


def gated_spectra(count, high, low, blocks):
    steps = list(blocks)
    width, columns = blocks[0].shape
    return pl.pallas_call(
        functools.partial(gated_kernel, steps),
        out_shape=jax.ShapeDtypeStruct((count, 2 * width, columns), jnp.float32),
        in_specs=[WHOLE] * (2 + len(steps)),
        out_specs=WHOLE,
        compiler_params=pltpu.CompilerParams(vmem_limit_bytes=16 * MIB),
        cost_estimate=transform_cost(len(steps), width, columns, 2),
    )(high, low, *[blocks[k] for k in steps])


def early_kernel(count, steps, last, lag_ref, high_ref, low_ref, *refs):
    blocks, (block, _, gs, fs, ss) = refs[:count], refs[count:]
    gs[partner(last)] = transform(high_ref[...], low_ref[...], block[...])
    width, columns = gs.shape[1] // 2, gs.shape[2]
    for at, (k, block) in enumerate(zip(steps, blocks)):
        fs[at] = jnp.zeros(fs.shape[1:], jnp.float32)
        fs[count + lag_ref[partner(k)]] = transform(high_ref[...], low_ref[...], block[...])

    def tile(re_rows, im_rows, lanes, sign):
        f = [(fs[count + i, re_rows, lanes], fs[count + i, im_rows, lanes]) for i in range(count)]
        h, last = [], None
        for i in range(count):
            here = (gs[i, re_rows, lanes], gs[i, im_rows, lanes])
            if last is None:
                h.append(here)
            elif sign > 0:
                h.append((here[0] - last[1], here[1] + last[0]))
            else:
                h.append((here[0] + last[1], here[1] - last[0]))
            last = here
        for j in range(count):
            s_re = f[0][0] * h[j][0] - f[0][1] * h[j][1]
            s_im = f[0][0] * h[j][1] + f[0][1] * h[j][0]
            for i in range(1, j + 1):
                s_re = s_re + f[i][0] * h[j - i][0] - f[i][1] * h[j - i][1]
                s_im = s_im + f[i][0] * h[j - i][1] + f[i][1] * h[j - i][0]
            ss[j, re_rows, lanes] = s_re
            ss[j, im_rows, lanes] = s_im

    tiles(width, columns, tile)


def early_products(lag_of_block, high, low, blocks, last, block, gated):
    steps = list(blocks)
    count, twice, columns = gated.shape
    return pl.pallas_call(
        functools.partial(early_kernel, count, steps, last),
        out_shape=[
            jax.ShapeDtypeStruct(gated.shape, jnp.float32),
            jax.ShapeDtypeStruct((2 * count, twice, columns), jnp.float32),
            jax.ShapeDtypeStruct(gated.shape, jnp.float32),
        ],
        in_specs=[pl.BlockSpec(memory_space=pltpu.SMEM)] + [WHOLE] * (4 + count),
        out_specs=[WHOLE, WHOLE, WHOLE],
        input_output_aliases={4 + count: 0},
        compiler_params=pltpu.CompilerParams(vmem_limit_bytes=16 * MIB),
        cost_estimate=transform_cost(count, twice // 2, columns, 2),
    )(lag_of_block, high, low, *[blocks[k] for k in steps], block, gated)[1:]


def inverse(table_high, table_low, total):
    high = total.astype(jnp.bfloat16)
    low = (total - high.astype(jnp.float32)).astype(jnp.bfloat16)
    return (dot(table_high, high) + dot(table_high, low) + dot(table_low, high)).astype(jnp.bfloat16)


def late_kernel(count, steps, first, fh_ref, fl_ref, ih_ref, il_ref, fs, sums, *refs):
    blocks, ss, outs, gs = refs[: len(steps)], refs[len(steps)], refs[len(steps) + 1 : -1], refs[-1]
    width, columns = blocks[0].shape
    for at, block in enumerate(blocks):
        gs[at] = transform(fh_ref[...], fl_ref[...], block[...])
    shifted = [fs.at[pl.ds(count - partner(k), count)] for k in steps]

    def tile(re_rows, im_rows, lanes, sign):
        def both(ref, i):
            return ref[i, re_rows, lanes], ref[i, im_rows, lanes]

        g = [both(gs, at) for at in range(len(steps))]
        f = [[both(view, j) for view in shifted] for j in range(count)]
        s = [both(ss, j) for j in range(count)]
        d = []
        for j in range(count):
            d_re = d_im = None
            for (f_re, f_im), (g_re, g_im) in zip(f[j], g):
                p_re, p_im = f_re * g_re - f_im * g_im, f_re * g_im + f_im * g_re
                d_re, d_im = (p_re, p_im) if d_re is None else (d_re + p_re, d_im + p_im)
            d.append((d_re, d_im))
        for j in range(count):
            s_re, s_im = s[j][0] + d[j][0], s[j][1] + d[j][1]
            if j and sign > 0:
                s_re, s_im = s_re - d[j - 1][1], s_im + d[j - 1][0]
            elif j:
                s_re, s_im = s_re + d[j - 1][1], s_im - d[j - 1][0]
            ss[j, re_rows, lanes] = s_re
            ss[j, im_rows, lanes] = s_im

    tiles(width, columns, tile)
    for k, out in zip(first, outs):
        out[...] = inverse(ih_ref[...], il_ref[...], ss[partner(k)])


def late_products(first, tabs, filt, sums, blocks):
    steps = list(blocks)
    count, twice, columns = sums.shape
    width = twice // 2
    found = pl.pallas_call(
        functools.partial(late_kernel, count, steps, first),
        out_shape=[jax.ShapeDtypeStruct(sums.shape, jnp.float32)]
        + [jax.ShapeDtypeStruct((width, columns), jnp.bfloat16)] * len(first),
        in_specs=[WHOLE] * (6 + len(steps)),
        out_specs=[WHOLE] * (1 + len(first)),
        scratch_shapes=[pltpu.VMEM((len(steps), twice, columns), jnp.float32)],
        input_output_aliases={5: 0},
        compiler_params=pltpu.CompilerParams(vmem_limit_bytes=16 * MIB),
        cost_estimate=transform_cost(count, width, columns, 3),
    )(*tabs, filt, sums, *[blocks[k] for k in steps])
    return found[0], dict(zip(first, found[1:]))


def inverse_kernel(steps, ih_ref, il_ref, ss, *outs):
    for k, out in zip(steps, outs):
        out[...] = inverse(ih_ref[...], il_ref[...], ss[partner(k)])


def inverses(steps, tabs, sums):
    count, twice, columns = sums.shape
    width = twice // 2
    found = pl.pallas_call(
        functools.partial(inverse_kernel, steps),
        out_shape=[jax.ShapeDtypeStruct((width, columns), jnp.bfloat16)] * len(steps),
        in_specs=[WHOLE] * 3,
        out_specs=[WHOLE] * len(steps),
        compiler_params=pltpu.CompilerParams(vmem_limit_bytes=16 * MIB),
        cost_estimate=transform_cost(len(steps), width, columns, 3),
    )(*tabs[2:], sums)
    return dict(zip(steps, found))


def pre_kernel(steps, before, after, query_ref, skip_ref, *refs):
    count = len(steps)
    refs = list(refs)
    total = jnp.zeros((query_ref.shape[0], 128), jnp.float32)
    if before:
        refs.pop(0)
        total = refs.pop(0)[...]
    convs, gates, (pre_ref, square_ref) = refs[:count], refs[count : 2 * count], refs[2 * count :]
    width, part = convs[0].shape
    for at_k, k in enumerate(steps):
        start = partner(k) * part if part < query_ref.shape[1] else 0
        for at in range(0, part, 128):
            lanes, cols = pl.ds(at, 128), pl.ds(pl.multiple_of(start + at, 128), 128)
            gated = gates[at_k][:, lanes].astype(jnp.float32)
            conv = convs[at_k][:, lanes].astype(jnp.float32)
            pre = query_ref[:, cols].astype(jnp.float32) * (conv + skip_ref[:, cols] * gated)
            pre_ref[:, cols] = pre
            total = total + pre * pre
    if after:
        square_ref[...] = total
    else:
        square_ref[...] = jnp.sum(total.T, axis=0, keepdims=True)


def together(blocks):
    count, width = len(blocks), blocks[0].shape[0]
    order = jnp.arange(count, dtype=jnp.int32) ^ lax.axis_index("tok")
    stacked = jnp.take(jnp.stack([blocks[k] for k in range(count)]), order, axis=0)
    return {0: stacked.transpose(1, 0, 2).reshape(width, -1)}


def gated_output(query, skip, early, convs, gates):
    width, columns = query.shape
    groups = [early, [k for k in convs if k not in early]]
    if convs[0].shape[1] % 128:
        convs, gates, groups = together(convs), together(gates), [[0]]
    found = []
    for at, steps in enumerate(groups):
        rest = at + 1 < len(groups)
        found = pl.pallas_call(
            functools.partial(pre_kernel, steps, at > 0, rest),
            out_shape=(
                jax.ShapeDtypeStruct((width, columns), jnp.float32),
                jax.ShapeDtypeStruct((width, 128) if rest else (1, width), jnp.float32),
            ),
            in_specs=[WHOLE] * (2 + len(found) + 2 * len(steps)),
            out_specs=(WHOLE, WHOLE),
            input_output_aliases={2: 0} if found else {},
            compiler_params=pltpu.CompilerParams(vmem_limit_bytes=16 * MIB),
            cost_estimate=pl.CostEstimate(
                flops=3 * width * columns, bytes_accessed=5 * width * columns, transcendentals=0
            ),
        )(query, skip, *found, *[convs[k] for k in steps], *[gates[k] for k in steps])
    return found


def scale_kernel(channels, steps, pre_ref, gain_ref, *refs):
    squares, (out_ref, buf, sems) = refs[:-3], refs[-3:]
    width = pre_ref.shape[0]
    rows = width // steps
    total = squares[0][...]
    for square in squares[1:]:
        total = total + square[...]
    scale = lax.rsqrt(total * (1.0 / channels) + 1e-06)
    scale = jnp.broadcast_to(scale, (128, width)).T
    copies = []
    for s in range(steps):
        for at in range(0, pre_ref.shape[1], 128):
            cols = pl.ds(at, 128)
            here = scale[s * rows : (s + 1) * rows, :]
            buf[pl.ds(s * rows, rows), cols] = gain_ref[:, cols] * pre_ref[pl.ds(s * rows, rows), cols] * here
        window = pl.ds(s * rows, rows)
        copies.append(pltpu.make_async_copy(buf.at[window, :], out_ref.at[window, :], sems.at[s]))
        copies[-1].start()
    for copy in copies:
        copy.wait()


def scaled(channels, pre, squares, out_gain):
    width, columns = pre.shape
    steps = 8
    return pl.pallas_call(
        functools.partial(scale_kernel, channels, steps),
        out_shape=jax.ShapeDtypeStruct((width, columns), jnp.float32),
        in_specs=[WHOLE] * (2 + len(squares)),
        out_specs=IN_HBM,
        scratch_shapes=[pltpu.VMEM((width, columns), jnp.float32), pltpu.SemaphoreType.DMA((steps,))],
        compiler_params=pltpu.CompilerParams(vmem_limit_bytes=16 * MIB),
        cost_estimate=pl.CostEstimate(flops=2 * width * columns, bytes_accessed=8 * width * columns, transcendentals=0),
    )(pre, out_gain, *squares)


def local(query, key_in, value_in, filter_store, lag_of_block, skip, out_gain):
    width, columns = query.shape
    count = lax.axis_size("tok")
    tabs = [jnp.asarray(t) for t in tables(width)]
    own = split(count, filter_store)
    order = sending_order(count)
    gates, convs = {}, {}
    filts = {k: send(own[k], k, count) for k in order}
    filts[order[0]], key_in, value_in = lax.optimization_barrier((filts[order[0]], key_in, value_in))
    mine = gate(count, key_in, value_in)
    for k in order:
        gates[k] = send(mine[k], k, count)
    filts[0], gates[0] = own[0], mine[0]
    early = order[: count // 2] + [0]
    gated = gated_spectra(count, *tabs[:2], {k: gates[k] for k in early})
    last = order[-1]
    filt, sums = early_products(lag_of_block, *tabs[:2], filts, last, gates[last], gated)
    sums, found = late_products(order[:1], tabs, filt, sums, {k: gates[k] for k in gates if k not in early + [last]})
    found.update(inverses(order[1:] + [0], tabs, sums))
    for at, k in enumerate(order):
        block = found[k]
        if at == 6:
            block, convs[order[0]] = lax.optimization_barrier((block, convs[order[0]]))
        convs[k] = send(block, k, count)
    convs[0] = found[0]
    pre, square = gated_output(query, skip[None, :], order[: count // 2] + [0], convs, mine)
    others = lax.axis_size("chan")
    step = 1
    while step < others:
        square = square + lax.ppermute(square, "chan", [(d, d ^ step) for d in range(others)])
        step *= 2
    return scaled(columns * others, pre, [square], out_gain[None, :])


def solution(mesh):
    in_specs = (
        P("tok", "chan"),
        P("tok", "chan"),
        P("tok", "chan"),
        P("tok", "chan"),
        P(),
        P("chan"),
        P("chan"),
    )
    return jax.shard_map(local, mesh=mesh, in_specs=in_specs, out_specs=P("tok", "chan"), check_vma=False)
```

```python
import functools
import math

import jax
import jax.numpy as jnp
import ml_dtypes
import numpy as np
from jax import lax
from jax.experimental import pallas as pl
from jax.experimental.pallas import tpu as pltpu
from jax.sharding import PartitionSpec as P

MIB = 1024 * 1024
BIG = 48 * MIB
WHOLE = pl.BlockSpec(memory_space=pltpu.VMEM)
IN_HBM = pl.BlockSpec(memory_space=pltpu.HBM)


def split_bf16(table):
    high = table.astype(ml_dtypes.bfloat16)
    low = (table - high.astype(np.float64)).astype(ml_dtypes.bfloat16)
    return high, low


def tables(width):
    freq = np.concatenate([np.arange(0, width, 2), np.arange(1, width, 2)])
    place = np.arange(width)
    steps = ((2 * freq[:, None] + 1) * place[None, :]) % (4 * width)
    angle = math.pi / (2 * width) * steps
    forward = np.concatenate([np.cos(angle), -np.sin(angle)], axis=0)
    inverse = forward.T / width
    return split_bf16(forward) + split_bf16(inverse)


def partner(step):
    return lax.axis_index("tok") ^ step


def send(block, step, count):
    return lax.ppermute(block, "tok", [(d, d ^ step) for d in range(count)])


def sending_order(count):
    half = count // 2
    far = list(range(half, count, 2)) + list(range(half + 1, count, 2))
    near = list(range(2, half)) + [1]
    order = []
    for at in range(half - 1):
        order += [far[at], near[at]]
    return order[:-1] + far[-1:] + order[-1:]


def columns_of(step, part):
    return pl.ds(pl.multiple_of(partner(step) * part, 128), part)


def split_kernel(count, part, filt_ref, *refs):
    outs, sems = refs[:count], refs[count]
    copies = []
    for k in range(count):
        copies.append(pltpu.make_async_copy(filt_ref.at[:, columns_of(k, part)], outs[k], sems.at[k]))
        copies[-1].start()
    for copy in copies:
        copy.wait()


def gate_kernel(count, part, key_ref, value_ref, *refs):
    outs, (key_buf, value_buf, sems) = refs[:count], refs[count:]
    copies = []
    for k in range(count):
        cols = columns_of(k, part)
        copies.append(
            (
                pltpu.make_async_copy(key_ref.at[:, cols], key_buf.at[k], sems.at[0, k]),
                pltpu.make_async_copy(value_ref.at[:, cols], value_buf.at[k], sems.at[1, k]),
            )
        )
        for copy in copies[-1]:
            copy.start()
    for k in range(count):
        for copy in copies[k]:
            copy.wait()
        product = key_buf[k].astype(jnp.float32) * value_buf[k].astype(jnp.float32)
        outs[k][...] = product.astype(jnp.bfloat16)


def pieces(x, count):
    part = x.shape[1] // count
    return [lax.dynamic_slice_in_dim(x, partner(k) * part, part, axis=1) for k in range(count)]


def split(count, filter_store):
    width, columns = filter_store.shape
    part = columns // count
    if part % 128:
        return pieces(filter_store, count)
    return pl.pallas_call(
        functools.partial(split_kernel, count, part),
        out_shape=[jax.ShapeDtypeStruct((width, part), jnp.bfloat16)] * count,
        in_specs=[IN_HBM],
        out_specs=[WHOLE] * count,
        scratch_shapes=[pltpu.SemaphoreType.DMA((count,))],
        compiler_params=pltpu.CompilerParams(vmem_limit_bytes=BIG),
        cost_estimate=pl.CostEstimate(flops=0, bytes_accessed=4 * width * columns, transcendentals=0),
    )(filter_store)


def gate(count, key_in, value_in):
    width, columns = key_in.shape
    part = columns // count
    if part % 128:
        gated = (key_in.astype(jnp.float32) * value_in.astype(jnp.float32)).astype(jnp.bfloat16)
        return pieces(gated, count)
    block = pltpu.VMEM((count, width, part), jnp.bfloat16)
    return pl.pallas_call(
        functools.partial(gate_kernel, count, part),
        out_shape=[jax.ShapeDtypeStruct((width, part), jnp.bfloat16)] * count,
        in_specs=[IN_HBM] * 2,
        out_specs=[WHOLE] * count,
        scratch_shapes=[block, block, pltpu.SemaphoreType.DMA((2, count))],
        compiler_params=pltpu.CompilerParams(vmem_limit_bytes=BIG),
        cost_estimate=pl.CostEstimate(flops=width * columns, bytes_accessed=6 * width * columns, transcendentals=0),
    )(key_in, value_in)


def dot(x, y):
    return jnp.dot(x, y, preferred_element_type=jnp.float32)


def transform(high, low, block):
    return dot(high, block) + dot(low, block)


def transform_cost(count, width, columns, passes):
    return pl.CostEstimate(
        flops=4 * passes * count * width * width * columns,
        bytes_accessed=10 * count * width * columns,
        transcendentals=0,
    )


def tiles(width, columns, tile):
    half = width // 16
    lane = min(128, columns)

    def run(row, sign):
        re_rows = pl.ds(pl.multiple_of(row * 8, 8), 8)
        im_rows = pl.ds(pl.multiple_of(row * 8 + width, 8), 8)
        for at in range(0, columns, lane):
            tile(re_rows, im_rows, pl.ds(at, lane), sign)

    @pl.loop(0, half)
    def _(row):
        run(row, 1)

    @pl.loop(half, 2 * half)
    def _(row):
        run(row, -1)


def gated_kernel(steps, high_ref, low_ref, *refs):
    blocks, out = refs[:-1], refs[-1]
    for k in range(out.shape[0]):
        if k not in steps:
            out[partner(k)] = jnp.zeros(out.shape[1:], jnp.float32)
    for k, block in zip(steps, blocks):
        out[partner(k)] = transform(high_ref[...], low_ref[...], block[...])


def gated_spectra(count, high, low, blocks):
    steps = list(blocks)
    width, columns = blocks[0].shape
    return pl.pallas_call(
        functools.partial(gated_kernel, steps),
        out_shape=jax.ShapeDtypeStruct((count, 2 * width, columns), jnp.float32),
        in_specs=[WHOLE] * (2 + len(steps)),
        out_specs=WHOLE,
        compiler_params=pltpu.CompilerParams(vmem_limit_bytes=16 * MIB),
        cost_estimate=transform_cost(len(steps), width, columns, 2),
    )(high, low, *[blocks[k] for k in steps])


def early_kernel(count, steps, last, lag_ref, high_ref, low_ref, *refs):
    blocks, (block, _, gs, fs, ss) = refs[:count], refs[count:]
    gs[partner(last)] = transform(high_ref[...], low_ref[...], block[...])
    width, columns = gs.shape[1] // 2, gs.shape[2]
    for at, (k, block) in enumerate(zip(steps, blocks)):
        fs[at] = jnp.zeros(fs.shape[1:], jnp.float32)
        fs[count + lag_ref[partner(k)]] = transform(high_ref[...], low_ref[...], block[...])

    def tile(re_rows, im_rows, lanes, sign):
        f = [(fs[count + i, re_rows, lanes], fs[count + i, im_rows, lanes]) for i in range(count)]
        h, last = [], None
        for i in range(count):
            here = (gs[i, re_rows, lanes], gs[i, im_rows, lanes])
            if last is None:
                h.append(here)
            elif sign > 0:
                h.append((here[0] - last[1], here[1] + last[0]))
            else:
                h.append((here[0] + last[1], here[1] - last[0]))
            last = here
        for j in range(count):
            s_re = f[0][0] * h[j][0] - f[0][1] * h[j][1]
            s_im = f[0][0] * h[j][1] + f[0][1] * h[j][0]
            for i in range(1, j + 1):
                s_re = s_re + f[i][0] * h[j - i][0] - f[i][1] * h[j - i][1]
                s_im = s_im + f[i][0] * h[j - i][1] + f[i][1] * h[j - i][0]
            ss[j, re_rows, lanes] = s_re
            ss[j, im_rows, lanes] = s_im

    tiles(width, columns, tile)


def early_products(lag_of_block, high, low, blocks, last, block, gated):
    steps = list(blocks)
    count, twice, columns = gated.shape
    return pl.pallas_call(
        functools.partial(early_kernel, count, steps, last),
        out_shape=[
            jax.ShapeDtypeStruct(gated.shape, jnp.float32),
            jax.ShapeDtypeStruct((2 * count, twice, columns), jnp.float32),
            jax.ShapeDtypeStruct(gated.shape, jnp.float32),
        ],
        in_specs=[pl.BlockSpec(memory_space=pltpu.SMEM)] + [WHOLE] * (4 + count),
        out_specs=[WHOLE, WHOLE, WHOLE],
        input_output_aliases={4 + count: 0},
        compiler_params=pltpu.CompilerParams(vmem_limit_bytes=16 * MIB),
        cost_estimate=transform_cost(count, twice // 2, columns, 2),
    )(lag_of_block, high, low, *[blocks[k] for k in steps], block, gated)[1:]


def inverse(table_high, table_low, total):
    high = total.astype(jnp.bfloat16)
    low = (total - high.astype(jnp.float32)).astype(jnp.bfloat16)
    return (dot(table_high, high) + dot(table_high, low) + dot(table_low, high)).astype(jnp.bfloat16)


def first_kernel(count, steps, first, fh_ref, fl_ref, ih_ref, il_ref, fs, ss, *refs):
    blocks, (gs, out, total) = refs[: len(steps)], refs[len(steps) :]
    width, columns = blocks[0].shape
    for at, block in enumerate(blocks):
        gs[at] = transform(fh_ref[...], fl_ref[...], block[...])
    here = partner(first)
    views = [(fs.at[count - partner(k) + here], fs.at[count - partner(k) + here - 1]) for k in steps]
    sums = ss.at[here]

    def tile(re_rows, im_rows, lanes, sign):
        s_re, s_im = sums[re_rows, lanes], sums[im_rows, lanes]
        for at, (now, before) in enumerate(views):
            g_re, g_im = gs[at, re_rows, lanes], gs[at, im_rows, lanes]
            f_re, f_im = now[re_rows, lanes], now[im_rows, lanes]
            b_re, b_im = before[re_rows, lanes], before[im_rows, lanes]
            f_re, f_im = (f_re - b_im, f_im + b_re) if sign > 0 else (f_re + b_im, f_im - b_re)
            s_re = s_re + f_re * g_re - f_im * g_im
            s_im = s_im + f_re * g_im + f_im * g_re
        total[re_rows, lanes] = s_re
        total[im_rows, lanes] = s_im

    tiles(width, columns, tile)
    out[...] = inverse(ih_ref[...], il_ref[...], total[...])


def rest_kernel(count, late, steps, ih_ref, il_ref, fs, sums, gs, *refs):
    outs, ss = refs[:-1], refs[-1]
    width, columns = outs[0].shape
    shifted = [fs.at[pl.ds(count - partner(k), count)] for k in late]

    def tile(re_rows, im_rows, lanes, sign):
        def both(ref, i):
            return ref[i, re_rows, lanes], ref[i, im_rows, lanes]

        g = [both(gs, at) for at in range(len(late))]
        d = []
        for j in range(count):
            d_re = d_im = None
            for view, (g_re, g_im) in zip(shifted, g):
                f_re, f_im = both(view, j)
                p_re, p_im = f_re * g_re - f_im * g_im, f_re * g_im + f_im * g_re
                d_re, d_im = (p_re, p_im) if d_re is None else (d_re + p_re, d_im + p_im)
            d.append((d_re, d_im))
        for j in range(count):
            s_re, s_im = both(sums, j)
            s_re, s_im = s_re + d[j][0], s_im + d[j][1]
            if j and sign > 0:
                s_re, s_im = s_re - d[j - 1][1], s_im + d[j - 1][0]
            elif j:
                s_re, s_im = s_re + d[j - 1][1], s_im - d[j - 1][0]
            ss[j, re_rows, lanes] = s_re
            ss[j, im_rows, lanes] = s_im

    tiles(width, columns, tile)
    for k, out in zip(steps, outs):
        out[...] = inverse(ih_ref[...], il_ref[...], ss[partner(k)])


def first_product(first, tabs, filt, sums, blocks):
    steps = list(blocks)
    count, twice, columns = sums.shape
    width = twice // 2
    return pl.pallas_call(
        functools.partial(first_kernel, count, steps, first),
        out_shape=[
            jax.ShapeDtypeStruct((len(steps), twice, columns), jnp.float32),
            jax.ShapeDtypeStruct((width, columns), jnp.bfloat16),
        ],
        in_specs=[WHOLE] * (6 + len(steps)),
        out_specs=[WHOLE, WHOLE],
        scratch_shapes=[pltpu.VMEM((twice, columns), jnp.float32)],
        compiler_params=pltpu.CompilerParams(vmem_limit_bytes=16 * MIB),
        cost_estimate=transform_cost(count, width, columns, 1),
    )(*tabs, filt, sums, *[blocks[k] for k in steps])


def rest_products(steps, tabs, filt, sums, late, spectra):
    count, twice, columns = sums.shape
    width = twice // 2
    found = pl.pallas_call(
        functools.partial(rest_kernel, count, late, steps),
        out_shape=[jax.ShapeDtypeStruct((width, columns), jnp.bfloat16)] * len(steps),
        in_specs=[WHOLE] * 5,
        out_specs=[WHOLE] * len(steps),
        scratch_shapes=[pltpu.VMEM(sums.shape, jnp.float32)],
        compiler_params=pltpu.CompilerParams(vmem_limit_bytes=16 * MIB),
        cost_estimate=transform_cost(count, width, columns, 3),
    )(*tabs[2:], filt, sums, spectra)
    return dict(zip(steps, found))


def pre_kernel(steps, before, after, query_ref, skip_ref, *refs):
    count = len(steps)
    refs = list(refs)
    total = jnp.zeros((query_ref.shape[0], 128), jnp.float32)
    if before:
        refs.pop(0)
        total = refs.pop(0)[...]
    convs, gates, (pre_ref, square_ref) = refs[:count], refs[count : 2 * count], refs[2 * count :]
    width, part = convs[0].shape
    for at_k, k in enumerate(steps):
        start = partner(k) * part if part < query_ref.shape[1] else 0
        for at in range(0, part, 128):
            lanes, cols = pl.ds(at, 128), pl.ds(pl.multiple_of(start + at, 128), 128)
            gated = gates[at_k][:, lanes].astype(jnp.float32)
            conv = convs[at_k][:, lanes].astype(jnp.float32)
            pre = query_ref[:, cols].astype(jnp.float32) * (conv + skip_ref[:, cols] * gated)
            pre_ref[:, cols] = pre
            total = total + pre * pre
    if after:
        square_ref[...] = total
    else:
        square_ref[...] = jnp.sum(total.T, axis=0, keepdims=True)


def together(blocks):
    count, width = len(blocks), blocks[0].shape[0]
    order = jnp.arange(count, dtype=jnp.int32) ^ lax.axis_index("tok")
    stacked = jnp.take(jnp.stack([blocks[k] for k in range(count)]), order, axis=0)
    return {0: stacked.transpose(1, 0, 2).reshape(width, -1)}


def gated_output(query, skip, early, convs, gates):
    width, columns = query.shape
    groups = [early, [k for k in convs if k not in early]]
    if convs[0].shape[1] % 128:
        convs, gates, groups = together(convs), together(gates), [[0]]
    found = []
    for at, steps in enumerate(groups):
        rest = at + 1 < len(groups)
        found = pl.pallas_call(
            functools.partial(pre_kernel, steps, at > 0, rest),
            out_shape=(
                jax.ShapeDtypeStruct((width, columns), jnp.float32),
                jax.ShapeDtypeStruct((width, 128) if rest else (1, width), jnp.float32),
            ),
            in_specs=[WHOLE] * (2 + len(found) + 2 * len(steps)),
            out_specs=(WHOLE, WHOLE),
            input_output_aliases={2: 0} if found else {},
            compiler_params=pltpu.CompilerParams(vmem_limit_bytes=16 * MIB),
            cost_estimate=pl.CostEstimate(
                flops=3 * width * columns, bytes_accessed=5 * width * columns, transcendentals=0
            ),
        )(query, skip, *found, *[convs[k] for k in steps], *[gates[k] for k in steps])
    return found


def scale_kernel(channels, steps, pre_ref, gain_ref, *refs):
    squares, (out_ref, buf, sems) = refs[:-3], refs[-3:]
    width = pre_ref.shape[0]
    rows = width // steps
    total = squares[0][...]
    for square in squares[1:]:
        total = total + square[...]
    scale = lax.rsqrt(total * (1.0 / channels) + 1e-06)
    scale = jnp.broadcast_to(scale, (128, width)).T
    copies = []
    for s in range(steps):
        for at in range(0, pre_ref.shape[1], 128):
            cols = pl.ds(at, 128)
            here = scale[s * rows : (s + 1) * rows, :]
            buf[pl.ds(s * rows, rows), cols] = gain_ref[:, cols] * pre_ref[pl.ds(s * rows, rows), cols] * here
        window = pl.ds(s * rows, rows)
        copies.append(pltpu.make_async_copy(buf.at[window, :], out_ref.at[window, :], sems.at[s]))
        copies[-1].start()
    for copy in copies:
        copy.wait()


def scaled(channels, pre, squares, out_gain):
    width, columns = pre.shape
    steps = 8
    return pl.pallas_call(
        functools.partial(scale_kernel, channels, steps),
        out_shape=jax.ShapeDtypeStruct((width, columns), jnp.float32),
        in_specs=[WHOLE] * (2 + len(squares)),
        out_specs=IN_HBM,
        scratch_shapes=[pltpu.VMEM((width, columns), jnp.float32), pltpu.SemaphoreType.DMA((steps,))],
        compiler_params=pltpu.CompilerParams(vmem_limit_bytes=16 * MIB),
        cost_estimate=pl.CostEstimate(flops=2 * width * columns, bytes_accessed=8 * width * columns, transcendentals=0),
    )(pre, out_gain, *squares)


def local(query, key_in, value_in, filter_store, lag_of_block, skip, out_gain):
    width, columns = query.shape
    count = lax.axis_size("tok")
    tabs = [jnp.asarray(t) for t in tables(width)]
    own = split(count, filter_store)
    order = sending_order(count)
    gates, convs = {}, {}
    filts = {k: send(own[k], k, count) for k in order}
    filts[order[0]], key_in, value_in = lax.optimization_barrier((filts[order[0]], key_in, value_in))
    mine = gate(count, key_in, value_in)
    for k in order:
        gates[k] = send(mine[k], k, count)
    filts[0], gates[0] = own[0], mine[0]
    early = order[: count // 2] + [0]
    gated = gated_spectra(count, *tabs[:2], {k: gates[k] for k in early})
    last = order[-1]
    filt, sums = early_products(lag_of_block, *tabs[:2], filts, last, gates[last], gated)
    late = {k: gates[k] for k in gates if k not in early + [last]}
    spectra, ahead = first_product(order[0], tabs, filt, sums, late)
    found = rest_products(order[1:] + [0], tabs, filt, sums, list(late), spectra)
    found[order[0]] = ahead
    for at, k in enumerate(order):
        block = found[k]
        if at == 6:
            block, convs[order[0]] = lax.optimization_barrier((block, convs[order[0]]))
        convs[k] = send(block, k, count)
    convs[0] = found[0]
    pre, square = gated_output(query, skip[None, :], order[: count // 2] + [0], convs, mine)
    others = lax.axis_size("chan")
    step = 1
    while step < others:
        square = square + lax.ppermute(square, "chan", [(d, d ^ step) for d in range(others)])
        step *= 2
    return scaled(columns * others, pre, [square], out_gain[None, :])


def solution(mesh):
    in_specs = (
        P("tok", "chan"),
        P("tok", "chan"),
        P("tok", "chan"),
        P("tok", "chan"),
        P(),
        P("chan"),
        P("chan"),
    )
    return jax.shard_map(local, mesh=mesh, in_specs=in_specs, out_specs=P("tok", "chan"), check_vma=False)
```

```python
import functools
import math

import jax
import jax.numpy as jnp
import ml_dtypes
import numpy as np
from jax import lax
from jax.experimental import pallas as pl
from jax.experimental.pallas import tpu as pltpu
from jax.sharding import PartitionSpec as P

MIB = 1024 * 1024
BIG = 48 * MIB
WHOLE = pl.BlockSpec(memory_space=pltpu.VMEM)
IN_HBM = pl.BlockSpec(memory_space=pltpu.HBM)


def split_bf16(table):
    high = table.astype(ml_dtypes.bfloat16)
    low = (table - high.astype(np.float64)).astype(ml_dtypes.bfloat16)
    return high, low


def tables(width):
    freq = np.concatenate([np.arange(0, width, 2), np.arange(1, width, 2)])
    place = np.arange(width)
    steps = ((2 * freq[:, None] + 1) * place[None, :]) % (4 * width)
    angle = math.pi / (2 * width) * steps
    forward = np.concatenate([np.cos(angle), -np.sin(angle)], axis=0)
    inverse = forward.T / width
    return split_bf16(forward) + split_bf16(inverse)


def partner(step):
    return lax.axis_index("tok") ^ step


def send(block, step, count):
    return lax.ppermute(block, "tok", [(d, d ^ step) for d in range(count)])


def sending_order(count):
    half = count // 2
    far = list(range(half, count, 2)) + list(range(half + 1, count, 2))
    near = list(range(2, half)) + [1]
    order = []
    for at in range(half - 1):
        order += [far[at], near[at]]
    return order[:-1] + far[-1:] + order[-1:]


def columns_of(step, part):
    return pl.ds(pl.multiple_of(partner(step) * part, 128), part)


def split_kernel(count, part, filt_ref, *refs):
    outs, sems = refs[:count], refs[count]
    copies = []
    for k in range(count):
        copies.append(pltpu.make_async_copy(filt_ref.at[:, columns_of(k, part)], outs[k], sems.at[k]))
        copies[-1].start()
    for copy in copies:
        copy.wait()


def gate_kernel(count, part, key_ref, value_ref, *refs):
    outs, (key_buf, value_buf, sems) = refs[:count], refs[count:]
    copies = []
    for k in range(count):
        cols = columns_of(k, part)
        copies.append(
            (
                pltpu.make_async_copy(key_ref.at[:, cols], key_buf.at[k], sems.at[0, k]),
                pltpu.make_async_copy(value_ref.at[:, cols], value_buf.at[k], sems.at[1, k]),
            )
        )
        for copy in copies[-1]:
            copy.start()
    for k in range(count):
        for copy in copies[k]:
            copy.wait()
        product = key_buf[k].astype(jnp.float32) * value_buf[k].astype(jnp.float32)
        outs[k][...] = product.astype(jnp.bfloat16)


def pieces(x, count):
    part = x.shape[1] // count
    return [lax.dynamic_slice_in_dim(x, partner(k) * part, part, axis=1) for k in range(count)]


def split(count, filter_store):
    width, columns = filter_store.shape
    part = columns // count
    if part % 128:
        return pieces(filter_store, count)
    return pl.pallas_call(
        functools.partial(split_kernel, count, part),
        out_shape=[jax.ShapeDtypeStruct((width, part), jnp.bfloat16)] * count,
        in_specs=[IN_HBM],
        out_specs=[WHOLE] * count,
        scratch_shapes=[pltpu.SemaphoreType.DMA((count,))],
        compiler_params=pltpu.CompilerParams(vmem_limit_bytes=BIG),
        cost_estimate=pl.CostEstimate(flops=0, bytes_accessed=4 * width * columns, transcendentals=0),
    )(filter_store)


def gate(count, key_in, value_in):
    width, columns = key_in.shape
    part = columns // count
    if part % 128:
        gated = (key_in.astype(jnp.float32) * value_in.astype(jnp.float32)).astype(jnp.bfloat16)
        return pieces(gated, count)
    block = pltpu.VMEM((count, width, part), jnp.bfloat16)
    return pl.pallas_call(
        functools.partial(gate_kernel, count, part),
        out_shape=[jax.ShapeDtypeStruct((width, part), jnp.bfloat16)] * count,
        in_specs=[IN_HBM] * 2,
        out_specs=[WHOLE] * count,
        scratch_shapes=[block, block, pltpu.SemaphoreType.DMA((2, count))],
        compiler_params=pltpu.CompilerParams(vmem_limit_bytes=BIG),
        cost_estimate=pl.CostEstimate(flops=width * columns, bytes_accessed=6 * width * columns, transcendentals=0),
    )(key_in, value_in)


def dot(x, y):
    return jnp.dot(x, y, preferred_element_type=jnp.float32)


def transform(high, low, block):
    return dot(high, block) + dot(low, block)


def transform_cost(count, width, columns, passes):
    return pl.CostEstimate(
        flops=4 * passes * count * width * width * columns,
        bytes_accessed=10 * count * width * columns,
        transcendentals=0,
    )


def tiles(width, columns, tile):
    half = width // 16
    lane = min(128, columns)

    def run(row, sign):
        re_rows = pl.ds(pl.multiple_of(row * 8, 8), 8)
        im_rows = pl.ds(pl.multiple_of(row * 8 + width, 8), 8)
        for at in range(0, columns, lane):
            tile(re_rows, im_rows, pl.ds(at, lane), sign)

    @pl.loop(0, half)
    def _(row):
        run(row, 1)

    @pl.loop(half, 2 * half)
    def _(row):
        run(row, -1)


def gated_kernel(steps, high_ref, low_ref, *refs):
    blocks, out = refs[:-1], refs[-1]
    for k in range(out.shape[0]):
        if k not in steps:
            out[partner(k)] = jnp.zeros(out.shape[1:], jnp.float32)
    for k, block in zip(steps, blocks):
        out[partner(k)] = transform(high_ref[...], low_ref[...], block[...])


def gated_spectra(count, high, low, blocks):
    steps = list(blocks)
    width, columns = blocks[0].shape
    return pl.pallas_call(
        functools.partial(gated_kernel, steps),
        out_shape=jax.ShapeDtypeStruct((count, 2 * width, columns), jnp.float32),
        in_specs=[WHOLE] * (2 + len(steps)),
        out_specs=WHOLE,
        compiler_params=pltpu.CompilerParams(vmem_limit_bytes=16 * MIB),
        cost_estimate=transform_cost(len(steps), width, columns, 2),
    )(high, low, *[blocks[k] for k in steps])


def early_kernel(count, steps, last, lag_ref, high_ref, low_ref, *refs):
    blocks, (block, _, gs, fs, ss) = refs[:count], refs[count:]
    gs[partner(last)] = transform(high_ref[...], low_ref[...], block[...])
    width, columns = gs.shape[1] // 2, gs.shape[2]
    for at, (k, block) in enumerate(zip(steps, blocks)):
        fs[at] = jnp.zeros(fs.shape[1:], jnp.float32)
        fs[count + lag_ref[partner(k)]] = transform(high_ref[...], low_ref[...], block[...])

    def tile(re_rows, im_rows, lanes, sign):
        f = [(fs[count + i, re_rows, lanes], fs[count + i, im_rows, lanes]) for i in range(count)]
        h, last = [], None
        for i in range(count):
            here = (gs[i, re_rows, lanes], gs[i, im_rows, lanes])
            if last is None:
                h.append(here)
            elif sign > 0:
                h.append((here[0] - last[1], here[1] + last[0]))
            else:
                h.append((here[0] + last[1], here[1] - last[0]))
            last = here
        for j in range(count):
            s_re = f[0][0] * h[j][0] - f[0][1] * h[j][1]
            s_im = f[0][0] * h[j][1] + f[0][1] * h[j][0]
            for i in range(1, j + 1):
                s_re = s_re + f[i][0] * h[j - i][0] - f[i][1] * h[j - i][1]
                s_im = s_im + f[i][0] * h[j - i][1] + f[i][1] * h[j - i][0]
            ss[j, re_rows, lanes] = s_re
            ss[j, im_rows, lanes] = s_im

    tiles(width, columns, tile)


def early_products(lag_of_block, high, low, blocks, last, block, gated):
    steps = list(blocks)
    count, twice, columns = gated.shape
    return pl.pallas_call(
        functools.partial(early_kernel, count, steps, last),
        out_shape=[
            jax.ShapeDtypeStruct(gated.shape, jnp.float32),
            jax.ShapeDtypeStruct((2 * count, twice, columns), jnp.float32),
            jax.ShapeDtypeStruct(gated.shape, jnp.float32),
        ],
        in_specs=[pl.BlockSpec(memory_space=pltpu.SMEM)] + [WHOLE] * (4 + count),
        out_specs=[WHOLE, WHOLE, WHOLE],
        input_output_aliases={4 + count: 0},
        compiler_params=pltpu.CompilerParams(vmem_limit_bytes=16 * MIB),
        cost_estimate=transform_cost(count, twice // 2, columns, 2),
    )(lag_of_block, high, low, *[blocks[k] for k in steps], block, gated)[1:]


def inverse(table_high, table_low, total):
    high = total.astype(jnp.bfloat16)
    low = (total - high.astype(jnp.float32)).astype(jnp.bfloat16)
    return (dot(table_high, high) + dot(table_high, low) + dot(table_low, high)).astype(jnp.bfloat16)


def first_kernel(count, steps, first, fh_ref, fl_ref, ih_ref, il_ref, fs, ss, *refs):
    blocks, (gs, out, total) = refs[: len(steps)], refs[len(steps) :]
    width, columns = blocks[0].shape
    for at, block in enumerate(blocks):
        gs[at] = transform(fh_ref[...], fl_ref[...], block[...])
    here = partner(first)
    views = [(fs.at[count - partner(k) + here], fs.at[count - partner(k) + here - 1]) for k in steps]
    sums = ss.at[here]

    def tile(re_rows, im_rows, lanes, sign):
        s_re, s_im = sums[re_rows, lanes], sums[im_rows, lanes]
        for at, (now, before) in enumerate(views):
            g_re, g_im = gs[at, re_rows, lanes], gs[at, im_rows, lanes]
            f_re, f_im = now[re_rows, lanes], now[im_rows, lanes]
            b_re, b_im = before[re_rows, lanes], before[im_rows, lanes]
            f_re, f_im = (f_re - b_im, f_im + b_re) if sign > 0 else (f_re + b_im, f_im - b_re)
            s_re = s_re + f_re * g_re - f_im * g_im
            s_im = s_im + f_re * g_im + f_im * g_re
        total[re_rows, lanes] = s_re
        total[im_rows, lanes] = s_im

    tiles(width, columns, tile)
    out[...] = inverse(ih_ref[...], il_ref[...], total[...])


def rest_kernel(count, late, steps, ih_ref, il_ref, fs, sums, gs, *refs):
    outs, ss = refs[:-1], refs[-1]
    width, columns = outs[0].shape
    shifted = [fs.at[pl.ds(count - partner(k), count)] for k in late]

    def tile(re_rows, im_rows, lanes, sign):
        def both(ref, i):
            return ref[i, re_rows, lanes], ref[i, im_rows, lanes]

        g = [both(gs, at) for at in range(len(late))]
        d = []
        for j in range(count):
            d_re = d_im = None
            for view, (g_re, g_im) in zip(shifted, g):
                f_re, f_im = both(view, j)
                p_re, p_im = f_re * g_re - f_im * g_im, f_re * g_im + f_im * g_re
                d_re, d_im = (p_re, p_im) if d_re is None else (d_re + p_re, d_im + p_im)
            d.append((d_re, d_im))
        for j in range(count):
            s_re, s_im = both(sums, j)
            s_re, s_im = s_re + d[j][0], s_im + d[j][1]
            if j and sign > 0:
                s_re, s_im = s_re - d[j - 1][1], s_im + d[j - 1][0]
            elif j:
                s_re, s_im = s_re + d[j - 1][1], s_im - d[j - 1][0]
            ss[j, re_rows, lanes] = s_re
            ss[j, im_rows, lanes] = s_im

    tiles(width, columns, tile)
    for k, out in zip(steps, outs):
        out[...] = inverse(ih_ref[...], il_ref[...], ss[partner(k)])


def first_product(first, tabs, filt, sums, blocks):
    steps = list(blocks)
    count, twice, columns = sums.shape
    width = twice // 2
    return pl.pallas_call(
        functools.partial(first_kernel, count, steps, first),
        out_shape=[
            jax.ShapeDtypeStruct((len(steps), twice, columns), jnp.float32),
            jax.ShapeDtypeStruct((width, columns), jnp.bfloat16),
        ],
        in_specs=[WHOLE] * (6 + len(steps)),
        out_specs=[WHOLE, WHOLE],
        scratch_shapes=[pltpu.VMEM((twice, columns), jnp.float32)],
        compiler_params=pltpu.CompilerParams(vmem_limit_bytes=16 * MIB),
        cost_estimate=transform_cost(count, width, columns, 1),
    )(*tabs, filt, sums, *[blocks[k] for k in steps])


def rest_products(steps, tabs, filt, sums, late, spectra):
    count, twice, columns = sums.shape
    width = twice // 2
    found = pl.pallas_call(
        functools.partial(rest_kernel, count, late, steps),
        out_shape=[jax.ShapeDtypeStruct((width, columns), jnp.bfloat16)] * len(steps),
        in_specs=[WHOLE] * 5,
        out_specs=[WHOLE] * len(steps),
        scratch_shapes=[pltpu.VMEM(sums.shape, jnp.float32)],
        compiler_params=pltpu.CompilerParams(vmem_limit_bytes=16 * MIB),
        cost_estimate=transform_cost(count, width, columns, 3),
    )(*tabs[2:], filt, sums, spectra)
    return dict(zip(steps, found))


def pre_kernel(steps, before, after, query_ref, skip_ref, *refs):
    count = len(steps)
    refs = list(refs)
    total = jnp.zeros((query_ref.shape[0], 128), jnp.float32)
    if before:
        refs.pop(0)
        total = refs.pop(0)[...]
    convs, gates, (pre_ref, square_ref) = refs[:count], refs[count : 2 * count], refs[2 * count :]
    width, part = convs[0].shape
    for at_k, k in enumerate(steps):
        start = partner(k) * part if part < query_ref.shape[1] else 0
        for at in range(0, part, 128):
            lanes, cols = pl.ds(at, 128), pl.ds(pl.multiple_of(start + at, 128), 128)
            gated = gates[at_k][:, lanes].astype(jnp.float32)
            conv = convs[at_k][:, lanes].astype(jnp.float32)
            pre = query_ref[:, cols].astype(jnp.float32) * (conv + skip_ref[:, cols] * gated)
            pre_ref[:, cols] = pre
            total = total + pre * pre
    if after:
        square_ref[...] = total
    else:
        square_ref[...] = jnp.sum(total.T, axis=0, keepdims=True)


def together(blocks):
    count, width = len(blocks), blocks[0].shape[0]
    order = jnp.arange(count, dtype=jnp.int32) ^ lax.axis_index("tok")
    stacked = jnp.take(jnp.stack([blocks[k] for k in range(count)]), order, axis=0)
    return {0: stacked.transpose(1, 0, 2).reshape(width, -1)}


def gated_output(query, skip, early, convs, gates):
    width, columns = query.shape
    groups = [early, [k for k in convs if k not in early]]
    if convs[0].shape[1] % 128:
        convs, gates, groups = together(convs), together(gates), [[0]]
    found = []
    for at, steps in enumerate(groups):
        rest = at + 1 < len(groups)
        found = pl.pallas_call(
            functools.partial(pre_kernel, steps, at > 0, rest),
            out_shape=(
                jax.ShapeDtypeStruct((width, columns), jnp.float32),
                jax.ShapeDtypeStruct((width, 128) if rest else (1, width), jnp.float32),
            ),
            in_specs=[WHOLE] * (2 + len(found) + 2 * len(steps)),
            out_specs=(WHOLE, WHOLE),
            input_output_aliases={2: 0} if found else {},
            compiler_params=pltpu.CompilerParams(vmem_limit_bytes=16 * MIB),
            cost_estimate=pl.CostEstimate(
                flops=3 * width * columns, bytes_accessed=5 * width * columns, transcendentals=0
            ),
        )(query, skip, *found, *[convs[k] for k in steps], *[gates[k] for k in steps])
    return found


def scale_kernel(channels, steps, pre_ref, gain_ref, *refs):
    squares, (out_ref, buf, sems) = refs[:-3], refs[-3:]
    width = pre_ref.shape[0]
    rows = width // steps
    total = squares[0][...]
    for square in squares[1:]:
        total = total + square[...]
    scale = lax.rsqrt(total * (1.0 / channels) + 1e-06)
    scale = jnp.broadcast_to(scale, (128, width)).T
    copies = []
    for s in range(steps):
        for at in range(0, pre_ref.shape[1], 128):
            cols = pl.ds(at, 128)
            here = scale[s * rows : (s + 1) * rows, :]
            buf[pl.ds(s * rows, rows), cols] = gain_ref[:, cols] * pre_ref[pl.ds(s * rows, rows), cols] * here
        window = pl.ds(s * rows, rows)
        copies.append(pltpu.make_async_copy(buf.at[window, :], out_ref.at[window, :], sems.at[s]))
        copies[-1].start()
    for copy in copies:
        copy.wait()


def scaled(channels, pre, squares, out_gain):
    width, columns = pre.shape
    steps = 8
    return pl.pallas_call(
        functools.partial(scale_kernel, channels, steps),
        out_shape=jax.ShapeDtypeStruct((width, columns), jnp.float32),
        in_specs=[WHOLE] * (2 + len(squares)),
        out_specs=IN_HBM,
        scratch_shapes=[pltpu.VMEM((width, columns), jnp.float32), pltpu.SemaphoreType.DMA((steps,))],
        compiler_params=pltpu.CompilerParams(vmem_limit_bytes=16 * MIB),
        cost_estimate=pl.CostEstimate(flops=2 * width * columns, bytes_accessed=8 * width * columns, transcendentals=0),
    )(pre, out_gain, *squares)


def local(query, key_in, value_in, filter_store, lag_of_block, skip, out_gain):
    width, columns = query.shape
    count = lax.axis_size("tok")
    tabs = [jnp.asarray(t) for t in tables(width)]
    own = split(count, filter_store)
    order = sending_order(count)
    gates, convs = {}, {}
    filts = {k: send(own[k], k, count) for k in order}
    filts[order[0]], key_in, value_in = lax.optimization_barrier((filts[order[0]], key_in, value_in))
    mine = gate(count, key_in, value_in)
    for k in order:
        gates[k] = send(mine[k], k, count)
    filts[0], gates[0] = own[0], mine[0]
    early = order[: count // 2] + [0]
    gated = gated_spectra(count, *tabs[:2], {k: gates[k] for k in early})
    last = order[-1]
    filt, sums = early_products(lag_of_block, *tabs[:2], filts, last, gates[last], gated)
    late = {k: gates[k] for k in gates if k not in early + [last]}
    spectra, ahead = first_product(order[0], tabs, filt, sums, late)
    found = rest_products([order[2], order[1]] + order[3:] + [0], tabs, filt, sums, list(late), spectra)
    found[order[0]] = ahead
    returns = [order[0], order[2], order[1]] + order[3:]
    for at, k in enumerate(returns):
        block = found[k]
        if at == 6:
            block, convs[order[0]] = lax.optimization_barrier((block, convs[order[0]]))
        convs[k] = send(block, k, count)
    convs[0] = found[0]
    pre, square = gated_output(query, skip[None, :], returns[: count // 2] + [0], convs, mine)
    others = lax.axis_size("chan")
    step = 1
    while step < others:
        square = square + lax.ppermute(square, "chan", [(d, d ^ step) for d in range(others)])
        step *= 2
    return scaled(columns * others, pre, [square], out_gain[None, :])


def solution(mesh):
    in_specs = (
        P("tok", "chan"),
        P("tok", "chan"),
        P("tok", "chan"),
        P("tok", "chan"),
        P(),
        P("chan"),
        P("chan"),
    )
    return jax.shard_map(local, mesh=mesh, in_specs=in_specs, out_specs=P("tok", "chan"), check_vma=False)
```

```python
import functools
import math

import jax
import jax.numpy as jnp
import ml_dtypes
import numpy as np
from jax import lax
from jax.experimental import pallas as pl
from jax.experimental.pallas import tpu as pltpu
from jax.sharding import PartitionSpec as P

MIB = 1024 * 1024
BIG = 48 * MIB
WHOLE = pl.BlockSpec(memory_space=pltpu.VMEM)
IN_HBM = pl.BlockSpec(memory_space=pltpu.HBM)


def split_bf16(table):
    high = table.astype(ml_dtypes.bfloat16)
    low = (table - high.astype(np.float64)).astype(ml_dtypes.bfloat16)
    return high, low


def tables(width):
    freq = np.concatenate([np.arange(0, width, 2), np.arange(1, width, 2)])
    place = np.arange(width)
    steps = ((2 * freq[:, None] + 1) * place[None, :]) % (4 * width)
    angle = math.pi / (2 * width) * steps
    forward = np.concatenate([np.cos(angle), -np.sin(angle)], axis=0)
    inverse = forward.T / width
    return split_bf16(forward) + split_bf16(inverse)


def partner(step):
    return lax.axis_index("tok") ^ step


def send(block, step, count):
    return lax.ppermute(block, "tok", [(d, d ^ step) for d in range(count)])


def sending_order(count):
    half = count // 2
    far = list(range(half, count, 2)) + list(range(half + 1, count, 2))
    near = list(range(2, half)) + [1]
    order = []
    for at in range(half - 1):
        order += [far[at], near[at]]
    return order[:-1] + far[-1:] + order[-1:]


def columns_of(step, part):
    return pl.ds(pl.multiple_of(partner(step) * part, 128), part)


def split_kernel(count, part, filt_ref, *refs):
    outs, sems = refs[:count], refs[count]
    copies = []
    for k in range(count):
        copies.append(pltpu.make_async_copy(filt_ref.at[:, columns_of(k, part)], outs[k], sems.at[k]))
        copies[-1].start()
    for copy in copies:
        copy.wait()


def gate_kernel(count, part, key_ref, value_ref, *refs):
    outs, (key_buf, value_buf, sems) = refs[:count], refs[count:]
    copies = []
    for k in range(count):
        cols = columns_of(k, part)
        copies.append(
            (
                pltpu.make_async_copy(key_ref.at[:, cols], key_buf.at[k], sems.at[0, k]),
                pltpu.make_async_copy(value_ref.at[:, cols], value_buf.at[k], sems.at[1, k]),
            )
        )
        for copy in copies[-1]:
            copy.start()
    for k in range(count):
        for copy in copies[k]:
            copy.wait()
        product = key_buf[k].astype(jnp.float32) * value_buf[k].astype(jnp.float32)
        outs[k][...] = product.astype(jnp.bfloat16)


def pieces(x, count):
    part = x.shape[1] // count
    return [lax.dynamic_slice_in_dim(x, partner(k) * part, part, axis=1) for k in range(count)]


def split(count, filter_store):
    width, columns = filter_store.shape
    part = columns // count
    if part % 128:
        return pieces(filter_store, count)
    return pl.pallas_call(
        functools.partial(split_kernel, count, part),
        out_shape=[jax.ShapeDtypeStruct((width, part), jnp.bfloat16)] * count,
        in_specs=[IN_HBM],
        out_specs=[WHOLE] * count,
        scratch_shapes=[pltpu.SemaphoreType.DMA((count,))],
        compiler_params=pltpu.CompilerParams(vmem_limit_bytes=BIG),
        cost_estimate=pl.CostEstimate(flops=0, bytes_accessed=4 * width * columns, transcendentals=0),
    )(filter_store)


def gate(count, key_in, value_in):
    width, columns = key_in.shape
    part = columns // count
    if part % 128:
        gated = (key_in.astype(jnp.float32) * value_in.astype(jnp.float32)).astype(jnp.bfloat16)
        return pieces(gated, count)
    block = pltpu.VMEM((count, width, part), jnp.bfloat16)
    return pl.pallas_call(
        functools.partial(gate_kernel, count, part),
        out_shape=[jax.ShapeDtypeStruct((width, part), jnp.bfloat16)] * count,
        in_specs=[IN_HBM] * 2,
        out_specs=[WHOLE] * count,
        scratch_shapes=[block, block, pltpu.SemaphoreType.DMA((2, count))],
        compiler_params=pltpu.CompilerParams(vmem_limit_bytes=BIG),
        cost_estimate=pl.CostEstimate(flops=width * columns, bytes_accessed=6 * width * columns, transcendentals=0),
    )(key_in, value_in)


def dot(x, y):
    return jnp.dot(x, y, preferred_element_type=jnp.float32)


def transform(high, low, block):
    return dot(high, block) + dot(low, block)


def transform_cost(count, width, columns, passes):
    return pl.CostEstimate(
        flops=4 * passes * count * width * width * columns,
        bytes_accessed=10 * count * width * columns,
        transcendentals=0,
    )


def tiles(width, columns, tile):
    half = width // 16
    lane = min(128, columns)

    def run(row, sign):
        re_rows = pl.ds(pl.multiple_of(row * 8, 8), 8)
        im_rows = pl.ds(pl.multiple_of(row * 8 + width, 8), 8)
        for at in range(0, columns, lane):
            tile(re_rows, im_rows, pl.ds(at, lane), sign)

    @pl.loop(0, half)
    def _(row):
        run(row, 1)

    @pl.loop(half, 2 * half)
    def _(row):
        run(row, -1)


def gated_kernel(steps, high_ref, low_ref, *refs):
    blocks, out = refs[:-1], refs[-1]
    for k in range(out.shape[0]):
        if k not in steps:
            out[partner(k)] = jnp.zeros(out.shape[1:], jnp.float32)
    for k, block in zip(steps, blocks):
        out[partner(k)] = transform(high_ref[...], low_ref[...], block[...])


def gated_spectra(count, high, low, blocks):
    steps = list(blocks)
    width, columns = blocks[0].shape
    return pl.pallas_call(
        functools.partial(gated_kernel, steps),
        out_shape=jax.ShapeDtypeStruct((count, 2 * width, columns), jnp.float32),
        in_specs=[WHOLE] * (2 + len(steps)),
        out_specs=WHOLE,
        compiler_params=pltpu.CompilerParams(vmem_limit_bytes=16 * MIB),
        cost_estimate=transform_cost(len(steps), width, columns, 2),
    )(high, low, *[blocks[k] for k in steps])


def early_kernel(count, steps, last, lag_ref, high_ref, low_ref, *refs):
    blocks, (block, _, gs, fs, ss) = refs[:count], refs[count:]
    gs[partner(last)] = transform(high_ref[...], low_ref[...], block[...])
    width, columns = gs.shape[1] // 2, gs.shape[2]
    for at, (k, block) in enumerate(zip(steps, blocks)):
        fs[at] = jnp.zeros(fs.shape[1:], jnp.float32)
        fs[count + lag_ref[partner(k)]] = transform(high_ref[...], low_ref[...], block[...])

    def tile(re_rows, im_rows, lanes, sign):
        f = [(fs[count + i, re_rows, lanes], fs[count + i, im_rows, lanes]) for i in range(count)]
        h, last = [], None
        for i in range(count):
            here = (gs[i, re_rows, lanes], gs[i, im_rows, lanes])
            if last is None:
                h.append(here)
            elif sign > 0:
                h.append((here[0] - last[1], here[1] + last[0]))
            else:
                h.append((here[0] + last[1], here[1] - last[0]))
            last = here
        for j in range(count):
            s_re = f[0][0] * h[j][0] - f[0][1] * h[j][1]
            s_im = f[0][0] * h[j][1] + f[0][1] * h[j][0]
            for i in range(1, j + 1):
                s_re = s_re + f[i][0] * h[j - i][0] - f[i][1] * h[j - i][1]
                s_im = s_im + f[i][0] * h[j - i][1] + f[i][1] * h[j - i][0]
            ss[j, re_rows, lanes] = s_re
            ss[j, im_rows, lanes] = s_im

    tiles(width, columns, tile)


def early_products(lag_of_block, high, low, blocks, last, block, gated):
    steps = list(blocks)
    count, twice, columns = gated.shape
    return pl.pallas_call(
        functools.partial(early_kernel, count, steps, last),
        out_shape=[
            jax.ShapeDtypeStruct(gated.shape, jnp.float32),
            jax.ShapeDtypeStruct((2 * count, twice, columns), jnp.float32),
            jax.ShapeDtypeStruct(gated.shape, jnp.float32),
        ],
        in_specs=[pl.BlockSpec(memory_space=pltpu.SMEM)] + [WHOLE] * (4 + count),
        out_specs=[WHOLE, WHOLE, WHOLE],
        input_output_aliases={4 + count: 0},
        compiler_params=pltpu.CompilerParams(vmem_limit_bytes=16 * MIB),
        cost_estimate=transform_cost(count, twice // 2, columns, 2),
    )(lag_of_block, high, low, *[blocks[k] for k in steps], block, gated)[1:]


def inverse(table_high, table_low, total):
    high = total.astype(jnp.bfloat16)
    low = (total - high.astype(jnp.float32)).astype(jnp.bfloat16)
    return (dot(table_high, high) + dot(table_high, low) + dot(table_low, high)).astype(jnp.bfloat16)


def first_kernel(count, steps, first, fh_ref, fl_ref, ih_ref, il_ref, fs, ss, *refs):
    blocks, (gs, out, total) = refs[: len(steps)], refs[len(steps) :]
    width, columns = blocks[0].shape
    for at, block in enumerate(blocks):
        gs[at] = transform(fh_ref[...], fl_ref[...], block[...])
    here = partner(first)
    views = [(fs.at[count - partner(k) + here], fs.at[count - partner(k) + here - 1]) for k in steps]
    sums = ss.at[here]

    def tile(re_rows, im_rows, lanes, sign):
        s_re, s_im = sums[re_rows, lanes], sums[im_rows, lanes]
        for at, (now, before) in enumerate(views):
            g_re, g_im = gs[at, re_rows, lanes], gs[at, im_rows, lanes]
            f_re, f_im = now[re_rows, lanes], now[im_rows, lanes]
            b_re, b_im = before[re_rows, lanes], before[im_rows, lanes]
            f_re, f_im = (f_re - b_im, f_im + b_re) if sign > 0 else (f_re + b_im, f_im - b_re)
            s_re = s_re + f_re * g_re - f_im * g_im
            s_im = s_im + f_re * g_im + f_im * g_re
        total[re_rows, lanes] = s_re
        total[im_rows, lanes] = s_im

    tiles(width, columns, tile)
    out[...] = inverse(ih_ref[...], il_ref[...], total[...])


def rest_kernel(count, late, steps, ih_ref, il_ref, fs, sums, gs, *refs):
    outs, ss = refs[:-1], refs[-1]
    width, columns = outs[0].shape
    shifted = [fs.at[pl.ds(count - partner(k), count)] for k in late]

    def tile(re_rows, im_rows, lanes, sign):
        def both(ref, i):
            return ref[i, re_rows, lanes], ref[i, im_rows, lanes]

        g = [both(gs, at) for at in range(len(late))]
        d = []
        for j in range(count):
            d_re = d_im = None
            for view, (g_re, g_im) in zip(shifted, g):
                f_re, f_im = both(view, j)
                p_re, p_im = f_re * g_re - f_im * g_im, f_re * g_im + f_im * g_re
                d_re, d_im = (p_re, p_im) if d_re is None else (d_re + p_re, d_im + p_im)
            d.append((d_re, d_im))
        for j in range(count):
            s_re, s_im = both(sums, j)
            s_re, s_im = s_re + d[j][0], s_im + d[j][1]
            if j and sign > 0:
                s_re, s_im = s_re - d[j - 1][1], s_im + d[j - 1][0]
            elif j:
                s_re, s_im = s_re + d[j - 1][1], s_im - d[j - 1][0]
            ss[j, re_rows, lanes] = s_re
            ss[j, im_rows, lanes] = s_im

    tiles(width, columns, tile)
    for k, out in zip(steps, outs):
        out[...] = inverse(ih_ref[...], il_ref[...], ss[partner(k)])


def first_product(first, tabs, filt, sums, blocks):
    steps = list(blocks)
    count, twice, columns = sums.shape
    width = twice // 2
    return pl.pallas_call(
        functools.partial(first_kernel, count, steps, first),
        out_shape=[
            jax.ShapeDtypeStruct((len(steps), twice, columns), jnp.float32),
            jax.ShapeDtypeStruct((width, columns), jnp.bfloat16),
        ],
        in_specs=[WHOLE] * (6 + len(steps)),
        out_specs=[WHOLE, WHOLE],
        scratch_shapes=[pltpu.VMEM((twice, columns), jnp.float32)],
        compiler_params=pltpu.CompilerParams(vmem_limit_bytes=16 * MIB),
        cost_estimate=transform_cost(count, width, columns, 1),
    )(*tabs, filt, sums, *[blocks[k] for k in steps])


def rest_products(steps, tabs, filt, sums, late, spectra):
    count, twice, columns = sums.shape
    width = twice // 2
    found = pl.pallas_call(
        functools.partial(rest_kernel, count, late, steps),
        out_shape=[jax.ShapeDtypeStruct((width, columns), jnp.bfloat16)] * len(steps),
        in_specs=[WHOLE] * 5,
        out_specs=[WHOLE] * len(steps),
        scratch_shapes=[pltpu.VMEM(sums.shape, jnp.float32)],
        compiler_params=pltpu.CompilerParams(vmem_limit_bytes=16 * MIB),
        cost_estimate=transform_cost(count, width, columns, 3),
    )(*tabs[2:], filt, sums, spectra)
    return dict(zip(steps, found))


def pre_kernel(steps, before, after, query_ref, skip_ref, *refs):
    count = len(steps)
    refs = list(refs)
    total = jnp.zeros((query_ref.shape[0], 128), jnp.float32)
    if before:
        refs.pop(0)
        total = refs.pop(0)[...]
    convs, gates, (pre_ref, square_ref) = refs[:count], refs[count : 2 * count], refs[2 * count :]
    width, part = convs[0].shape
    for at_k, k in enumerate(steps):
        start = partner(k) * part if part < query_ref.shape[1] else 0
        for at in range(0, part, 128):
            lanes, cols = pl.ds(at, 128), pl.ds(pl.multiple_of(start + at, 128), 128)
            gated = gates[at_k][:, lanes].astype(jnp.float32)
            conv = convs[at_k][:, lanes].astype(jnp.float32)
            pre = query_ref[:, cols].astype(jnp.float32) * (conv + skip_ref[:, cols] * gated)
            pre_ref[:, cols] = pre
            total = total + pre * pre
    if after:
        square_ref[...] = total
    else:
        square_ref[...] = jnp.sum(total.T, axis=0, keepdims=True)


def together(blocks):
    count, width = len(blocks), blocks[0].shape[0]
    order = jnp.arange(count, dtype=jnp.int32) ^ lax.axis_index("tok")
    stacked = jnp.take(jnp.stack([blocks[k] for k in range(count)]), order, axis=0)
    return {0: stacked.transpose(1, 0, 2).reshape(width, -1)}


def gated_output(query, skip, early, convs, gates):
    width, columns = query.shape
    groups = [early, [k for k in convs if k not in early]]
    if convs[0].shape[1] % 128:
        convs, gates, groups = together(convs), together(gates), [[0]]
    found = []
    for at, steps in enumerate(groups):
        rest = at + 1 < len(groups)
        found = pl.pallas_call(
            functools.partial(pre_kernel, steps, at > 0, rest),
            out_shape=(
                jax.ShapeDtypeStruct((width, columns), jnp.float32),
                jax.ShapeDtypeStruct((width, 128) if rest else (1, width), jnp.float32),
            ),
            in_specs=[WHOLE] * (2 + len(found) + 2 * len(steps)),
            out_specs=(WHOLE, WHOLE),
            input_output_aliases={2: 0} if found else {},
            compiler_params=pltpu.CompilerParams(vmem_limit_bytes=16 * MIB),
            cost_estimate=pl.CostEstimate(
                flops=3 * width * columns, bytes_accessed=5 * width * columns, transcendentals=0
            ),
        )(query, skip, *found, *[convs[k] for k in steps], *[gates[k] for k in steps])
    return found


def scale_kernel(channels, steps, pre_ref, gain_ref, *refs):
    squares, (out_ref, buf, sems) = refs[:-3], refs[-3:]
    width = pre_ref.shape[0]
    rows = width // steps
    total = squares[0][...]
    for square in squares[1:]:
        total = total + square[...]
    scale = lax.rsqrt(total * (1.0 / channels) + 1e-06)
    scale = jnp.broadcast_to(scale, (128, width)).T
    copies = []
    for s in range(steps):
        for at in range(0, pre_ref.shape[1], 128):
            cols = pl.ds(at, 128)
            here = scale[s * rows : (s + 1) * rows, :]
            buf[pl.ds(s * rows, rows), cols] = gain_ref[:, cols] * pre_ref[pl.ds(s * rows, rows), cols] * here
        window = pl.ds(s * rows, rows)
        copies.append(pltpu.make_async_copy(buf.at[window, :], out_ref.at[window, :], sems.at[s]))
        copies[-1].start()
    for copy in copies:
        copy.wait()


def scaled(channels, pre, squares, out_gain):
    width, columns = pre.shape
    steps = 8
    return pl.pallas_call(
        functools.partial(scale_kernel, channels, steps),
        out_shape=jax.ShapeDtypeStruct((width, columns), jnp.float32),
        in_specs=[WHOLE] * (2 + len(squares)),
        out_specs=IN_HBM,
        scratch_shapes=[pltpu.VMEM((width, columns), jnp.float32), pltpu.SemaphoreType.DMA((steps,))],
        compiler_params=pltpu.CompilerParams(vmem_limit_bytes=16 * MIB),
        cost_estimate=pl.CostEstimate(flops=2 * width * columns, bytes_accessed=8 * width * columns, transcendentals=0),
    )(pre, out_gain, *squares)


def local(query, key_in, value_in, filter_store, lag_of_block, skip, out_gain):
    width, columns = query.shape
    count = lax.axis_size("tok")
    tabs = [jnp.asarray(t) for t in tables(width)]
    own = split(count, filter_store)
    order = sending_order(count)
    gates, convs = {}, {}
    filts = {k: send(own[k], k, count) for k in order}
    filts[order[0]], key_in, value_in = lax.optimization_barrier((filts[order[0]], key_in, value_in))
    mine = gate(count, key_in, value_in)
    for k in order:
        gates[k] = send(mine[k], k, count)
    filts[0], gates[0] = own[0], mine[0]
    early = order[: count // 2] + [0]
    gated = gated_spectra(count, *tabs[:2], {k: gates[k] for k in early})
    last = order[-1]
    filt, sums = early_products(lag_of_block, *tabs[:2], filts, last, gates[last], gated)
    late = {k: gates[k] for k in gates if k not in early + [last]}
    spectra, ahead = first_product(order[0], tabs, filt, sums, late)
    found = rest_products([order[2], order[1], order[4], order[3]] + order[5:] + [0], tabs, filt, sums, list(late), spectra)
    found[order[0]] = ahead
    returns = [order[0], order[2], order[1], order[4], order[3]] + order[5:]
    for at, k in enumerate(returns):
        block = found[k]
        if at == 6:
            block, convs[order[0]] = lax.optimization_barrier((block, convs[order[0]]))
        convs[k] = send(block, k, count)
    convs[0] = found[0]
    pre, square = gated_output(query, skip[None, :], returns[: count // 2] + [0], convs, mine)
    others = lax.axis_size("chan")
    step = 1
    while step < others:
        square = square + lax.ppermute(square, "chan", [(d, d ^ step) for d in range(others)])
        step *= 2
    return scaled(columns * others, pre, [square], out_gain[None, :])


def solution(mesh):
    in_specs = (
        P("tok", "chan"),
        P("tok", "chan"),
        P("tok", "chan"),
        P("tok", "chan"),
        P(),
        P("chan"),
        P("chan"),
    )
    return jax.shard_map(local, mesh=mesh, in_specs=in_specs, out_specs=P("tok", "chan"), check_vma=False)
```
